128 devices in a mesh: seq: 16 (over x, y), grp: 8 (over z, core).
Axes of the slice: x: 4, y: 4, z: 4, core: 2. Of those that a mesh axis runs over, the one named last changes fastest.
Arguments:
- queries: bfloat16 [8, 16, 128, 2560], P('grp', 'seq'), may hold values from -140 to 140
- out_grad: bfloat16 [8, 16, 128, 2560], P('grp', 'seq'), may hold values from -48 to 48
- saved_output: bfloat16 [8, 16, 128, 2560], P('grp', 'seq'), may hold values from -3 to 3
- key_rows: bfloat16 [8, 16, 128, 512], P('grp', 'seq'), may hold values from -6 to 6
- value_rows: bfloat16 [8, 16, 128, 512], P('grp', 'seq'), may hold values from -6 to 6
- hidden_rows: bfloat16 [8, 16, 128, 5120], P('grp', 'seq'), may hold values from -6 to 6
- prefix_keys: bfloat16 [8, 128, 512], replicated, may hold values from -8 to 8
- prefix_values: bfloat16 [8, 128, 512], replicated, may hold values from -6 to 6
- prefix_hidden: bfloat16 [8, 128, 5120], P('grp', 'seq'), may hold values from -6 to 6
- block_mask: int32 [8, 16, 16], P('grp'), may hold values from 0 to 1, as said below
- prefix_list: int32 [8, 2], P('grp'), may hold values from 0 to 7, as said below
- key_down: bfloat16 [5120, 64], replicated, may hold values from -0.078125 to 0.078125
- value_down: bfloat16 [5120, 64], replicated, may hold values from -0.078125 to 0.078125
- key_up: bfloat16 [64, 512], replicated, may hold values from -0.75 to 0.75
- value_up: bfloat16 [64, 512], replicated, may hold values from -0.75 to 0.75
Outputs:
- pair_grads: bfloat16 [8, 2048, 1024], P('grp', 'seq')
- prefix_grads: float32 [8, 128, 1024], P('grp', 'seq')
- down_grads: float32 [2, 5120, 64], replicated
- up_grads: float32 [2, 64, 512], replicated
The draws below stay inside these ranges and needn't reach their ends.
Inputs may be any that keep to these rules, and one draw needn't show every extreme that they name: block_mask[g, i, j] is 1 where j = i and 0 where j > i. `prefix_list`: each row names 2 distinct prefix blocks.
All inputs are finite; a program needn't handle non-finite values.
Results may differ from the reference program's by a relative error of at most 0.024.
Values may be sent and summed in bfloat16 or wider, within the bound.
A program may use at most 128 MiB of HBM per device.

```python
import jax
import jax.numpy as jnp
from jax import lax

D = 5120
QUERY_HEAD_COUNT = 20
KEY_VALUE_HEADS = 4
HEAD_SIZE = 128
RANK = 64
BLK = 128
RESPONSE_TOKENS = 128
PB_DEV = 1
PL = 2
ROLL = 16
ROLLOUT_GROUPS = 8
NPB = 8
NB = 16
KVW = 512
QW = 2560
N_SEQ = 16
N_GRP = 8


def list_table(key):
    source = jax.random.fold_in(key, 23)
    favored = jax.random.randint(jax.random.fold_in(source, 1), (), 0, NPB)
    picker = jax.random.randint(jax.random.fold_in(source, 2), (ROLLOUT_GROUPS,), 0, 4)
    other = jax.random.randint(jax.random.fold_in(source, 3), (ROLLOUT_GROUPS,), 0, NPB)
    start = jnp.where(picker == 0, other, favored)
    start = start.at[0].set(NPB - 1)
    return ((start[:, None] + jnp.arange(PL, dtype=jnp.int32)[None, :]) % NPB).astype(jnp.int32)


def prefix_table(key):
    base = jnp.clip(jax.random.normal(jax.random.fold_in(key, 37), (NPB, BLK, KVW), jnp.float32), -6.0, 6.0)
    return base


def draw_prefix_keys(key, part):
    return prefix_table(key).astype(jnp.bfloat16)


def draw_prefix_list(key, part):
    return list_table(key)


def draw_block_mask(key, part):
    bits = jax.random.randint(jax.random.fold_in(key, 11), (ROLLOUT_GROUPS, NB, NB), 0, 2)
    row_index = jnp.arange(NB, dtype=jnp.int32)[:, None]
    col_index = jnp.arange(NB, dtype=jnp.int32)[None, :]
    lower = jnp.where(col_index < row_index, bits, jnp.where(col_index == row_index, 1, 0))
    return lower.astype(jnp.int32)


def draw_queries(key, part):
    base = jnp.clip(jax.random.normal(jax.random.fold_in(key, 41), (ROLLOUT_GROUPS, ROLL, RESPONSE_TOKENS, QUERY_HEAD_COUNT * HEAD_SIZE), jnp.float32), -6.0, 6.0)
    return base.astype(jnp.bfloat16)


def block_scale(stream_key, extent, split, low, high):
    level, own = 1.0, jax.random.fold_in(stream_key, 6)
    for dim, shards_of in split:
        steps = jnp.exp(jax.random.uniform(jax.random.fold_in(own, dim), (shards_of,), jnp.float32, low / len(split), high / len(split)))
        level = level * jnp.repeat(steps, extent[dim] // shards_of).reshape([-1 if axis == dim else 1 for axis in range(len(extent))])
    return level


def scatter_about(key, dims, spread, bound, cuts=(), kind=jnp.bfloat16):
    entries = jax.random.normal(key, dims, jnp.float32) * spread
    if len(cuts) > 0:
        entries = block_scale(key, dims, cuts, -0.22, 0.18) * entries
    return jnp.clip(entries, min=-bound, max=bound).astype(kind)


def setup_inputs(seed: int = 0) -> dict:
    keys = jax.random.split(jax.random.key(seed), 16)
    return {
        "queries": draw_queries(jax.random.fold_in(keys[15], 71), 0),
        "out_grad": scatter_about(keys[1], (ROLLOUT_GROUPS, ROLL, RESPONSE_TOKENS, QW), 8.0, 48.0, ((0, 8), (1, 16))),
        "saved_output": scatter_about(keys[2], (ROLLOUT_GROUPS, ROLL, RESPONSE_TOKENS, QW), 0.5, 3.0, ((0, 8), (1, 16))),
        "key_rows": scatter_about(keys[3], (ROLLOUT_GROUPS, ROLL, RESPONSE_TOKENS, KVW), 1.0, 6.0, ((0, 8), (1, 16))),
        "value_rows": scatter_about(keys[4], (ROLLOUT_GROUPS, ROLL, RESPONSE_TOKENS, KVW), 1.0, 6.0, ((0, 8), (1, 16))),
        "hidden_rows": scatter_about(keys[5], (ROLLOUT_GROUPS, ROLL, RESPONSE_TOKENS, D), 1.0, 6.0, ((0, 8), (1, 16))),
        "prefix_keys": draw_prefix_keys(jax.random.fold_in(keys[15], 71), 0),
        "prefix_values": scatter_about(keys[7], (NPB, BLK, KVW), 1.0, 6.0),
        "prefix_hidden": scatter_about(keys[8], (NPB, BLK, D), 1.0, 6.0, ((0, 8), (1, 16))),
        "block_mask": draw_block_mask(jax.random.fold_in(keys[15], 71), 0),
        "prefix_list": draw_prefix_list(jax.random.fold_in(keys[15], 71), 0),
        "key_down": scatter_about(keys[11], (D, RANK), D ** -0.5, 0.078125),
        "value_down": scatter_about(keys[12], (D, RANK), D ** -0.5, 0.078125),
        "key_up": scatter_about(keys[13], (RANK, KVW), RANK ** -0.5, 0.75),
        "value_up": scatter_about(keys[14], (RANK, KVW), RANK ** -0.5, 0.75),
    }


adapter_scale = 2.0
masked_score = -1.0e30


def float_einsum(pattern, former, latter):
    return jnp.einsum(pattern, former.astype(jnp.float32), latter.astype(jnp.float32))


def tree_order(source):
    columns = source.shape[-1]
    blocks = source.reshape(N_SEQ, N_SEQ, RESPONSE_TOKENS // N_SEQ, columns)
    return jnp.transpose(blocks, (1, 0, 2, 3)).reshape(N_SEQ * RESPONSE_TOKENS, columns)


def visible_table(mask_rows, slice_index):
    span = RESPONSE_TOKENS // N_SEQ
    local = jnp.arange(RESPONSE_TOKENS, dtype=jnp.int32)
    query_place = (local // span) * RESPONSE_TOKENS + slice_index.astype(jnp.int32) * span + local % span
    key_index = jnp.arange(N_SEQ * RESPONSE_TOKENS, dtype=jnp.int32)
    key_rest = key_index % RESPONSE_TOKENS
    key_place = (key_rest // span) * RESPONSE_TOKENS + (key_index // RESPONSE_TOKENS) * span + key_rest % span
    picked = jnp.take(mask_rows, query_place // BLK, axis=0)
    broadcast_copies = jnp.take(picked, key_place // BLK, axis=1)
    same_block = (query_place[:, None] // BLK) == (key_place[None, :] // BLK)
    causal = key_place[None, :] <= query_place[:, None]
    return (broadcast_copies == 1) & (jnp.logical_not(same_block) | causal)


def head_grads(query_head, grad_head, key_head, value_head, allowed, log_total, delta_head):
    scale_factor = HEAD_SIZE ** -0.5
    scores = float_einsum("tgd,kd->tgk", query_head, key_head) * scale_factor
    attention = jnp.exp(scores - log_total[:, :, None])
    if allowed is not None:
        attention = jnp.where(allowed[:, None, :], attention, 0.0)
    attention_low = attention.astype(jnp.bfloat16)
    grad_attention = float_einsum("tgd,kd->tgk", grad_head, value_head)
    grad_scores = (attention * (grad_attention - delta_head[:, :, None]) * scale_factor).astype(jnp.bfloat16)
    key_grad = float_einsum("tgk,tgd->kd", grad_scores, query_head)
    value_grad = float_einsum("tgk,tgd->kd", attention_low, grad_head)
    return key_grad, value_grad


def slice_terms(query_rows, gradient_rows, stored_rows, tree_pairs, prefix_pairs, allowed):
    rollouts_per_group = QUERY_HEAD_COUNT // KEY_VALUE_HEADS
    pairing_width = KEY_VALUE_HEADS * HEAD_SIZE
    scale_factor = HEAD_SIZE ** -0.5
    delta_row_values = jnp.sum((gradient_rows.astype(jnp.float32) * stored_rows.astype(jnp.float32)).reshape(RESPONSE_TOKENS, KEY_VALUE_HEADS, rollouts_per_group, HEAD_SIZE), axis=-1)
    key_parts, value_parts, prefix_key_parts, prefix_value_parts = [], [], [], []
    for head_position in range(KEY_VALUE_HEADS):
        offset = head_position * rollouts_per_group * HEAD_SIZE
        query_head = query_rows[:, offset:offset + rollouts_per_group * HEAD_SIZE].reshape(RESPONSE_TOKENS, rollouts_per_group, HEAD_SIZE)
        grad_head = gradient_rows[:, offset:offset + rollouts_per_group * HEAD_SIZE].reshape(RESPONSE_TOKENS, rollouts_per_group, HEAD_SIZE)
        key_head = tree_pairs[:, head_position * HEAD_SIZE:(head_position + 1) * HEAD_SIZE]
        value_head = tree_pairs[:, pairing_width + head_position * HEAD_SIZE:pairing_width + (head_position + 1) * HEAD_SIZE]
        prefix_key = prefix_pairs[:, head_position * HEAD_SIZE:(head_position + 1) * HEAD_SIZE]
        prefix_value = prefix_pairs[:, pairing_width + head_position * HEAD_SIZE:pairing_width + (head_position + 1) * HEAD_SIZE]
        scores = jnp.where(allowed[:, None, :], float_einsum("tgd,kd->tgk", query_head, key_head) * scale_factor, masked_score)
        prefix_scores = float_einsum("tgd,kd->tgk", query_head, prefix_key) * scale_factor
        largest = jnp.maximum(jnp.max(scores, axis=-1), jnp.max(prefix_scores, axis=-1))
        summed = jnp.sum(jnp.exp(scores - largest[:, :, None]), axis=-1) + jnp.sum(jnp.exp(prefix_scores - largest[:, :, None]), axis=-1)
        log_total = largest + jnp.log(summed)
        key_grad, value_grad = head_grads(query_head, grad_head, key_head, value_head, allowed, log_total, delta_row_values[:, head_position])
        prefix_key_grad, prefix_value_grad = head_grads(query_head, grad_head, prefix_key, prefix_value, None, log_total, delta_row_values[:, head_position])
        key_parts.append(key_grad)
        value_parts.append(value_grad)
        prefix_key_parts.append(prefix_key_grad)
        prefix_value_parts.append(prefix_value_grad)
    return jnp.concatenate(key_parts + value_parts, axis=-1), jnp.concatenate(prefix_key_parts + prefix_value_parts, axis=-1)


def reference(queries, out_grad, saved_output, key_rows, value_rows, hidden_rows, prefix_keys, prefix_values, prefix_hidden, block_mask, prefix_list, key_down, value_down, key_up, value_up):
    pairing_width = KEY_VALUE_HEADS * HEAD_SIZE
    tree_count = N_SEQ * RESPONSE_TOKENS

    def one_group(group_index):
        query_tree = tree_order(queries[group_index])
        grad_tree = tree_order(out_grad[group_index])
        saved_tree = tree_order(saved_output[group_index])
        pair_tree = tree_order(jnp.concatenate([key_rows[group_index], value_rows[group_index]], axis=-1))
        listed = prefix_list[group_index]
        prefix_pairs = jnp.concatenate([jnp.take(prefix_keys, listed, axis=0), jnp.take(prefix_values, listed, axis=0)], axis=-1).reshape(PL * BLK, 2 * pairing_width)
        mask_rows = block_mask[group_index]

        def one_slice(running, slice_index):
            start = (slice_index * RESPONSE_TOKENS).astype(jnp.int32)
            query_rows = lax.dynamic_slice_in_dim(query_tree, start, RESPONSE_TOKENS, 0)
            gradient_rows = lax.dynamic_slice_in_dim(grad_tree, start, RESPONSE_TOKENS, 0)
            stored_rows = lax.dynamic_slice_in_dim(saved_tree, start, RESPONSE_TOKENS, 0)
            allowed = visible_table(mask_rows, slice_index)
            pair_term, prefix_term = slice_terms(query_rows, gradient_rows, stored_rows, pair_tree, prefix_pairs, allowed)
            rounded = lax.optimization_barrier(pair_term.astype(jnp.bfloat16))
            return (running[0] + rounded.astype(jnp.float32), running[1] + prefix_term), None

        initial = (jnp.zeros((tree_count, 2 * pairing_width), jnp.float32), jnp.zeros((PL * BLK, 2 * pairing_width), jnp.float32))
        (pair_sum, prefix_sum), _ = lax.scan(one_slice, initial, jnp.arange(N_SEQ, dtype=jnp.int32))
        return pair_sum.astype(jnp.bfloat16), prefix_sum

    pair_grads, prefix_terms = lax.map(one_group, jnp.arange(N_GRP, dtype=jnp.int32))
    pool = jnp.zeros((PB_DEV * N_GRP, BLK, 2 * pairing_width), jnp.float32)
    prefix_grads = pool.at[prefix_list.reshape(-1)].add(prefix_terms.reshape(N_GRP * PL, BLK, 2 * pairing_width))

    hidden_tree = jax.vmap(tree_order)(hidden_rows).reshape(-1, D)
    all_hidden = jnp.concatenate([hidden_tree, prefix_hidden.reshape(-1, D)], axis=0)
    all_grads = jnp.concatenate([pair_grads.reshape(-1, 2 * pairing_width), prefix_grads.astype(jnp.bfloat16).reshape(-1, 2 * pairing_width)], axis=0)
    down_pair = jnp.concatenate([key_down, value_down], axis=1)
    projected = jnp.dot(all_hidden, down_pair, preferred_element_type=jnp.float32).astype(jnp.bfloat16)
    back_key = jnp.dot(all_grads[:, :pairing_width], key_up.T, preferred_element_type=jnp.float32)
    back_value = jnp.dot(all_grads[:, pairing_width:], value_up.T, preferred_element_type=jnp.float32)
    back_rows = jnp.concatenate([back_key, back_value], axis=1).astype(jnp.bfloat16)
    down_all = jnp.dot(all_hidden.T, back_rows, preferred_element_type=jnp.float32)
    multiplier = adapter_scale / (N_GRP * N_SEQ)
    down_grads = jnp.stack([down_all[:, :RANK], down_all[:, RANK:]]) * multiplier
    up_key = jnp.dot(projected[:, :RANK].T, all_grads[:, :pairing_width], preferred_element_type=jnp.float32)
    up_value = jnp.dot(projected[:, RANK:].T, all_grads[:, pairing_width:], preferred_element_type=jnp.float32)
    up_grads = jnp.stack([up_key, up_value]) * multiplier
    return (pair_grads, prefix_grads, down_grads, up_grads)
```

```python
import functools

import jax
import jax.numpy as jnp
from jax import lax
from jax.experimental import pallas as pl
from jax.experimental.pallas import tpu as pltpu
from jax.sharding import PartitionSpec as P

HEAD = 128
BLK = 128
NX = 4
SEQ = 16
GRP = 8
REP = 5
KV = 4
ROLLS = 4
SPAN = 8
D = 5120
KVW = 512
TILE = 768
DT = 640
MESH = pl.DeviceIdType.MESH
SCALE = HEAD ** (-0.5)
LOG2E = 1.4426950408889634
MASKED = -1e30
NT = (((1,), (1,)), ((), ()))
TN = (((0,), (0,)), ((), ()))
f32 = jnp.float32
bf16 = jnp.bfloat16


def vmem():
    return pl.BlockSpec(memory_space=pltpu.VMEM)


def hbm():
    return pl.BlockSpec(memory_space=pl.ANY)


def smem():
    return pl.BlockSpec(memory_space=pltpu.SMEM)


def remote(src, dst, send, recv, device):
    copy = pltpu.make_async_remote_copy(
        src_ref=src, dst_ref=dst, send_sem=send, recv_sem=recv, device_id=device, device_id_type=MESH
    )
    copy.start()
    return copy


def greet(devices):
    barrier = pltpu.get_barrier_semaphore()
    for device in devices:
        pl.semaphore_signal(barrier, inc=1, device_id=device, device_id_type=MESH)
    pl.semaphore_wait(barrier, len(devices))


def seq_peers(me):
    return [{"seq": lax.rem(me + o, SEQ)} for o in range(1, SEQ)]


def exchange_kernel(q, g, dl, k, v, qo, go, dlo, ko, vo, send_q, recv_q, send_k, recv_k, own):
    me = lax.axis_index("seq")
    x, y = me // NX, lax.rem(me, NX)
    greet(seq_peers(me))

    def cols(i, width):
        return pl.ds(pl.multiple_of(i * width, 128), width)

    copies = []
    for o in range(1, SEQ):
        d = lax.rem(me + o, SEQ)
        tx = d // NX
        for n, (src, dst) in enumerate(((k, ko), (v, vo))):
            copies.append(
                remote(src.at[:, cols(tx, HEAD)], dst.at[me], send_k.at[n, o], recv_k.at[n, o], {"seq": d})
            )
        if o % NX == 0:
            i = o // NX
            for n, (src, dst) in enumerate(((q, qo), (g, go))):
                copies.append(
                    remote(src.at[:, cols(tx, DT)], dst.at[x], send_q.at[n, i], recv_q.at[n, i], {"seq": d})
                )
            copies.append(remote(dl.at[tx], dlo.at[x], send_q.at[2, i], recv_q.at[2, i], {"seq": d}))
    mine = [
        pltpu.make_async_copy(q.at[:, cols(x, DT)], qo.at[x], own.at[0]),
        pltpu.make_async_copy(g.at[:, cols(x, DT)], go.at[x], own.at[1]),
        pltpu.make_async_copy(k.at[:, cols(x, HEAD)], ko.at[me], own.at[2]),
        pltpu.make_async_copy(v.at[:, cols(x, HEAD)], vo.at[me], own.at[3]),
        pltpu.make_async_copy(dl.at[x], dlo.at[x], own.at[4]),
    ]
    for copy in mine:
        copy.start()
    for copy in copies + mine:
        copy.wait()


def exchange(q, g, dl, k, v):
    return pl.pallas_call(
        exchange_kernel,
        out_shape=(
            jax.ShapeDtypeStruct((ROLLS, BLK, DT), bf16),
            jax.ShapeDtypeStruct((ROLLS, BLK, DT), bf16),
            jax.ShapeDtypeStruct((ROLLS, REP, BLK), f32),
            jax.ShapeDtypeStruct((SEQ, BLK, HEAD), bf16),
            jax.ShapeDtypeStruct((SEQ, BLK, HEAD), bf16),
        ),
        in_specs=[hbm()] * 5,
        out_specs=(hbm(),) * 5,
        scratch_shapes=[
            pltpu.SemaphoreType.DMA((3, NX)),
            pltpu.SemaphoreType.DMA((3, NX)),
            pltpu.SemaphoreType.DMA((2, SEQ)),
            pltpu.SemaphoreType.DMA((2, SEQ)),
            pltpu.SemaphoreType.DMA((5,)),
        ],
        compiler_params=pltpu.CompilerParams(collective_id=0, has_side_effects=True),
        name="exchange",
    )(q, g, dl, k, v)


def attention_kernel(mask, q, g, dl, k, v, pk, pv, out, s_ref, acc, qs, gs, m_ref, l_ref):
    y = lax.rem(lax.axis_index("seq"), NX)
    factor = SCALE * LOG2E
    acc[...] = jnp.zeros_like(acc)
    key_at = lax.broadcasted_iota(jnp.int32, (BLK, BLK), 0)
    query_at = lax.broadcasted_iota(jnp.int32, (BLK, BLK), 1)
    causal = key_at <= query_at

    def rollout(kk, carry):
        r = y + NX * kk
        for t in range(REP):
            qs[t] = q[kk, :, t * HEAD : (t + 1) * HEAD]
            gs[t] = g[kk, :, t * HEAD : (t + 1) * HEAD]
        m_ref[...] = jnp.full_like(m_ref, MASKED)
        l_ref[...] = jnp.zeros_like(l_ref)

        def score(slot, keys, diagonal):
            for t in range(REP):
                s = lax.dot_general(keys, qs[t], NT, preferred_element_type=f32) * factor
                if diagonal:
                    s = jnp.where(causal, s, MASKED)
                s_ref[slot, t] = s
                cut = s.reshape(BLK // 8, 8, BLK)
                before = m_ref[t]
                now = jnp.maximum(before, jnp.max(cut, axis=0))
                part = jnp.sum(jnp.exp2(cut - now[None]), axis=0)
                l_ref[t] = l_ref[t] * jnp.exp2(before - now) + part
                m_ref[t] = now

        for i in range(2):
            score(SEQ + i, pk[i], False)

        def visit(j, c):
            @pl.when(mask[r, j] == 1)
            def _():
                score(j, k[j], False)

            return c

        lax.fori_loop(0, r, visit, 0)
        score(r, k[r], True)

        lses = []
        for t in range(REP):
            top = jnp.max(m_ref[t], axis=0, keepdims=True)
            total = jnp.sum(l_ref[t] * jnp.exp2(m_ref[t] - top), axis=0, keepdims=True)
            lses.append(top + jnp.log2(total))
        for t in range(REP):
            m_ref[t] = jnp.broadcast_to(lses[t], (8, BLK))
            l_ref[t] = jnp.broadcast_to(dl[kk, t : t + 1, :], (8, BLK))

        def grads(slot, values):
            dk = jnp.zeros((BLK, HEAD), f32)
            dv = jnp.zeros((BLK, HEAD), f32)
            for t in range(REP):
                cut = s_ref[slot, t].reshape(BLK // 8, 8, BLK)
                p = jnp.exp2(cut - m_ref[t][None])
                dp = lax.dot_general(values, gs[t], NT, preferred_element_type=f32)
                ds = p * (dp.reshape(BLK // 8, 8, BLK) - l_ref[t][None])
                p = p.reshape(BLK, BLK).astype(bf16)
                ds = ds.reshape(BLK, BLK).astype(bf16)
                dk += jnp.dot(ds, qs[t], preferred_element_type=f32)
                dv += jnp.dot(p, gs[t], preferred_element_type=f32)
            acc[slot, :, 0:HEAD] += dk
            acc[slot, :, HEAD : 2 * HEAD] += dv

        for i in range(2):
            grads(SEQ + i, pv[i])

        def revisit(j, c):
            @pl.when(mask[r, j] == 1)
            def _():
                grads(j, v[j])

            return c

        lax.fori_loop(0, r + 1, revisit, 0)
        return carry

    lax.fori_loop(0, ROLLS, rollout, 0)

    for d in range(SEQ):
        rows = acc[:, d * SPAN : (d + 1) * SPAN, :]
        out[d, :, :, 0:HEAD] = (rows[:, :, 0:HEAD] * SCALE).astype(bf16)
        out[d, :, :, HEAD : 2 * HEAD] = rows[:, :, HEAD : 2 * HEAD].astype(bf16)


def attention(mask, q, g, dl, k, v, pk, pv):
    return pl.pallas_call(
        attention_kernel,
        out_shape=jax.ShapeDtypeStruct((SEQ, SEQ + 2, SPAN, 2 * HEAD), bf16),
        in_specs=[smem()] + [vmem()] * 7,
        out_specs=vmem(),
        scratch_shapes=[
            pltpu.VMEM((SEQ + 2, REP, BLK, BLK), f32),
            pltpu.VMEM((SEQ + 2, BLK, 2 * HEAD), f32),
            pltpu.VMEM((REP, BLK, HEAD), bf16),
            pltpu.VMEM((REP, BLK, HEAD), bf16),
            pltpu.VMEM((REP, 8, BLK), f32),
            pltpu.VMEM((REP, 8, BLK), f32),
        ],
        compiler_params=pltpu.CompilerParams(vmem_limit_bytes=40 * 2**20),
        name="attention",
    )(mask, q, g, dl, k, v, pk, pv)


def gather_kernel(
    listed, terms, proj, up, pair, prefix, back_r, back_p, proj_r,
    rt, pt, rp, bs, send_t, recv_t, send_j, recv_j, send_b, recv_b, send_p, recv_p,
):
    me, grp = lax.axis_index("seq"), lax.axis_index("grp")
    grp_peers = [{"grp": lax.rem(grp + i, GRP)} for i in range(1, GRP)]
    greet(seq_peers(me) + grp_peers)
    copies = []
    tree = []
    for o in range(1, SEQ):
        d = lax.rem(me + o, SEQ)
        tree.append(remote(terms.at[d], rt.at[me], send_t.at[o], recv_t.at[o], {"seq": d}))
    for o in range(1, SEQ):
        d = lax.rem(me + o, SEQ)
        copies.append(remote(proj.at[d], proj_r.at[me], send_j.at[o], recv_j.at[o], {"seq": d}))
    rt[me] = terms[me]
    proj_r[me] = proj[me]
    for copy in tree:
        copy.wait_recv()
    for h in range(KV):
        for side in range(2):
            lanes = slice(side * HEAD, (side + 1) * HEAD)
            place = slice(side * KVW + h * HEAD, side * KVW + (h + 1) * HEAD)
            for i in range(2):
                part = rt[NX * h, SEQ + i, :, lanes].astype(f32)
                for a in range(1, NX):
                    part += rt[NX * h + a, SEQ + i, :, lanes].astype(f32)
                rp[i, :, place] = part
    for b in range(GRP):
        pt[b] = rp[0] * (listed[0, 0] == b).astype(f32) + rp[1] * (listed[0, 1] == b).astype(f32)
    owners = []
    for i in range(1, GRP):
        b = lax.rem(grp + i, GRP)
        owners.append(remote(pt.at[b], rp.at[1 + i], send_p.at[i], recv_p.at[i], {"grp": b}))
    for h in range(KV):
        for side in range(2):
            lanes = slice(side * HEAD, (side + 1) * HEAD)
            place = slice(side * KVW + h * HEAD, side * KVW + (h + 1) * HEAD)
            total = rt[NX * h, 0:SEQ, :, lanes].astype(f32)
            for a in range(1, NX):
                total += rt[NX * h + a, 0:SEQ, :, lanes].astype(f32)
            pair[:, place] = total.reshape(BLK, HEAD).astype(bf16)
    back = lax.dot_general(pair[...], up[...], NT, preferred_element_type=f32)
    bs[...] = back.reshape(SEQ, SPAN, HEAD).astype(bf16)
    for o in range(1, SEQ):
        d = lax.rem(me + o, SEQ)
        copies.append(remote(bs.at[d], back_r.at[me], send_b.at[o], recv_b.at[o], {"seq": d}))
    back_r[me] = bs[me]
    for copy in owners:
        copy.wait_recv()
    total = pt[grp]
    for i in range(1, GRP):
        total += rp[1 + i]
    prefix[...] = total
    back_p[...] = lax.dot_general(total.astype(bf16), up[...], NT, preferred_element_type=f32).astype(bf16)
    for copy in tree + owners:
        copy.wait_send()
    for copy in copies:
        copy.wait()


def gather(listed, terms, proj, up):
    return pl.pallas_call(
        gather_kernel,
        out_shape=(
            jax.ShapeDtypeStruct((BLK, 2 * KVW), bf16),
            jax.ShapeDtypeStruct((SPAN, 2 * KVW), f32),
            jax.ShapeDtypeStruct((SEQ, SPAN, HEAD), bf16),
            jax.ShapeDtypeStruct((SPAN, HEAD), bf16),
            jax.ShapeDtypeStruct((SEQ, SPAN, HEAD), bf16),
        ),
        in_specs=[smem()] + [vmem()] * 3,
        out_specs=(vmem(),) * 5,
        scratch_shapes=[
            pltpu.VMEM((SEQ, SEQ + 2, SPAN, 2 * HEAD), bf16),
            pltpu.VMEM((GRP, SPAN, 2 * KVW), f32),
            pltpu.VMEM((GRP + 1, SPAN, 2 * KVW), f32),
            pltpu.VMEM((SEQ, SPAN, HEAD), bf16),
        ]
        + [pltpu.SemaphoreType.DMA((SEQ,))] * 6
        + [pltpu.SemaphoreType.DMA((GRP,))] * 2,
        compiler_params=pltpu.CompilerParams(
            collective_id=1, has_side_effects=True, vmem_limit_bytes=40 * 2**20
        ),
        name="gather",
    )(listed, terms, proj, up)


def adapters_kernel(
    back, back_p, proj, proj_p, pair, prefix, hidden, hidden_p, out,
    s0, r0, s1, r1, s2, r2, fin, a2,
    send0, recv0, send1, recv1, send2, recv2, send3, recv3, send4, recv4, send5, recv5,
):
    me, grp = lax.axis_index("seq"), lax.axis_index("grp")
    z, c = grp // 2, lax.rem(grp, 2)
    sibling = {"grp": grp + 1 - 2 * c}
    z_peers = [{"grp": lax.rem(z + i, 4) * 2 + c} for i in range(1, 4)]
    greet([sibling] + z_peers + seq_peers(me))

    back_rows = back[...].reshape(BLK, HEAD)
    back_tail = back_p[...].astype(f32)
    proj_rows = proj[...].reshape(BLK, HEAD)
    proj_tail = proj_p[...].astype(f32)
    prefix_low = prefix[...].astype(bf16).astype(f32)
    for core in range(2):
        for zz in range(4):
            b = 2 * zz + core
            cut = slice(b * DT, (b + 1) * DT)
            down = lax.dot_general(back_rows, hidden[:, cut], TN, preferred_element_type=f32)
            down += lax.dot_general(back_tail, hidden_p[:, cut].astype(f32), TN, preferred_element_type=f32)
            s0[core, zz, :, 0:DT] = down.astype(bf16)
            cut = slice(b * HEAD, (b + 1) * HEAD)
            rise = lax.dot_general(proj_rows, pair[:, cut], TN, preferred_element_type=f32)
            rise += lax.dot_general(proj_tail, prefix_low[:, cut], TN, preferred_element_type=f32)
            s0[core, zz, :, DT:TILE] = rise.astype(bf16)
    first = remote(s0.at[1 - c], r0, send0, recv0, sibling)
    first.wait_recv()
    for i in range(4):
        s1[i] = (s0[c, i].astype(f32) + r0[i].astype(f32)).astype(bf16)
    second = []
    for i in range(1, 4):
        tz = lax.rem(z + i, 4)
        second.append(remote(s1.at[tz], r1.at[i - 1], send1.at[i], recv1.at[i], {"grp": tz * 2 + c}))
    for copy in second:
        copy.wait_recv()
    total = s1[z].astype(f32)
    for i in range(3):
        total += r1[i].astype(f32)
    s2[...] = total.reshape(SEQ, SPAN, TILE).astype(bf16)
    third = []
    for o in range(1, SEQ):
        d = lax.rem(me + o, SEQ)
        third.append(remote(s2.at[d], r2.at[o], send2.at[o], recv2.at[o], {"seq": d}))
    for copy in third:
        copy.wait_recv()
    total = s2[me].astype(f32)
    for o in range(1, SEQ):
        total += r2[o].astype(f32)
    fin[...] = total.astype(bf16)
    fourth = []
    for o in range(1, SEQ):
        d = lax.rem(me + o, SEQ)
        fourth.append(remote(fin, a2.at[me], send3.at[o], recv3.at[o], {"seq": d}))
    a2[me] = fin[...]
    for copy in fourth:
        copy.wait_recv()
    fifth = []
    for i in range(1, 4):
        tz = lax.rem(z + i, 4)
        fifth.append(remote(a2, out.at[c, z], send4.at[i], recv4.at[i], {"grp": tz * 2 + c}))
    out[c, z] = a2[...]
    for copy in fifth:
        copy.wait_recv()
    sixth = remote(out.at[c], out.at[c], send5, recv5, sibling)
    sixth.wait_recv()
    for copy in [first] + second + third + fourth + fifth + [sixth]:
        copy.wait_send()


def adapters(back, back_p, proj, proj_p, pair, prefix, hidden, hidden_p):
    dma = pltpu.SemaphoreType.DMA
    return pl.pallas_call(
        adapters_kernel,
        out_shape=jax.ShapeDtypeStruct((2, 4, SEQ, SPAN, TILE), bf16),
        in_specs=[vmem()] * 8,
        out_specs=vmem(),
        scratch_shapes=[
            pltpu.VMEM((2, 4, BLK, TILE), bf16),
            pltpu.VMEM((4, BLK, TILE), bf16),
            pltpu.VMEM((4, BLK, TILE), bf16),
            pltpu.VMEM((3, BLK, TILE), bf16),
            pltpu.VMEM((SEQ, SPAN, TILE), bf16),
            pltpu.VMEM((SEQ, SPAN, TILE), bf16),
            pltpu.VMEM((SPAN, TILE), bf16),
            pltpu.VMEM((SEQ, SPAN, TILE), bf16),
            dma, dma,
            dma((4,)), dma((4,)),
            dma((SEQ,)), dma((SEQ,)),
            dma((SEQ,)), dma((SEQ,)),
            dma((4,)), dma((4,)),
            dma, dma,
        ],
        compiler_params=pltpu.CompilerParams(
            collective_id=2, has_side_effects=True, vmem_limit_bytes=48 * 2**20
        ),
        name="adapters",
    )(back, back_p, proj, proj_p, pair, prefix, hidden, hidden_p)


def on_device(
    queries, out_grad, saved_output, key_rows, value_rows, hidden_rows, prefix_keys, prefix_values,
    prefix_hidden, block_mask, prefix_list, key_down, value_down, key_up, value_up,
):
    me = lax.axis_index("seq")
    x = me // NX
    q, g = queries[0, 0], out_grad[0, 0]
    hidden = hidden_rows[0, 0]
    hidden_p = prefix_hidden[0]
    delta = jnp.sum(
        (g.astype(f32) * saved_output[0, 0].astype(f32)).reshape(BLK, KV * REP, HEAD), axis=-1
    )
    delta = delta.T.reshape(KV, REP, BLK)
    qo, go, dlo, ko, vo = exchange(q, g, delta, key_rows[0, 0], value_rows[0, 0])

    def picked(pool):
        return jnp.concatenate(
            [
                lax.dynamic_slice(pool, (prefix_list[0, i], 0, x * HEAD), (1, BLK, HEAD))
                for i in range(2)
            ]
        )

    terms = attention(
        block_mask[0], qo, go, dlo, ko, vo, picked(prefix_keys), picked(prefix_values)
    )
    down_pair = jnp.concatenate([key_down, value_down], axis=1)
    proj = jnp.dot(hidden, down_pair, preferred_element_type=f32).astype(bf16)
    proj_p = jnp.dot(hidden_p, down_pair, preferred_element_type=f32).astype(bf16)
    gap = jnp.zeros_like(key_up)
    up = jnp.concatenate(
        [jnp.concatenate([key_up, gap], axis=1), jnp.concatenate([gap, value_up], axis=1)], axis=0
    )
    pair, prefix, back_r, back_p, proj_r = gather(
        prefix_list, terms, proj.reshape(SEQ, SPAN, HEAD), up
    )
    summed = adapters(back_r, back_p, proj_r, proj_p, pair, prefix, hidden, hidden_p)
    summed = summed.reshape(2, 4, BLK, TILE)
    factor = 2.0 / (GRP * SEQ)
    down = jnp.transpose(summed[..., :DT], (2, 1, 0, 3)).reshape(2, BLK // 2, D).astype(f32) * factor
    rise = jnp.transpose(summed[..., DT:], (2, 1, 0, 3)).reshape(2, BLK // 2, 2, KVW)
    up_grads = jnp.stack([rise[0, :, 0], rise[1, :, 1]]).astype(f32) * factor
    return pair[None], prefix[None], jnp.swapaxes(down, 1, 2), up_grads


def solution(mesh):
    row = P("grp", "seq", None, None)
    in_specs = (
        row, row, row, row, row, row, P(), P(),
        P("grp", "seq", None), P("grp", None, None), P("grp", None), P(), P(), P(), P(),
    )
    out_specs = (P("grp", "seq", None), P("grp", "seq", None), P(), P())
    return jax.shard_map(
        on_device, mesh=mesh, in_specs=in_specs, out_specs=out_specs, check_vma=False
    )
```

```python
import jax
import jax.numpy as jnp
from jax import lax
from jax.experimental import pallas as pl
from jax.experimental.pallas import tpu as pltpu
from jax.sharding import PartitionSpec as P

HEAD = 128
BLK = 128
NX = 4
SEQ = 16
GRP = 8
REP = 5
KV = 4
SPAN = 8
D = 5120
KVW = 512
DT = 640
TILE = DT + HEAD
W = REP * BLK
TREE = SEQ * BLK
GROUP = 4 * BLK
PAIR = 2 * HEAD
CHUNKS = ((0, 256), (256, 512), (512, 640))
MESH = pl.DeviceIdType.MESH
SCALE = HEAD ** (-0.5)
LOG2E = 1.4426950408889634
MASKED = -1e30
NT = (((1,), (1,)), ((), ()))
TN = (((0,), (0,)), ((), ()))
f32 = jnp.float32
bf16 = jnp.bfloat16


def vmem():
    return pl.BlockSpec(memory_space=pltpu.VMEM)


def hbm():
    return pl.BlockSpec(memory_space=pl.ANY)


def smem():
    return pl.BlockSpec(memory_space=pltpu.SMEM)


def remote(src, dst, send, recv, device):
    copy = pltpu.make_async_remote_copy(
        src_ref=src, dst_ref=dst, send_sem=send, recv_sem=recv, device_id=device, device_id_type=MESH
    )
    copy.start()
    return copy


def greet(devices):
    barrier = pltpu.get_barrier_semaphore()
    for device in devices:
        pl.semaphore_signal(barrier, inc=1, device_id=device, device_id_type=MESH)
    pl.semaphore_wait(barrier, len(devices))


def cols(i, width):
    return pl.ds(pl.multiple_of(i * width, 128), width)


def rows(i, count):
    return pl.ds(pl.multiple_of(i * count, count), count)


def kernel(
    mask, listed, q, g, saved, k, v, hidden, hidden_p, pool_k, pool_v, down_k, down_v, up_k, up_v,
    pair, prefix, out,
    q_in, g_in, delta_in, kv, own_g, own_s, own_h, own_p, down, pool, up, delta_out,
    s_ref, acc, qs, gs, pb, dsb, top, low, diag,
    tsend, rt, proj_s, proj_r, pt, rp, back_s, back_r,
    s0, r0, s1, r1, s2, r2, fin, a2,
    sem_in, kvx_s, kvx_r, kvy_s, kvy_r, q_s, q_r, t_s, t_r, j_s, j_r, b_s, b_r, p_s, p_r,
    s0_s, s0_r, s1_s, s1_r, s2_s, s2_r, a2_s, a2_r, a1_s, a1_r, a0_s, a0_r,
):
    me, grp = lax.axis_index("seq"), lax.axis_index("grp")
    x, y = me // NX, lax.rem(me, NX)
    z, c = grp // 2, lax.rem(grp, 2)
    peers = [lax.rem(me + o, SEQ) for o in range(1, SEQ)]

    def local(src, dst, i):
        copy = pltpu.make_async_copy(src, dst, sem_in.at[i])
        copy.start()
        return copy

    mine = rows(me, BLK)
    keep = [
        local(k.at[:, cols(x, HEAD)], kv.at[mine, 0:HEAD], 0),
        local(v.at[:, cols(x, HEAD)], kv.at[mine, HEAD:PAIR], 1),
        local(q.at[:, cols(x, DT)], q_in.at[x], 2),
        local(g.at[:, cols(x, DT)], g_in.at[x], 3),
        local(g, own_g, 4),
        local(saved, own_s, 5),
        local(hidden, own_h, 6),
        local(down_k, down.at[0:64], 7),
        local(down_v, down.at[64:128], 8),
        local(hidden_p, own_p, 9),
        local(pool_k.at[:, :, cols(x, HEAD)], pool.at[:, :, 0:HEAD], 10),
        local(pool_v.at[:, :, cols(x, HEAD)], pool.at[:, :, HEAD:PAIR], 11),
    ]
    greet([{"seq": d} for d in peers] + [{"grp": lax.rem(grp + i, GRP)} for i in range(1, GRP)])

    step_x = []
    for i in range(1, NX):
        tx = lax.rem(x + i, NX)
        device = {"seq": tx * NX + y}
        step_x.append(
            (
                remote(k.at[:, cols(tx, HEAD)], kv.at[mine, 0:HEAD], kvx_s.at[0, i], kvx_r.at[0, i], device),
                remote(v.at[:, cols(tx, HEAD)], kv.at[mine, HEAD:PAIR], kvx_s.at[1, i], kvx_r.at[1, i], device),
            )
        )
    step_q = []
    for i in range(1, NX):
        tx = lax.rem(x + i, NX)
        device = {"seq": tx * NX + y}
        step_q.append(remote(q.at[:, cols(tx, DT)], q_in.at[x], q_s.at[0, i], q_r.at[0, i], device))
        step_q.append(remote(g.at[:, cols(tx, DT)], g_in.at[x], q_s.at[1, i], q_r.at[1, i], device))
    keep[0].wait()
    keep[1].wait()
    step_y = []
    for n in range(NX):
        if n:
            for copy in step_x[n - 1]:
                copy.wait_recv()
        block = rows(lax.rem(x + NX - n, NX) * NX + y, BLK)
        for i in range(1, NX):
            device = {"seq": x * NX + lax.rem(y + i, NX)}
            step_y.append(remote(kv.at[block], kv.at[block], kvy_s.at[n, i], kvy_r.at[n, i], device))

    keep[4].wait()
    keep[5].wait()
    ones = jnp.ones((8, HEAD), f32)
    for h in range(KV):
        for t in range(REP):
            cut = slice((h * REP + t) * HEAD, (h * REP + t + 1) * HEAD)
            prod = own_g[:, cut].astype(f32) * own_s[:, cut].astype(f32)
            delta_out[h, :, t * BLK : (t + 1) * BLK] = lax.dot_general(
                ones, prod, NT, preferred_element_type=f32, precision=lax.Precision.HIGHEST
            )
    for i in range(1, NX):
        tx = lax.rem(x + i, NX)
        step_q.append(
            remote(delta_out.at[tx], delta_in.at[x], q_s.at[2, i], q_r.at[2, i], {"seq": tx * NX + y})
        )
    delta_in[x] = delta_out[x]

    for i in range(6, 10):
        keep[i].wait()
    proj = lax.dot_general(own_h[...], down[...], NT, preferred_element_type=f32)
    proj_s[...] = proj.reshape(SEQ, SPAN, HEAD).astype(bf16)
    step_j = []
    for o, d in enumerate(peers):
        step_j.append(remote(proj_s.at[d], proj_r.at[me], j_s.at[o], j_r.at[o], {"seq": d}))
    proj_r[me] = proj_s[me]
    proj_tail = lax.dot_general(own_p[...], down[...], NT, preferred_element_type=f32).astype(bf16)
    up[...] = jnp.zeros_like(up)
    up[0:64, 0:KVW] = up_k[...]
    up[64:128, KVW : 2 * KVW] = up_v[...]

    keep[10].wait()
    keep[11].wait()
    for i in range(2):
        kv[TREE + i * BLK : TREE + (i + 1) * BLK, :] = pool[listed[0, i]]
    acc[...] = jnp.zeros_like(acc)
    key_at = lax.broadcasted_iota(jnp.int32, (GROUP, BLK), 0)
    query_at = lax.broadcasted_iota(jnp.int32, (GROUP, BLK), 1)
    diag[...] = jnp.where(key_at <= y * BLK + query_at, 0.0, MASKED).astype(f32)
    keep[2].wait()
    keep[3].wait()
    for copy in step_q + step_y:
        copy.wait_recv()

    def rollout(step, carry):
        kk = NX - 1 - step
        r = y + NX * kk
        for t in range(REP):
            span = slice(t * BLK, (t + 1) * BLK)
            qs[span, :] = q_in[kk, :, span]
            gs[span, :] = g_in[kk, :, span]
        top[...] = jnp.full_like(top, MASKED)
        low[...] = jnp.zeros_like(low)

        def hides(m):
            return [(mask[r, m * 4 + b].astype(f32) - 1.0) * 1e30 for b in range(4)]

        def score(place, hidden_by, diagonal, n):
            for lo, hi in CHUNKS:
                w = hi - lo
                s = lax.dot_general(kv[place, 0:HEAD], qs[lo:hi, :], NT, preferred_element_type=f32)
                s = s * (SCALE * LOG2E)
                if diagonal:
                    s = s + jnp.concatenate([diag[...]] * (w // BLK), axis=1)
                s_ref[place, lo:hi] = s
                cut = s.reshape(n, BLK // 8, 8, w)
                before = top[:, lo:hi]
                now = before
                for b in range(n):
                    now = jnp.maximum(now, jnp.max(cut[b], axis=0) + hidden_by[b])
                part = low[:, lo:hi] * jnp.exp2(before - now)
                for b in range(n):
                    part += jnp.sum(jnp.exp2(cut[b] - (now - hidden_by[b])[None]), axis=0)
                low[:, lo:hi] = part
                top[:, lo:hi] = now

        def score_group(m, cc):
            score(rows(m, GROUP), hides(m), False, 4)
            return cc

        ends = slice(TREE, TREE + 2 * BLK)
        score(ends, [0.0, 0.0], False, 2)
        lax.fori_loop(0, kk, score_group, 0)
        score(rows(kk, GROUP), hides(kk), True, 4)
        best = jnp.max(top[...], axis=0, keepdims=True)
        total = jnp.sum(low[...] * jnp.exp2(top[...] - best), axis=0, keepdims=True)
        top[...] = jnp.broadcast_to(best + jnp.log2(total), (8, W))
        low[...] = delta_in[kk]

        def grads(place, hidden_by, n):
            for lo, hi in CHUNKS:
                w = hi - lo
                dp = lax.dot_general(kv[place, HEAD:PAIR], gs[lo:hi, :], NT, preferred_element_type=f32)
                dp = dp.reshape(n, BLK // 8, 8, w)
                cut = s_ref[place, lo:hi].reshape(n, BLK // 8, 8, w)
                for b in range(n):
                    span = slice(b * BLK, (b + 1) * BLK)
                    p = jnp.exp2(cut[b] - (top[:, lo:hi] - hidden_by[b])[None])
                    ds = p * (dp[b] - low[:, lo:hi][None])
                    pb[span, lo:hi] = p.reshape(BLK, w).astype(bf16)
                    dsb[span, lo:hi] = ds.reshape(BLK, w).astype(bf16)
            acc[place, 0:HEAD] += jnp.dot(dsb[0 : n * BLK, :], qs[...], preferred_element_type=f32)
            acc[place, HEAD:PAIR] += jnp.dot(pb[0 : n * BLK, :], gs[...], preferred_element_type=f32)

        def grads_group(m, cc):
            grads(rows(m, GROUP), hides(m), 4)
            return cc

        grads(ends, [0.0, 0.0], 2)
        lax.fori_loop(0, kk + 1, grads_group, 0)

        for b in range(4):
            j = kk * 4 + b
            part = acc[rows(j, BLK), :].reshape(SEQ, SPAN, PAIR)
            tsend[:, j, :, 0:HEAD] = (part[:, :, 0:HEAD] * SCALE).astype(bf16)
            tsend[:, j, :, HEAD:PAIR] = part[:, :, HEAD:PAIR].astype(bf16)

        @pl.when(step < NX - 1)
        def _():
            for o, d in enumerate(peers):
                four = pl.ds(kk * 4, 4)
                remote(tsend.at[d, four], rt.at[me, four], t_s.at[kk, o], t_r.at[kk, o], {"seq": d})

        return carry

    lax.fori_loop(0, NX, rollout, 0)
    for i in range(2):
        part = acc[TREE + i * BLK : TREE + (i + 1) * BLK, :].reshape(SEQ, SPAN, PAIR)
        tsend[:, SEQ + i, :, 0:HEAD] = (part[:, :, 0:HEAD] * SCALE).astype(bf16)
        tsend[:, SEQ + i, :, HEAD:PAIR] = part[:, :, HEAD:PAIR].astype(bf16)
    step_e = []
    two = pl.ds(SEQ, 2)
    for o, d in enumerate(peers):
        step_e.append(remote(tsend.at[d, two], rt.at[me, two], t_s.at[4, o], t_r.at[4, o], {"seq": d}))
    step_t = []
    for kk in range(NX):
        four = pl.ds(kk * 4, 4)
        for o, d in enumerate(peers):
            copy = pltpu.make_async_remote_copy(
                src_ref=tsend.at[d, four], dst_ref=rt.at[me, four], send_sem=t_s.at[kk, o],
                recv_sem=t_r.at[kk, o], device_id={"seq": d}, device_id_type=MESH,
            )
            if kk == 0:
                copy.start()
            step_t.append(copy)
    rt[me] = tsend[me]
    for copy in step_e:
        copy.wait_recv()
    for h in range(KV):
        for side in range(2):
            lanes = slice(side * HEAD, (side + 1) * HEAD)
            place = slice(side * KVW + h * HEAD, side * KVW + (h + 1) * HEAD)
            for i in range(2):
                part = rt[NX * h, SEQ + i, :, lanes].astype(f32)
                for a in range(1, NX):
                    part += rt[NX * h + a, SEQ + i, :, lanes].astype(f32)
                rp[i, :, place] = part
    for b in range(GRP):
        pt[b] = rp[0] * (listed[0, 0] == b).astype(f32) + rp[1] * (listed[0, 1] == b).astype(f32)
    step_p = []
    for i in range(1, GRP):
        b = lax.rem(grp + i, GRP)
        step_p.append(remote(pt.at[b], rp.at[1 + i], p_s.at[i], p_r.at[i], {"grp": b}))
    for copy in step_t:
        copy.wait_recv()
    for h in range(KV):
        for side in range(2):
            lanes = slice(side * HEAD, (side + 1) * HEAD)
            place = slice(side * KVW + h * HEAD, side * KVW + (h + 1) * HEAD)
            total = rt[NX * h, 0:SEQ, :, lanes].astype(f32)
            for a in range(1, NX):
                total += rt[NX * h + a, 0:SEQ, :, lanes].astype(f32)
            pair[:, place] = total.reshape(BLK, HEAD).astype(bf16)
    back = lax.dot_general(pair[...], up[...], NT, preferred_element_type=f32)
    back_s[...] = back.reshape(SEQ, SPAN, HEAD).astype(bf16)
    step_b = []
    for o, d in enumerate(peers):
        step_b.append(remote(back_s.at[d], back_r.at[me], b_s.at[o], b_r.at[o], {"seq": d}))
    back_r[me] = back_s[me]
    for copy in step_p:
        copy.wait_recv()
    total = pt[grp]
    for i in range(1, GRP):
        total += rp[1 + i]
    prefix[...] = total
    prefix_low = total.astype(bf16)
    back_tail = lax.dot_general(prefix_low, up[...], NT, preferred_element_type=f32).astype(bf16)
    for copy in step_j:
        copy.wait_recv()
    proj_rows = proj_r[...].reshape(BLK, HEAD)
    proj_tail = proj_tail.astype(f32)
    prefix_low = prefix_low.astype(f32)
    for b in range(GRP):
        cut = slice(b * HEAD, (b + 1) * HEAD)
        rise = lax.dot_general(proj_rows, pair[:, cut], TN, preferred_element_type=f32)
        rise += lax.dot_general(proj_tail, prefix_low[:, cut], TN, preferred_element_type=f32)
        s0[b % 2, b // 2, :, DT:TILE] = rise.astype(bf16)
    for copy in step_b:
        copy.wait_recv()

    back_rows = back_r[...].reshape(BLK, HEAD)
    back_tail = back_tail.astype(f32)
    for b in range(GRP):
        cut = slice(b * DT, (b + 1) * DT)
        part = lax.dot_general(back_rows, own_h[:, cut], TN, preferred_element_type=f32)
        part += lax.dot_general(back_tail, own_p[:, cut].astype(f32), TN, preferred_element_type=f32)
        s0[b % 2, b // 2, :, 0:DT] = part.astype(bf16)
    sibling = {"grp": grp + 1 - 2 * c}
    first = remote(s0.at[1 - c], r0, s0_s, s0_r, sibling)
    first.wait_recv()
    for i in range(4):
        s1[i] = (s0[c, i].astype(f32) + r0[i].astype(f32)).astype(bf16)
    second = []
    for i in range(1, 4):
        tz = lax.rem(z + i, 4)
        second.append(remote(s1.at[tz], r1.at[i - 1], s1_s.at[i], s1_r.at[i], {"grp": tz * 2 + c}))
    for copy in second:
        copy.wait_recv()
    total = s1[z].astype(f32)
    for i in range(3):
        total += r1[i].astype(f32)
    s2[...] = total.reshape(SEQ, SPAN, TILE).astype(bf16)
    third = []
    for o, d in enumerate(peers):
        third.append(remote(s2.at[d], r2.at[o], s2_s.at[o], s2_r.at[o], {"seq": d}))
    for copy in third:
        copy.wait_recv()
    total = s2[me].astype(f32)
    for o in range(SEQ - 1):
        total += r2[o].astype(f32)
    fin[...] = total.astype(bf16)
    fourth = []
    for o, d in enumerate(peers):
        fourth.append(remote(fin, a2.at[me], a2_s.at[o], a2_r.at[o], {"seq": d}))
    a2[me] = fin[...]
    for copy in fourth:
        copy.wait_recv()
    fifth = []
    for i in range(1, 4):
        tz = lax.rem(z + i, 4)
        fifth.append(remote(a2, out.at[c, z], a1_s.at[i], a1_r.at[i], {"grp": tz * 2 + c}))
    out[c, z] = a2[...]
    for copy in fifth:
        copy.wait_recv()
    sixth = remote(out.at[c], out.at[c], a0_s, a0_r, sibling)
    sixth.wait_recv()

    for pairs in step_x:
        for copy in pairs:
            copy.wait_send()
    for copy in (
        step_q + step_y + step_j + step_e + step_t + step_p + step_b
        + [first] + second + third + fourth + fifth + [sixth]
    ):
        copy.wait_send()


def backward(*operands):
    dma = pltpu.SemaphoreType.DMA

    def low(*shape):
        return pltpu.VMEM(shape, bf16)

    def wide(*shape):
        return pltpu.VMEM(shape, f32)

    return pl.pallas_call(
        kernel,
        out_shape=(
            jax.ShapeDtypeStruct((BLK, 2 * KVW), bf16),
            jax.ShapeDtypeStruct((SPAN, 2 * KVW), f32),
            jax.ShapeDtypeStruct((2, 4, SEQ, SPAN, TILE), bf16),
        ),
        in_specs=[smem()] * 2 + [hbm()] * 11 + [vmem()] * 2,
        out_specs=(vmem(),) * 3,
        scratch_shapes=[
            low(NX, BLK, DT), low(NX, BLK, DT), wide(NX, 8, W), low(TREE + 2 * BLK, PAIR),
            low(BLK, 4 * DT), low(BLK, 4 * DT), low(BLK, D), low(SPAN, D), low(HEAD, D),
            low(GRP, BLK, PAIR), low(HEAD, 2 * KVW), wide(KV, 8, W),
            wide(TREE + 2 * BLK, W), wide(TREE + 2 * BLK, PAIR), low(W, HEAD), low(W, HEAD),
            low(GROUP, W), low(GROUP, W), wide(8, W), wide(8, W), wide(GROUP, BLK),
            low(SEQ, SEQ + 2, SPAN, PAIR), low(SEQ, SEQ + 2, SPAN, PAIR),
            low(SEQ, SPAN, HEAD), low(SEQ, SPAN, HEAD),
            wide(GRP, SPAN, 2 * KVW), wide(GRP + 1, SPAN, 2 * KVW),
            low(SEQ, SPAN, HEAD), low(SEQ, SPAN, HEAD),
            low(2, 4, BLK, TILE), low(4, BLK, TILE), low(4, BLK, TILE), low(3, BLK, TILE),
            low(SEQ, SPAN, TILE), low(SEQ, SPAN, TILE), low(SPAN, TILE), low(SEQ, SPAN, TILE),
            dma((12,)),
            dma((2, NX)), dma((2, NX)), dma((NX, NX)), dma((NX, NX)), dma((3, NX)), dma((3, NX)),
            dma((5, SEQ)), dma((5, SEQ)), dma((SEQ,)), dma((SEQ,)), dma((SEQ,)), dma((SEQ,)),
            dma((GRP,)), dma((GRP,)),
            dma, dma, dma((4,)), dma((4,)), dma((SEQ,)), dma((SEQ,)), dma((SEQ,)), dma((SEQ,)),
            dma((4,)), dma((4,)), dma, dma,
        ],
        compiler_params=pltpu.CompilerParams(
            collective_id=0, has_side_effects=True, vmem_limit_bytes=56 * 2**20
        ),
        name="backward",
    )(*operands)


def spread_kernel(summed, down, rise):
    factor = 2.0 / (GRP * SEQ)
    b = pl.program_id(0)
    part = summed[0, 0].reshape(BLK, TILE).astype(f32) * factor
    down[...] = part[:, 0:DT]
    rise[0] = jnp.where(b < 4, part[0:64, DT:TILE], part[64:128, DT:TILE])


def spread(summed):
    return pl.pallas_call(
        spread_kernel,
        grid=(GRP,),
        out_shape=(
            jax.ShapeDtypeStruct((BLK, D), f32),
            jax.ShapeDtypeStruct((2, 64, KVW), f32),
        ),
        in_specs=[pl.BlockSpec((1, 1, SEQ, SPAN, TILE), lambda b: (b % 2, b // 2, 0, 0, 0))],
        out_specs=(
            pl.BlockSpec((BLK, DT), lambda b: (0, b)),
            pl.BlockSpec((1, 64, HEAD), lambda b: (b // 4, 0, b % 4)),
        ),
        name="spread",
    )(summed)


def on_device(
    queries, out_grad, saved_output, key_rows, value_rows, hidden_rows, prefix_keys, prefix_values,
    prefix_hidden, block_mask, prefix_list, key_down, value_down, key_up, value_up,
):
    pair, prefix, summed = backward(
        block_mask[0], prefix_list, queries[0, 0], out_grad[0, 0], saved_output[0, 0],
        key_rows[0, 0], value_rows[0, 0], hidden_rows[0, 0], prefix_hidden[0],
        prefix_keys, prefix_values, key_down.T, value_down.T, key_up, value_up,
    )
    down, rise = spread(summed)
    down = jnp.swapaxes(down.reshape(2, BLK // 2, D), 1, 2)
    return pair[None], prefix[None], down, rise


def solution(mesh):
    row = P("grp", "seq", None, None)
    in_specs = (
        row, row, row, row, row, row, P(), P(),
        P("grp", "seq", None), P("grp", None, None), P("grp", None), P(), P(), P(), P(),
    )
    out_specs = (P("grp", "seq", None), P("grp", "seq", None), P(), P())
    return jax.shard_map(
        on_device, mesh=mesh, in_specs=in_specs, out_specs=out_specs, check_vma=False
    )
```

```python
import jax
import jax.numpy as jnp
from jax import lax
from jax.experimental import pallas as pl
from jax.experimental.pallas import tpu as pltpu
from jax.sharding import PartitionSpec as P

HEAD = 128
BLK = 128
NX = 4
SEQ = 16
GRP = 8
REP = 5
KV = 4
SPAN = 8
D = 5120
KVW = 512
DT = 640
TILE = 256
DEPTH = 144
TYPES = 3
W = REP * BLK
TREE = SEQ * BLK
GROUP = 4 * BLK
PAIR = 2 * HEAD
CHUNKS = ((0, 256), (256, 512), (512, 640))
MESH = pl.DeviceIdType.MESH
SCALE = HEAD ** (-0.5)
LOG2E = 1.4426950408889634
MASKED = -1e30
NT = (((1,), (1,)), ((), ()))
TN = (((0,), (0,)), ((), ()))
f32 = jnp.float32
bf16 = jnp.bfloat16


def vmem():
    return pl.BlockSpec(memory_space=pltpu.VMEM)


def hbm():
    return pl.BlockSpec(memory_space=pl.ANY)


def smem():
    return pl.BlockSpec(memory_space=pltpu.SMEM)


def remote(src, dst, send, recv, device):
    copy = pltpu.make_async_remote_copy(
        src_ref=src, dst_ref=dst, send_sem=send, recv_sem=recv, device_id=device, device_id_type=MESH
    )
    copy.start()
    return copy


def greet(devices):
    barrier = pltpu.get_barrier_semaphore()
    for device in devices:
        pl.semaphore_signal(barrier, inc=1, device_id=device, device_id_type=MESH)


def greeted(devices):
    pl.semaphore_wait(pltpu.get_barrier_semaphore(), len(devices))


def cols(i, width):
    return pl.ds(pl.multiple_of(i * width, 128), width)


def rows(i, count):
    return pl.ds(pl.multiple_of(i * count, count), count)


def kernel(
    mask, listed, q, g, saved, k, v, hidden, hidden_p, pool_k, pool_v, down_k, down_v, up_k, up_v,
    pair, prefix, out,
    q_in, g_in, delta_in, kv, own_g, own_s, own_h, own_p, down, pool, up, delta_out, all_g, back_all, back_t, proj_all, proj_t,
    s_ref, acc, qs, gs, pb, dsb, top, low, diag,
    tsend, rt, proj_s, proj_r, pt, rp, back_s, back_r,
    s0, r0, s1, r1, s2, r2,
    sem_in, kvx_s, kvx_r, kvy_s, kvy_r, q_s, q_r, t_s, t_r, j_s, j_r, b_s, b_r, p_s, p_r,
    s0_s, s0_r, s1_s, s1_r, s2_s, s2_r, a2_s, a2_r, a1_s, a1_r, a0_s, a0_r,
):
    me, grp = lax.axis_index("seq"), lax.axis_index("grp")
    x, y = me // NX, lax.rem(me, NX)
    z, c = grp // 2, lax.rem(grp, 2)
    peers = [lax.rem(me + o, SEQ) for o in range(1, SEQ)]

    def at(xx, yy, zz):
        return {"seq": xx * NX + yy, "grp": zz * 2 + c}

    def line(t, i):
        n = [lax.rem(place + i, NX) for place in (z, x, y)]
        return (at(x, y, n[0]), at(n[1], y, z), at(x, n[2], z))[t]

    def plane(t, e):
        u, w = e // NX, lax.rem(e, NX)
        return (at(u, w, z), at(x, u, w), at(u, y, w))[t]

    on_line = (z, x, y)
    on_plane = (me, y * NX + z, x * NX + z)
    met = [{"grp": lax.rem(grp + i, GRP)} for i in range(1, GRP)]
    met += [{"seq": d} for d in peers]
    for i in range(1, NX):
        for j in range(1, NX):
            met.append(at(x, lax.rem(y + i, NX), lax.rem(z + j, NX)))
            met.append(at(lax.rem(x + i, NX), y, lax.rem(z + j, NX)))
    greet(met)

    def local(src, dst, i):
        copy = pltpu.make_async_copy(src, dst, sem_in.at[i])
        copy.start()
        return copy

    mine = rows(me, BLK)
    keep = [
        local(k.at[:, cols(x, HEAD)], kv.at[mine, 0:HEAD], 0),
        local(v.at[:, cols(x, HEAD)], kv.at[mine, HEAD:PAIR], 1),
        local(q.at[:, cols(x, DT)], q_in.at[x], 2),
        local(g.at[:, cols(x, DT)], g_in.at[x], 3),
        local(g, own_g, 4),
        local(saved, own_s, 5),
        local(hidden, own_h.at[0:BLK], 6),
        local(down_k, down.at[0:64], 7),
        local(down_v, down.at[64:128], 8),
        local(hidden_p, own_p, 9),
        local(pool_k.at[:, :, cols(x, HEAD)], pool.at[:, :, 0:HEAD], 10),
        local(pool_v.at[:, :, cols(x, HEAD)], pool.at[:, :, HEAD:PAIR], 11),
    ]
    keep[4].wait()
    keep[5].wait()
    ones = jnp.ones((8, HEAD), f32)
    for h in range(KV):
        for t in range(REP):
            cut = slice((h * REP + t) * HEAD, (h * REP + t + 1) * HEAD)
            prod = own_g[:, cut].astype(f32) * own_s[:, cut].astype(f32)
            delta_out[h, :, t * BLK : (t + 1) * BLK] = lax.dot_general(
                ones, prod, NT, preferred_element_type=f32, precision=lax.Precision.HIGHEST
            )
    delta_in[x] = delta_out[x]
    greeted(met)

    step_x = []
    for i in range(1, NX):
        tx = lax.rem(x + i, NX)
        device = {"seq": tx * NX + y}
        step_x.append(
            (
                remote(k.at[:, cols(tx, HEAD)], kv.at[mine, 0:HEAD], kvx_s.at[0, i], kvx_r.at[0, i], device),
                remote(v.at[:, cols(tx, HEAD)], kv.at[mine, HEAD:PAIR], kvx_s.at[1, i], kvx_r.at[1, i], device),
            )
        )
    keep[0].wait()
    keep[1].wait()
    step_y = []

    def forward(n):
        block = rows(lax.rem(x + NX - n, NX) * NX + y, BLK)
        for i in range(1, NX):
            device = {"seq": x * NX + lax.rem(y + i, NX)}
            step_y.append(remote(kv.at[block], kv.at[block], kvy_s.at[n, i], kvy_r.at[n, i], device))

    forward(0)
    step_q = []
    for i in range(1, NX):
        tx = lax.rem(x + i, NX)
        device = {"seq": tx * NX + y}
        step_q.append(remote(delta_out.at[tx], delta_in.at[x], q_s.at[2, i], q_r.at[2, i], device))
    for i in range(1, NX):
        tx = lax.rem(x + i, NX)
        device = {"seq": tx * NX + y}
        step_q.append(remote(q.at[:, cols(tx, DT)], q_in.at[x], q_s.at[0, i], q_r.at[0, i], device))
        step_q.append(remote(g.at[:, cols(tx, DT)], g_in.at[x], q_s.at[1, i], q_r.at[1, i], device))
    for n in (1, 3, 2):
        for copy in step_x[n - 1]:
            copy.wait_recv()
        forward(n)

    for i in range(6, 10):
        keep[i].wait()
    own_h[BLK : BLK + SPAN, :] = own_p[...]
    own_h[BLK + SPAN : DEPTH, :] = jnp.zeros((SPAN, D), bf16)
    proj = lax.dot_general(own_h[...], down[...], NT, preferred_element_type=f32)
    proj_s[...] = proj[0:BLK].reshape(SEQ, SPAN, HEAD).astype(bf16)
    proj_all[BLK:DEPTH, :] = proj[BLK:DEPTH].astype(bf16)
    step_j = []
    for o, d in enumerate(peers):
        step_j.append(remote(proj_s.at[d], proj_r.at[me], j_s.at[o], j_r.at[o], {"seq": d}))
    proj_r[me] = proj_s[me]
    up[...] = jnp.zeros_like(up)
    up[0:64, 0:KVW] = up_k[...]
    up[64:128, KVW : 2 * KVW] = up_v[...]

    keep[10].wait()
    keep[11].wait()
    for i in range(2):
        kv[TREE + i * BLK : TREE + (i + 1) * BLK, :] = pool[listed[0, i]]
    acc[...] = jnp.zeros_like(acc)
    key_at = lax.broadcasted_iota(jnp.int32, (GROUP, BLK), 0)
    query_at = lax.broadcasted_iota(jnp.int32, (GROUP, BLK), 1)
    diag[...] = jnp.where(key_at <= y * BLK + query_at, 0.0, MASKED).astype(f32)
    keep[2].wait()
    keep[3].wait()
    for copy in step_q + step_y:
        copy.wait_recv()

    def rollout(step, carry):
        kk = NX - 1 - step
        r = y + NX * kk
        for t in range(REP):
            span = slice(t * BLK, (t + 1) * BLK)
            qs[span, :] = q_in[kk, :, span]
            gs[span, :] = g_in[kk, :, span]
        top[...] = jnp.full_like(top, MASKED)
        low[...] = jnp.zeros_like(low)

        def hides(m):
            return [(mask[r, m * 4 + b].astype(f32) - 1.0) * 1e30 for b in range(4)]

        def score(place, hidden_by, diagonal, n):
            for lo, hi in CHUNKS:
                w = hi - lo
                s = lax.dot_general(kv[place, 0:HEAD], qs[lo:hi, :], NT, preferred_element_type=f32)
                s = s * (SCALE * LOG2E)
                if diagonal:
                    s = s + jnp.concatenate([diag[...]] * (w // BLK), axis=1)
                s_ref[place, lo:hi] = s
                cut = s.reshape(n, BLK // 8, 8, w)
                before = top[:, lo:hi]
                now = before
                for b in range(n):
                    now = jnp.maximum(now, jnp.max(cut[b], axis=0) + hidden_by[b])
                part = low[:, lo:hi] * jnp.exp2(before - now)
                for b in range(n):
                    part += jnp.sum(jnp.exp2(cut[b] - (now - hidden_by[b])[None]), axis=0)
                low[:, lo:hi] = part
                top[:, lo:hi] = now

        def score_group(m, cc):
            score(rows(m, GROUP), hides(m), False, 4)
            return cc

        ends = slice(TREE, TREE + 2 * BLK)
        score(ends, [0.0, 0.0], False, 2)
        lax.fori_loop(0, kk, score_group, 0)
        score(rows(kk, GROUP), hides(kk), True, 4)
        best = jnp.max(top[...], axis=0, keepdims=True)
        total = jnp.sum(low[...] * jnp.exp2(top[...] - best), axis=0, keepdims=True)
        top[...] = jnp.broadcast_to(best + jnp.log2(total), (8, W))
        low[...] = delta_in[kk]

        def grads(place, hidden_by, n):
            for lo, hi in CHUNKS:
                w = hi - lo
                dp = lax.dot_general(kv[place, HEAD:PAIR], gs[lo:hi, :], NT, preferred_element_type=f32)
                dp = dp.reshape(n, BLK // 8, 8, w)
                cut = s_ref[place, lo:hi].reshape(n, BLK // 8, 8, w)
                for b in range(n):
                    span = slice(b * BLK, (b + 1) * BLK)
                    p = jnp.exp2(cut[b] - (top[:, lo:hi] - hidden_by[b])[None])
                    ds = p * (dp[b] - low[:, lo:hi][None])
                    pb[span, lo:hi] = p.reshape(BLK, w).astype(bf16)
                    dsb[span, lo:hi] = ds.reshape(BLK, w).astype(bf16)
            acc[place, 0:HEAD] += jnp.dot(dsb[0 : n * BLK, :], qs[...], preferred_element_type=f32)
            acc[place, HEAD:PAIR] += jnp.dot(pb[0 : n * BLK, :], gs[...], preferred_element_type=f32)

        def grads_group(m, cc):
            grads(rows(m, GROUP), hides(m), 4)
            return cc

        grads(ends, [0.0, 0.0], 2)
        lax.fori_loop(0, kk + 1, grads_group, 0)

        for b in range(4):
            j = kk * 4 + b
            part = acc[rows(j, BLK), :].reshape(SEQ, SPAN, PAIR)
            tsend[:, j, :, 0:HEAD] = (part[:, :, 0:HEAD] * SCALE).astype(bf16)
            tsend[:, j, :, HEAD:PAIR] = part[:, :, HEAD:PAIR].astype(bf16)

        @pl.when(step < NX - 1)
        def _():
            for o, d in enumerate(peers):
                four = pl.ds(kk * 4, 4)
                remote(tsend.at[d, four], rt.at[me, four], t_s.at[kk, o], t_r.at[kk, o], {"seq": d})

        return carry

    lax.fori_loop(0, NX, rollout, 0)
    for i in range(2):
        part = acc[TREE + i * BLK : TREE + (i + 1) * BLK, :].reshape(SEQ, SPAN, PAIR)
        tsend[:, SEQ + i, :, 0:HEAD] = (part[:, :, 0:HEAD] * SCALE).astype(bf16)
        tsend[:, SEQ + i, :, HEAD:PAIR] = part[:, :, HEAD:PAIR].astype(bf16)
    step_e = []
    two = pl.ds(SEQ, 2)
    for o, d in enumerate(peers):
        step_e.append(remote(tsend.at[d, two], rt.at[me, two], t_s.at[4, o], t_r.at[4, o], {"seq": d}))
    step_t = []
    for kk in range(NX):
        four = pl.ds(kk * 4, 4)
        for o, d in enumerate(peers):
            copy = pltpu.make_async_remote_copy(
                src_ref=tsend.at[d, four], dst_ref=rt.at[me, four], send_sem=t_s.at[kk, o],
                recv_sem=t_r.at[kk, o], device_id={"seq": d}, device_id_type=MESH,
            )
            if kk == 0:
                copy.start()
            step_t.append(copy)
    rt[me] = tsend[me]
    for copy in step_e:
        copy.wait_recv()
    for h in range(KV):
        for side in range(2):
            lanes = slice(side * HEAD, (side + 1) * HEAD)
            place = slice(side * KVW + h * HEAD, side * KVW + (h + 1) * HEAD)
            for i in range(2):
                part = rt[NX * h, SEQ + i, :, lanes].astype(f32)
                for a in range(1, NX):
                    part += rt[NX * h + a, SEQ + i, :, lanes].astype(f32)
                rp[i, :, place] = part
    for b in range(GRP):
        pt[b] = rp[0] * (listed[0, 0] == b).astype(f32) + rp[1] * (listed[0, 1] == b).astype(f32)
    step_p = []
    for i in range(1, GRP):
        b = lax.rem(grp + i, GRP)
        step_p.append(remote(pt.at[b], rp.at[1 + i], p_s.at[i], p_r.at[i], {"grp": b}))
    for copy in step_t:
        copy.wait_recv()
    for h in range(KV):
        for side in range(2):
            lanes = slice(side * HEAD, (side + 1) * HEAD)
            place = slice(side * KVW + h * HEAD, side * KVW + (h + 1) * HEAD)
            total = rt[NX * h, 0:SEQ, :, lanes].astype(f32)
            for a in range(1, NX):
                total += rt[NX * h + a, 0:SEQ, :, lanes].astype(f32)
            all_g[0:BLK, place] = total.reshape(BLK, HEAD).astype(bf16)
    back = lax.dot_general(all_g[0:BLK, :], up[...], NT, preferred_element_type=f32)
    back_s[...] = back.reshape(SEQ, SPAN, HEAD).astype(bf16)
    step_b = []
    for o, d in enumerate(peers):
        step_b.append(remote(back_s.at[d], back_r.at[me], b_s.at[o], b_r.at[o], {"seq": d}))
    back_r[me] = back_s[me]
    for copy in step_p:
        copy.wait_recv()
    total = pt[grp]
    for i in range(1, GRP):
        total += rp[1 + i]
    prefix[...] = total
    tail = jnp.concatenate([total, jnp.zeros_like(total)], axis=0).astype(bf16)
    all_g[BLK:DEPTH, :] = tail
    back_all[BLK:DEPTH, :] = lax.dot_general(tail, up[...], NT, preferred_element_type=f32).astype(bf16)
    pair[...] = all_g[0:BLK, :]
    for copy in step_j:
        copy.wait_recv()
    proj_all[0:BLK, :] = proj_r[...].reshape(BLK, HEAD)
    same = lax.broadcasted_iota(jnp.int32, (HEAD, HEAD), 0) == lax.broadcasted_iota(jnp.int32, (HEAD, HEAD), 1)
    eye = same.astype(f32).astype(bf16)
    proj_t[...] = lax.dot_general(eye, proj_all[...], NT, preferred_element_type=f32).astype(bf16)
    for a in range(NX):
        cut = slice(a * TILE, (a + 1) * TILE)
        s0[1, 2, a] = jnp.dot(proj_t[...], all_g[:, cut], preferred_element_type=f32).astype(bf16)
    for copy in step_b:
        copy.wait_recv()

    back_all[0:BLK, :] = back_r[...].reshape(BLK, HEAD)
    back_t[...] = lax.dot_general(eye, back_all[...], NT, preferred_element_type=f32).astype(bf16)
    sibling = {"grp": grp + 1 - 2 * c}
    zero, first, second, third, fourth, fifth = [], [], [], [], [], []
    for t in range(TYPES):
        for half in range(2):
            for a in range(NX):
                n = (half * TYPES + t) * NX + a
                if n < D // TILE:
                    cut = slice(n * TILE, (n + 1) * TILE)
                    part = jnp.dot(back_t[...], own_h[:, cut], preferred_element_type=f32)
                    s0[half, t, a] = part.astype(bf16)
        zero.append(remote(s0.at[1 - c, t], r0.at[t], s0_s.at[t], s0_r.at[t], sibling))
    for t in range(TYPES):
        zero[t].wait_recv()
        for a in range(NX):
            s1[t, a] = (s0[c, t, a].astype(f32) + r0[t, a].astype(f32)).astype(bf16)
        for i in range(1, NX):
            there = lax.rem(on_line[t] + i, NX)
            first.append(remote(s1.at[t, there], r1.at[t, i - 1], s1_s.at[t, i], s1_r.at[t, i], line(t, i)))
    for t in range(TYPES):
        for copy in first[t * 3 : t * 3 + 3]:
            copy.wait_recv()
        total = s1[t, on_line[t]].astype(f32)
        for i in range(NX - 1):
            total += r1[t, i].astype(f32)
        s2[t] = total.reshape(SEQ, SPAN, TILE).astype(bf16)
        for o in range(SEQ - 1):
            e = lax.rem(on_plane[t] + o + 1, SEQ)
            second.append(remote(s2.at[t, e], r2.at[t, o], s2_s.at[t, o], s2_r.at[t, o], plane(t, e)))
    for t in range(TYPES):
        for copy in second[t * 15 : t * 15 + 15]:
            copy.wait_recv()
        total = s2[t, on_plane[t]].astype(f32)
        for o in range(SEQ - 1):
            total += r2[t, o].astype(f32)
        out[c, t, on_line[t], on_plane[t]] = total.astype(bf16)
        piece = out.at[c, t, on_line[t], on_plane[t]]
        for o in range(SEQ - 1):
            e = lax.rem(on_plane[t] + o + 1, SEQ)
            third.append(remote(piece, piece, a2_s.at[t, o], a2_r.at[t, o], plane(t, e)))
    for t in range(TYPES):
        for copy in third[t * 15 : t * 15 + 15]:
            copy.wait_recv()
        piece = out.at[c, t, on_line[t]]
        for i in range(1, NX):
            fourth.append(remote(piece, piece, a1_s.at[t, i], a1_r.at[t, i], line(t, i)))
    for t in range(TYPES):
        for copy in fourth[t * 3 : t * 3 + 3]:
            copy.wait_recv()
        fifth.append(remote(out.at[c, t], out.at[c, t], a0_s.at[t], a0_r.at[t], sibling))
    for copy in fifth:
        copy.wait_recv()

    for pairs in step_x:
        for copy in pairs:
            copy.wait_send()
    for copy in (
        step_q + step_y + step_j + step_e + step_t + step_p + step_b
        + zero + first + second + third + fourth + fifth
    ):
        copy.wait_send()


def backward(*operands):
    dma = pltpu.SemaphoreType.DMA

    def low(*shape):
        return pltpu.VMEM(shape, bf16)

    def wide(*shape):
        return pltpu.VMEM(shape, f32)

    return pl.pallas_call(
        kernel,
        out_shape=(
            jax.ShapeDtypeStruct((BLK, 2 * KVW), bf16),
            jax.ShapeDtypeStruct((SPAN, 2 * KVW), f32),
            jax.ShapeDtypeStruct((2, TYPES, NX, SEQ, SPAN, TILE), bf16),
        ),
        in_specs=[smem()] * 2 + [hbm()] * 11 + [vmem()] * 2,
        out_specs=(vmem(),) * 3,
        scratch_shapes=[
            low(NX, BLK, DT), low(NX, BLK, DT), wide(NX, 8, W), low(TREE + 2 * BLK, PAIR),
            low(BLK, 4 * DT), low(BLK, 4 * DT), low(DEPTH, D), low(SPAN, D), low(HEAD, D),
            low(GRP, BLK, PAIR), low(HEAD, 2 * KVW), wide(KV, 8, W),
            low(DEPTH, 2 * KVW), low(DEPTH, HEAD), low(HEAD, DEPTH), low(DEPTH, HEAD), low(HEAD, DEPTH),
            wide(TREE + 2 * BLK, W), wide(TREE + 2 * BLK, PAIR), low(W, HEAD), low(W, HEAD),
            low(GROUP, W), low(GROUP, W), wide(8, W), wide(8, W), wide(GROUP, BLK),
            low(SEQ, SEQ + 2, SPAN, PAIR), low(SEQ, SEQ + 2, SPAN, PAIR),
            low(SEQ, SPAN, HEAD), low(SEQ, SPAN, HEAD),
            wide(GRP, SPAN, 2 * KVW), wide(GRP + 1, SPAN, 2 * KVW),
            low(SEQ, SPAN, HEAD), low(SEQ, SPAN, HEAD),
            low(2, TYPES, NX, BLK, TILE), low(TYPES, NX, BLK, TILE), low(TYPES, NX, BLK, TILE),
            low(TYPES, NX - 1, BLK, TILE), low(TYPES, SEQ, SPAN, TILE), low(TYPES, SEQ - 1, SPAN, TILE),
            dma((12,)),
            dma((2, NX)), dma((2, NX)), dma((NX, NX)), dma((NX, NX)), dma((3, NX)), dma((3, NX)),
            dma((5, SEQ)), dma((5, SEQ)), dma((SEQ,)), dma((SEQ,)), dma((SEQ,)), dma((SEQ,)),
            dma((GRP,)), dma((GRP,)),
            dma((TYPES,)), dma((TYPES,)), dma((TYPES, NX)), dma((TYPES, NX)),
            dma((TYPES, SEQ)), dma((TYPES, SEQ)), dma((TYPES, SEQ)), dma((TYPES, SEQ)),
            dma((TYPES, NX)), dma((TYPES, NX)), dma((TYPES,)), dma((TYPES,)),
        ],
        compiler_params=pltpu.CompilerParams(
            collective_id=0, has_side_effects=True, vmem_limit_bytes=56 * 2**20
        ),
        name="backward",
    )(*operands)


def spread_kernel(summed, down, rise):
    factor = 2.0 / (GRP * SEQ)
    step = pl.program_id(0)

    @pl.when(step < 5)
    def _():
        for a in range(NX):
            part = summed[0, a].reshape(BLK, TILE).astype(f32)
            down[:, a * TILE : (a + 1) * TILE] = part * factor

    @pl.when(step == 5)
    def _():
        for a in range(NX):
            part = summed[0, a].reshape(BLK, TILE).astype(f32)
            side = a // 2
            rise[side, :, (a % 2) * TILE : (a % 2 + 1) * TILE] = part[side * 64 : side * 64 + 64] * factor


def spread(summed):
    return pl.pallas_call(
        spread_kernel,
        grid=(2 * TYPES,),
        out_shape=(
            jax.ShapeDtypeStruct((BLK, D), f32),
            jax.ShapeDtypeStruct((2, 64, KVW), f32),
        ),
        in_specs=[pl.BlockSpec((1, NX, SEQ, SPAN, TILE), lambda b: (b, 0, 0, 0, 0))],
        out_specs=(
            pl.BlockSpec((BLK, NX * TILE), lambda b: (0, jnp.minimum(b, 4))),
            pl.BlockSpec((2, 64, KVW), lambda b: (0, 0, 0)),
        ),
        name="spread",
    )(summed.reshape(2 * TYPES, NX, SEQ, SPAN, TILE))


def on_device(
    queries, out_grad, saved_output, key_rows, value_rows, hidden_rows, prefix_keys, prefix_values,
    prefix_hidden, block_mask, prefix_list, key_down, value_down, key_up, value_up,
):
    pair, prefix, summed = backward(
        block_mask[0], prefix_list, queries[0, 0], out_grad[0, 0], saved_output[0, 0],
        key_rows[0, 0], value_rows[0, 0], hidden_rows[0, 0], prefix_hidden[0],
        prefix_keys, prefix_values, key_down.T, value_down.T, key_up, value_up,
    )
    down, rise = spread(summed)
    down = jnp.swapaxes(down.reshape(2, BLK // 2, D), 1, 2)
    return pair[None], prefix[None], down, rise


def solution(mesh):
    row = P("grp", "seq", None, None)
    in_specs = (
        row, row, row, row, row, row, P(), P(),
        P("grp", "seq", None), P("grp", None, None), P("grp", None), P(), P(), P(), P(),
    )
    out_specs = (P("grp", "seq", None), P("grp", "seq", None), P(), P())
    return jax.shard_map(
        on_device, mesh=mesh, in_specs=in_specs, out_specs=out_specs, check_vma=False
    )
```

```python
import jax
import jax.numpy as jnp
from jax import lax
from jax.experimental import pallas as pl
from jax.experimental.pallas import tpu as pltpu
from jax.sharding import PartitionSpec as P

HEAD = 128
BLK = 128
NX = 4
SEQ = 16
GRP = 8
REP = 5
KV = 4
SPAN = 8
D = 5120
KVW = 512
DT = 640
TILE = 256
DEPTH = 144
TYPES = 3
W = REP * BLK
TREE = SEQ * BLK
GROUP = 4 * BLK
PAIR = 2 * HEAD
CHUNKS = ((0, 256), (256, 512), (512, 640))
MESH = pl.DeviceIdType.MESH
SCALE = HEAD ** (-0.5)
LOG2E = 1.4426950408889634
MASKED = -1e30
NT = (((1,), (1,)), ((), ()))
TN = (((0,), (0,)), ((), ()))
f32 = jnp.float32
bf16 = jnp.bfloat16


def vmem():
    return pl.BlockSpec(memory_space=pltpu.VMEM)


def hbm():
    return pl.BlockSpec(memory_space=pl.ANY)


def smem():
    return pl.BlockSpec(memory_space=pltpu.SMEM)


def remote(src, dst, send, recv, device):
    copy = pltpu.make_async_remote_copy(
        src_ref=src, dst_ref=dst, send_sem=send, recv_sem=recv, device_id=device, device_id_type=MESH
    )
    copy.start()
    return copy


def greet(devices):
    barrier = pltpu.get_barrier_semaphore()
    for device in devices:
        pl.semaphore_signal(barrier, inc=1, device_id=device, device_id_type=MESH)


def greeted(devices):
    pl.semaphore_wait(pltpu.get_barrier_semaphore(), len(devices))


def cols(i, width):
    return pl.ds(pl.multiple_of(i * width, 128), width)


def rows(i, count):
    return pl.ds(pl.multiple_of(i * count, count), count)


def kernel(
    mask, listed, q, g, saved, k, v, hidden, hidden_p, pool_k, pool_v, down_k, down_v, up_k, up_v,
    pair, prefix, out,
    q_in, g_in, delta_in, kv, own_g, own_s, own_h, own_p, down, pool, up, delta_out, all_g, back_all, back_t, proj_all, proj_t,
    s_ref, acc, qs, gs, pb, dsb, stat, diag,
    tsend, rt, proj_s, proj_r, pt, rp, back_s, back_r,
    s0, r0, s1, r1, s2, r2, full, own_x,
    sem_in, kvx_s, kvx_r, kvy_s, kvy_r, q_s, q_r, t_s, t_r, j_s, j_r, b_s, b_r, p_s, p_r,
    s0_s, s0_r, s1_s, s1_r, s2_s, s2_r, a2_s, a2_r, a1_s, a1_r, a0_s, a0_r,
):
    me, grp = lax.axis_index("seq"), lax.axis_index("grp")
    x, y = me // NX, lax.rem(me, NX)
    z, c = grp // 2, lax.rem(grp, 2)
    peers = [lax.rem(me + o, SEQ) for o in range(1, SEQ)]

    def at(xx, yy, zz):
        return {"seq": xx * NX + yy, "grp": zz * 2 + c}

    def line(t, i):
        n = [lax.rem(place + i, NX) for place in (z, x, y)]
        return (at(x, y, n[0]), at(n[1], y, z), at(x, n[2], z))[t]

    def plane(t, e):
        u, w = e // NX, lax.rem(e, NX)
        return (at(u, w, z), at(x, u, w), at(u, y, w))[t]

    on_line = (z, x, y)
    on_plane = (me, y * NX + z, x * NX + z)
    met = [{"grp": lax.rem(grp + i, GRP)} for i in range(1, GRP)]
    met += [{"seq": d} for d in peers]
    for i in range(1, NX):
        for j in range(1, NX):
            met.append(at(x, lax.rem(y + i, NX), lax.rem(z + j, NX)))
            met.append(at(lax.rem(x + i, NX), y, lax.rem(z + j, NX)))
    greet(met)

    def local(src, dst, i):
        copy = pltpu.make_async_copy(src, dst, sem_in.at[i])
        copy.start()
        return copy

    mine = rows(me, BLK)
    keep = [
        local(k.at[:, cols(x, HEAD)], kv.at[mine, 0:HEAD], 0),
        local(v.at[:, cols(x, HEAD)], kv.at[mine, HEAD:PAIR], 1),
        local(q.at[:, cols(x, DT)], q_in.at[x], 2),
        local(g.at[:, cols(x, DT)], g_in.at[x], 3),
        local(g, own_g, 4),
        local(saved, own_s, 5),
        local(hidden, own_h.at[0:BLK], 6),
        local(down_k, down.at[0:64], 7),
        local(down_v, down.at[64:128], 8),
        local(hidden_p, own_p, 9),
        local(pool_k.at[:, :, cols(x, HEAD)], pool.at[:, :, 0:HEAD], 10),
        local(pool_v.at[:, :, cols(x, HEAD)], pool.at[:, :, HEAD:PAIR], 11),
    ]
    keep[4].wait()
    keep[5].wait()
    ones = jnp.ones((8, HEAD), f32)
    for h in range(KV):
        for t in range(REP):
            cut = slice((h * REP + t) * HEAD, (h * REP + t + 1) * HEAD)
            prod = own_g[:, cut].astype(f32) * own_s[:, cut].astype(f32)
            delta_out[h, :, t * BLK : (t + 1) * BLK] = lax.dot_general(
                ones, prod, NT, preferred_element_type=f32, precision=lax.Precision.HIGHEST
            )
    delta_in[x] = delta_out[x]
    greeted(met)

    step_x, step_y, step_q, step_g = ([], []), ([], []), [], []

    def send_x(n, source, lanes):
        for i in range(1, NX):
            tx = lax.rem(x + i, NX)
            step_x[n].append(
                remote(
                    source.at[:, cols(tx, HEAD)], kv.at[mine, lanes], kvx_s.at[n, i], kvx_r.at[n, i],
                    {"seq": tx * NX + y},
                )
            )

    def send_y(n, k, lanes):
        block = rows(lax.rem(x + NX - k, NX) * NX + y, BLK)
        for i in range(1, NX):
            device = {"seq": x * NX + lax.rem(y + i, NX)}
            piece = kv.at[block, lanes]
            step_y[n].append(remote(piece, piece, kvy_s.at[n, k, i], kvy_r.at[n, k, i], device))

    def send_rows(n, source, target, steps):
        for i in range(1, NX):
            tx = lax.rem(x + i, NX)
            steps.append(
                remote(
                    source.at[:, cols(tx, DT)], target.at[x], q_s.at[n, i], q_r.at[n, i],
                    {"seq": tx * NX + y},
                )
            )

    key_lanes, value_lanes = slice(0, HEAD), slice(HEAD, PAIR)
    send_x(0, k, key_lanes)
    keep[0].wait()
    send_y(0, 0, key_lanes)
    send_rows(0, q, q_in, step_q)
    for n in (1, 3, 2):
        step_x[0][n - 1].wait_recv()
        send_y(0, n, key_lanes)
    send_x(1, v, value_lanes)
    keep[1].wait()
    send_y(1, 0, value_lanes)
    for i in range(1, NX):
        tx = lax.rem(x + i, NX)
        device = {"seq": tx * NX + y}
        step_g.append(remote(delta_out.at[tx], delta_in.at[x], q_s.at[2, i], q_r.at[2, i], device))
    send_rows(1, g, g_in, step_g)
    for n in (1, 3, 2):
        step_x[1][n - 1].wait_recv()
        send_y(1, n, value_lanes)

    for i in range(6, 10):
        keep[i].wait()
    own_h[BLK : BLK + SPAN, :] = own_p[...]
    own_h[BLK + SPAN : DEPTH, :] = jnp.zeros((SPAN, D), bf16)
    proj = lax.dot_general(own_h[...], down[...], NT, preferred_element_type=f32)
    proj_s[...] = proj[0:BLK].reshape(SEQ, SPAN, HEAD).astype(bf16)
    proj_all[BLK:DEPTH, :] = proj[BLK:DEPTH].astype(bf16)
    step_j = []
    for o, d in enumerate(peers):
        step_j.append(remote(proj_s.at[d], proj_r.at[me], j_s.at[o], j_r.at[o], {"seq": d}))
    proj_r[me] = proj_s[me]
    up[...] = jnp.zeros_like(up)
    up[0:64, 0:KVW] = up_k[...]
    up[64:128, KVW : 2 * KVW] = up_v[...]

    keep[10].wait()
    keep[11].wait()
    for i in range(2):
        kv[TREE + i * BLK : TREE + (i + 1) * BLK, :] = pool[listed[0, i]]
    acc[...] = jnp.zeros_like(acc)
    key_at = lax.broadcasted_iota(jnp.int32, (GROUP, BLK), 0)
    query_at = lax.broadcasted_iota(jnp.int32, (GROUP, BLK), 1)
    diag[...] = jnp.where(key_at <= y * BLK + query_at, 0.0, MASKED).astype(f32)
    keep[2].wait()
    for copy in step_q + step_y[0]:
        copy.wait_recv()

    def score_rows(kk):
        return 2 * BLK * kk * (kk + 2)

    def score_place(start, m):
        return pl.ds(pl.multiple_of(start + 2 * BLK + m * GROUP, 2 * BLK), GROUP)

    def ends_place(start):
        return pl.ds(pl.multiple_of(start, 2 * BLK), 2 * BLK)

    ends = slice(TREE, TREE + 2 * BLK)

    def scores(step, carry):
        kk = NX - 1 - step
        r = y + NX * kk
        start = score_rows(kk)
        for t in range(REP):
            span = slice(t * BLK, (t + 1) * BLK)
            qs[kk, span, :] = q_in[kk, :, span]
        top = stat.at[0, kk]
        low = stat.at[1, kk]
        top[...] = jnp.full_like(top, MASKED)
        low[...] = jnp.zeros_like(low)

        def hides(m):
            return [(mask[r, m * 4 + b].astype(f32) - 1.0) * 1e30 for b in range(4)]

        def score(place, into, hidden_by, diagonal, n):
            for lo, hi in CHUNKS:
                w = hi - lo
                s = lax.dot_general(kv[place, 0:HEAD], qs[kk, lo:hi, :], NT, preferred_element_type=f32)
                s = s * (SCALE * LOG2E)
                if diagonal:
                    s = s + jnp.concatenate([diag[...]] * (w // BLK), axis=1)
                s_ref[into, lo:hi] = s
                cut = s.reshape(n, BLK // 8, 8, w)
                before = top[:, lo:hi]
                now = before
                for b in range(n):
                    now = jnp.maximum(now, jnp.max(cut[b], axis=0) + hidden_by[b])
                part = low[:, lo:hi] * jnp.exp2(before - now)
                for b in range(n):
                    part += jnp.sum(jnp.exp2(cut[b] - (now - hidden_by[b])[None]), axis=0)
                low[:, lo:hi] = part
                top[:, lo:hi] = now

        def score_group(m, cc):
            score(rows(m, GROUP), score_place(start, m), hides(m), False, 4)
            return cc

        score(ends, ends_place(start), [0.0, 0.0], False, 2)
        lax.fori_loop(0, kk, score_group, 0)
        score(rows(kk, GROUP), score_place(start, kk), hides(kk), True, 4)
        best = jnp.max(top[...], axis=0, keepdims=True)
        total = jnp.sum(low[...] * jnp.exp2(top[...] - best), axis=0, keepdims=True)
        top[...] = jnp.broadcast_to(best + jnp.log2(total), (8, W))
        return carry

    lax.fori_loop(0, NX, scores, 0)
    keep[3].wait()
    for copy in step_g + step_y[1]:
        copy.wait_recv()

    def rollout(step, carry):
        kk = NX - 1 - step
        r = y + NX * kk
        start = score_rows(kk)
        for t in range(REP):
            span = slice(t * BLK, (t + 1) * BLK)
            gs[span, :] = g_in[kk, :, span]
        top = stat.at[0, kk]
        low = delta_in.at[kk]

        def hides(m):
            return [(mask[r, m * 4 + b].astype(f32) - 1.0) * 1e30 for b in range(4)]

        def grads(place, into, hidden_by, n):
            for lo, hi in CHUNKS:
                w = hi - lo
                dp = lax.dot_general(kv[place, HEAD:PAIR], gs[lo:hi, :], NT, preferred_element_type=f32)
                dp = dp.reshape(n, BLK // 8, 8, w)
                cut = s_ref[into, lo:hi].reshape(n, BLK // 8, 8, w)
                for b in range(n):
                    span = slice(b * BLK, (b + 1) * BLK)
                    p = jnp.exp2(cut[b] - (top[:, lo:hi] - hidden_by[b])[None])
                    ds = p * (dp[b] - low[:, lo:hi][None])
                    pb[span, lo:hi] = p.reshape(BLK, w).astype(bf16)
                    dsb[span, lo:hi] = ds.reshape(BLK, w).astype(bf16)
            acc[place, 0:HEAD] += jnp.dot(dsb[0 : n * BLK, :], qs[kk], preferred_element_type=f32)
            acc[place, HEAD:PAIR] += jnp.dot(pb[0 : n * BLK, :], gs[...], preferred_element_type=f32)

        def grads_group(m, cc):
            grads(rows(m, GROUP), score_place(start, m), hides(m), 4)
            return cc

        grads(ends, ends_place(start), [0.0, 0.0], 2)
        lax.fori_loop(0, kk + 1, grads_group, 0)

        for b in range(4):
            j = kk * 4 + b
            part = acc[rows(j, BLK), :].reshape(SEQ, SPAN, PAIR)
            tsend[:, j, :, 0:HEAD] = (part[:, :, 0:HEAD] * SCALE).astype(bf16)
            tsend[:, j, :, HEAD:PAIR] = part[:, :, HEAD:PAIR].astype(bf16)

        @pl.when(step < NX - 1)
        def _():
            for o, d in enumerate(peers):
                four = pl.ds(kk * 4, 4)
                remote(tsend.at[d, four], rt.at[me, four], t_s.at[kk, o], t_r.at[kk, o], {"seq": d})

        return carry

    lax.fori_loop(0, NX, rollout, 0)
    for i in range(2):
        part = acc[TREE + i * BLK : TREE + (i + 1) * BLK, :].reshape(SEQ, SPAN, PAIR)
        tsend[:, SEQ + i, :, 0:HEAD] = (part[:, :, 0:HEAD] * SCALE).astype(bf16)
        tsend[:, SEQ + i, :, HEAD:PAIR] = part[:, :, HEAD:PAIR].astype(bf16)
    step_e = []
    two = pl.ds(SEQ, 2)
    for o, d in enumerate(peers):
        step_e.append(remote(tsend.at[d, two], rt.at[me, two], t_s.at[4, o], t_r.at[4, o], {"seq": d}))
    step_t = []
    for kk in range(NX):
        four = pl.ds(kk * 4, 4)
        for o, d in enumerate(peers):
            copy = pltpu.make_async_remote_copy(
                src_ref=tsend.at[d, four], dst_ref=rt.at[me, four], send_sem=t_s.at[kk, o],
                recv_sem=t_r.at[kk, o], device_id={"seq": d}, device_id_type=MESH,
            )
            if kk == 0:
                copy.start()
            step_t.append(copy)
    rt[me] = tsend[me]
    for copy in step_e:
        copy.wait_recv()
    for h in range(KV):
        for side in range(2):
            lanes = slice(side * HEAD, (side + 1) * HEAD)
            place = slice(side * KVW + h * HEAD, side * KVW + (h + 1) * HEAD)
            for i in range(2):
                part = rt[NX * h, SEQ + i, :, lanes].astype(f32)
                for a in range(1, NX):
                    part += rt[NX * h + a, SEQ + i, :, lanes].astype(f32)
                rp[i, :, place] = part
    for b in range(GRP):
        pt[b] = rp[0] * (listed[0, 0] == b).astype(f32) + rp[1] * (listed[0, 1] == b).astype(f32)
    step_p = []
    for i in range(1, GRP):
        b = lax.rem(grp + i, GRP)
        step_p.append(remote(pt.at[b], rp.at[1 + i], p_s.at[i], p_r.at[i], {"grp": b}))
    for copy in step_t:
        copy.wait_recv()
    for h in range(KV):
        for side in range(2):
            lanes = slice(side * HEAD, (side + 1) * HEAD)
            place = slice(side * KVW + h * HEAD, side * KVW + (h + 1) * HEAD)
            total = rt[NX * h, 0:SEQ, :, lanes].astype(f32)
            for a in range(1, NX):
                total += rt[NX * h + a, 0:SEQ, :, lanes].astype(f32)
            all_g[0:BLK, place] = total.reshape(BLK, HEAD).astype(bf16)
    back = lax.dot_general(all_g[0:BLK, :], up[...], NT, preferred_element_type=f32)
    back_s[...] = back.reshape(SEQ, SPAN, HEAD).astype(bf16)
    step_b = []
    for o, d in enumerate(peers):
        step_b.append(remote(back_s.at[d], back_r.at[me], b_s.at[o], b_r.at[o], {"seq": d}))
    back_r[me] = back_s[me]
    for copy in step_p:
        copy.wait_recv()
    total = pt[grp]
    for i in range(1, GRP):
        total += rp[1 + i]
    own_x[...] = total
    keep.append(local(own_x, prefix, 12))
    tail = jnp.concatenate([total, jnp.zeros_like(total)], axis=0).astype(bf16)
    all_g[BLK:DEPTH, :] = tail
    back_all[BLK:DEPTH, :] = lax.dot_general(tail, up[...], NT, preferred_element_type=f32).astype(bf16)
    keep.append(local(all_g.at[0:BLK], pair, 13))
    for copy in step_j:
        copy.wait_recv()
    proj_all[0:BLK, :] = proj_r[...].reshape(BLK, HEAD)
    same = lax.broadcasted_iota(jnp.int32, (HEAD, HEAD), 0) == lax.broadcasted_iota(jnp.int32, (HEAD, HEAD), 1)
    eye = same.astype(f32).astype(bf16)
    proj_t[...] = lax.dot_general(eye, proj_all[...], NT, preferred_element_type=f32).astype(bf16)
    for a in range(NX):
        cut = slice(a * TILE, (a + 1) * TILE)
        s0[1, 2, a] = jnp.dot(proj_t[...], all_g[:, cut], preferred_element_type=f32).astype(bf16)
    for copy in step_b:
        copy.wait_recv()

    back_all[0:BLK, :] = back_r[...].reshape(BLK, HEAD)
    back_t[...] = lax.dot_general(eye, back_all[...], NT, preferred_element_type=f32).astype(bf16)
    sibling = {"grp": grp + 1 - 2 * c}
    zero, first, second, third, fourth, fifth = [], [], [], [], [], []
    for t in range(TYPES):
        for half in range(2):
            for a in range(NX):
                n = (half * TYPES + t) * NX + a
                if n < D // TILE:
                    cut = slice(n * TILE, (n + 1) * TILE)
                    part = jnp.dot(back_t[...], own_h[:, cut], preferred_element_type=f32)
                    s0[half, t, a] = part.astype(bf16)
        zero.append(remote(s0.at[1 - c, t], r0.at[t], s0_s.at[t], s0_r.at[t], sibling))
    for t in range(TYPES):
        zero[t].wait_recv()
        for a in range(NX):
            s1[t, a] = (s0[c, t, a].astype(f32) + r0[t, a].astype(f32)).astype(bf16)
        for i in range(1, NX):
            there = lax.rem(on_line[t] + i, NX)
            first.append(remote(s1.at[t, there], r1.at[t, i - 1], s1_s.at[t, i], s1_r.at[t, i], line(t, i)))
    for t in range(TYPES):
        for copy in first[t * 3 : t * 3 + 3]:
            copy.wait_recv()
        total = s1[t, on_line[t]].astype(f32)
        for i in range(NX - 1):
            total += r1[t, i].astype(f32)
        s2[t] = total.reshape(SEQ, SPAN, TILE).astype(bf16)
        for o in range(SEQ - 1):
            e = lax.rem(on_plane[t] + o + 1, SEQ)
            second.append(remote(s2.at[t, e], r2.at[t, o], s2_s.at[t, o], s2_r.at[t, o], plane(t, e)))
    for t in range(TYPES):
        for copy in second[t * 15 : t * 15 + 15]:
            copy.wait_recv()
        total = s2[t, on_plane[t]].astype(f32)
        for o in range(SEQ - 1):
            total += r2[t, o].astype(f32)
        full[t, on_line[t], on_plane[t]] = total.astype(bf16)
        piece = full.at[t, on_line[t], on_plane[t]]
        for o in range(SEQ - 1):
            e = lax.rem(on_plane[t] + o + 1, SEQ)
            third.append(remote(piece, piece, a2_s.at[t, o], a2_r.at[t, o], plane(t, e)))
    for t in range(TYPES):
        for copy in third[t * 15 : t * 15 + 15]:
            copy.wait_recv()
        piece = full.at[t, on_line[t]]
        for i in range(1, NX):
            fourth.append(remote(piece, piece, a1_s.at[t, i], a1_r.at[t, i], line(t, i)))
    for t in range(TYPES):
        for copy in fourth[t * 3 : t * 3 + 3]:
            copy.wait_recv()
        fifth.append(remote(full.at[t], out.at[c, t], a0_s.at[t], a0_r.at[t], sibling))
        keep.append(local(full.at[t], out.at[c, t], 14 + t))
    for copy in fifth:
        copy.wait_recv()
    for copy in keep[12:]:
        copy.wait()

    for copy in (
        step_x[0] + step_x[1] + step_y[0] + step_y[1] + step_q + step_g + step_j + step_e + step_t + step_p + step_b
        + zero + first + second + third + fourth + fifth
    ):
        copy.wait_send()


def backward(*operands):
    dma = pltpu.SemaphoreType.DMA

    def low(*shape):
        return pltpu.VMEM(shape, bf16)

    def wide(*shape):
        return pltpu.VMEM(shape, f32)

    return pl.pallas_call(
        kernel,
        out_shape=(
            jax.ShapeDtypeStruct((BLK, 2 * KVW), bf16),
            jax.ShapeDtypeStruct((SPAN, 2 * KVW), f32),
            jax.ShapeDtypeStruct((2, TYPES, NX, SEQ, SPAN, TILE), bf16),
        ),
        in_specs=[smem()] * 2 + [hbm()] * 11 + [vmem()] * 2,
        out_specs=(hbm(),) * 3,
        scratch_shapes=[
            low(NX, BLK, DT), low(NX, BLK, DT), wide(NX, 8, W), low(TREE + 2 * BLK, PAIR),
            low(BLK, 4 * DT), low(BLK, 4 * DT), low(DEPTH, D), low(SPAN, D), low(HEAD, D),
            low(GRP, BLK, PAIR), low(HEAD, 2 * KVW), wide(KV, 8, W),
            low(DEPTH, 2 * KVW), low(DEPTH, HEAD), low(HEAD, DEPTH), low(DEPTH, HEAD), low(HEAD, DEPTH),
            wide(2 * BLK * NX * (NX + 2), W), wide(TREE + 2 * BLK, PAIR), low(NX, W, HEAD), low(W, HEAD),
            low(GROUP, W), low(GROUP, W), wide(2, NX, 8, W), wide(GROUP, BLK),
            low(SEQ, SEQ + 2, SPAN, PAIR), low(SEQ, SEQ + 2, SPAN, PAIR),
            low(SEQ, SPAN, HEAD), low(SEQ, SPAN, HEAD),
            wide(GRP, SPAN, 2 * KVW), wide(GRP + 1, SPAN, 2 * KVW),
            low(SEQ, SPAN, HEAD), low(SEQ, SPAN, HEAD),
            low(2, TYPES, NX, BLK, TILE), low(TYPES, NX, BLK, TILE), low(TYPES, NX, BLK, TILE),
            low(TYPES, NX - 1, BLK, TILE), low(TYPES, SEQ, SPAN, TILE), low(TYPES, SEQ - 1, SPAN, TILE),
            low(TYPES, NX, SEQ, SPAN, TILE), wide(SPAN, 2 * KVW),
            dma((17,)),
            dma((2, NX)), dma((2, NX)), dma((2, NX, NX)), dma((2, NX, NX)), dma((3, NX)), dma((3, NX)),
            dma((5, SEQ)), dma((5, SEQ)), dma((SEQ,)), dma((SEQ,)), dma((SEQ,)), dma((SEQ,)),
            dma((GRP,)), dma((GRP,)),
            dma((TYPES,)), dma((TYPES,)), dma((TYPES, NX)), dma((TYPES, NX)),
            dma((TYPES, SEQ)), dma((TYPES, SEQ)), dma((TYPES, SEQ)), dma((TYPES, SEQ)),
            dma((TYPES, NX)), dma((TYPES, NX)), dma((TYPES,)), dma((TYPES,)),
        ],
        compiler_params=pltpu.CompilerParams(
            collective_id=0, has_side_effects=True, vmem_limit_bytes=56 * 2**20
        ),
        name="backward",
    )(*operands)


def spread_kernel(summed, pair, prefix, down, rise, pair_out, prefix_out):
    factor = 2.0 / (GRP * SEQ)
    step = pl.program_id(0)

    @pl.when(step < 5)
    def _():
        for a in range(NX):
            part = summed[0, a].reshape(BLK, TILE).astype(f32)
            down[:, a * TILE : (a + 1) * TILE] = part * factor

    @pl.when(step == 0)
    def _():
        pair_out[...] = pair[...]
        prefix_out[...] = prefix[...]

    @pl.when(step == 5)
    def _():
        for a in range(NX):
            part = summed[0, a].reshape(BLK, TILE).astype(f32)
            side = a // 2
            rise[side, :, (a % 2) * TILE : (a % 2 + 1) * TILE] = part[side * 64 : side * 64 + 64] * factor


def spread(summed, pair, prefix):
    return pl.pallas_call(
        spread_kernel,
        grid=(2 * TYPES,),
        out_shape=(
            jax.ShapeDtypeStruct((BLK, D), f32),
            jax.ShapeDtypeStruct((2, 64, KVW), f32),
            jax.ShapeDtypeStruct((BLK, 2 * KVW), bf16),
            jax.ShapeDtypeStruct((SPAN, 2 * KVW), f32),
        ),
        in_specs=[
            pl.BlockSpec((1, NX, SEQ, SPAN, TILE), lambda b: (b, 0, 0, 0, 0)),
            pl.BlockSpec((BLK, 2 * KVW), lambda b: (0, 0)),
            pl.BlockSpec((SPAN, 2 * KVW), lambda b: (0, 0)),
        ],
        out_specs=(
            pl.BlockSpec((BLK, NX * TILE), lambda b: (0, jnp.minimum(b, 4))),
            pl.BlockSpec((2, 64, KVW), lambda b: (0, 0, 0)),
            pl.BlockSpec((BLK, 2 * KVW), lambda b: (0, 0)),
            pl.BlockSpec((SPAN, 2 * KVW), lambda b: (0, 0)),
        ),
        name="spread",
    )(summed.reshape(2 * TYPES, NX, SEQ, SPAN, TILE), pair, prefix)


def on_device(
    queries, out_grad, saved_output, key_rows, value_rows, hidden_rows, prefix_keys, prefix_values,
    prefix_hidden, block_mask, prefix_list, key_down, value_down, key_up, value_up,
):
    pair, prefix, summed = backward(
        block_mask[0], prefix_list, queries[0, 0], out_grad[0, 0], saved_output[0, 0],
        key_rows[0, 0], value_rows[0, 0], hidden_rows[0, 0], prefix_hidden[0],
        prefix_keys, prefix_values, key_down.T, value_down.T, key_up, value_up,
    )
    down, rise, pair, prefix = spread(summed, pair, prefix)
    down = jnp.swapaxes(down.reshape(2, BLK // 2, D), 1, 2)
    return pair[None], prefix[None], down, rise


def solution(mesh):
    row = P("grp", "seq", None, None)
    in_specs = (
        row, row, row, row, row, row, P(), P(),
        P("grp", "seq", None), P("grp", None, None), P("grp", None), P(), P(), P(), P(),
    )
    out_specs = (P("grp", "seq", None), P("grp", "seq", None), P(), P())
    return jax.shard_map(
        on_device, mesh=mesh, in_specs=in_specs, out_specs=out_specs, check_vma=False
    )
```

```python
import jax
import jax.numpy as jnp
from jax import lax
from jax.experimental import pallas as pl
from jax.experimental.pallas import tpu as pltpu
from jax.sharding import PartitionSpec as P

HEAD = 128
BLK = 128
NX = 4
SEQ = 16
GRP = 8
REP = 5
KV = 4
SPAN = 8
D = 5120
KVW = 512
DT = 640
TILE = 256
DEPTH = 144
TYPES = 3
W = REP * BLK
TREE = SEQ * BLK
GROUP = 4 * BLK
PAIR = 2 * HEAD
CHUNKS = ((0, 256), (256, 512), (512, 640))
MESH = pl.DeviceIdType.MESH
SCALE = HEAD ** (-0.5)
LOG2E = 1.4426950408889634
MASKED = -1e30
NT = (((1,), (1,)), ((), ()))
TN = (((0,), (0,)), ((), ()))
f32 = jnp.float32
bf16 = jnp.bfloat16


def vmem():
    return pl.BlockSpec(memory_space=pltpu.VMEM)


def hbm():
    return pl.BlockSpec(memory_space=pl.ANY)


def smem():
    return pl.BlockSpec(memory_space=pltpu.SMEM)


def remote(src, dst, send, recv, device):
    copy = pltpu.make_async_remote_copy(
        src_ref=src, dst_ref=dst, send_sem=send, recv_sem=recv, device_id=device, device_id_type=MESH
    )
    copy.start()
    return copy


def greet(devices):
    barrier = pltpu.get_barrier_semaphore()
    for device in devices:
        pl.semaphore_signal(barrier, inc=1, device_id=device, device_id_type=MESH)


def greeted(devices):
    pl.semaphore_wait(pltpu.get_barrier_semaphore(), len(devices))


def cols(i, width):
    return pl.ds(pl.multiple_of(i * width, 128), width)


def rows(i, count):
    return pl.ds(pl.multiple_of(i * count, count), count)


def kernel(
    mask, listed, q, g, saved, k, v, hidden, hidden_p, pool_k, pool_v, down_k, down_v, up_k, up_v,
    pair, prefix, out,
    q_in, g_in, delta_in, kv, own_g, own_s, own_h, own_p, down, pool, up, delta_out, all_g, back_all, back_t, proj_all, proj_t,
    s_ref, acc, qs, gs, pb, dsb, stat, diag,
    tsend, rt, proj_s, proj_r, pt, rp, back_s, back_r,
    s0, r0, s1, r1, s2, r2, full, own_x,
    sem_in, kvx_s, kvx_r, kvy_s, kvy_r, q_s, q_r, t_s, t_r, j_s, j_r, b_s, b_r, p_s, p_r,
    s0_s, s0_r, s1_s, s1_r, s2_s, s2_r, a2_s, a2_r, a1_s, a1_r, a0_s, a0_r,
):
    me, grp = lax.axis_index("seq"), lax.axis_index("grp")
    x, y = me // NX, lax.rem(me, NX)
    z, c = grp // 2, lax.rem(grp, 2)
    peers = [lax.rem(me + o, SEQ) for o in range(1, SEQ)]

    def at(xx, yy, zz):
        return {"seq": xx * NX + yy, "grp": zz * 2 + c}

    def line(t, i):
        n = [lax.rem(place + i, NX) for place in (z, x, y)]
        return (at(x, y, n[0]), at(n[1], y, z), at(x, n[2], z))[t]

    def plane(t, e):
        u, w = e // NX, lax.rem(e, NX)
        return (at(u, w, z), at(x, u, w), at(u, y, w))[t]

    on_line = (z, x, y)
    on_plane = (me, y * NX + z, x * NX + z)
    met = [{"grp": lax.rem(grp + i, GRP)} for i in range(1, GRP)]
    met += [{"seq": d} for d in peers]
    for i in range(1, NX):
        for j in range(1, NX):
            met.append(at(x, lax.rem(y + i, NX), lax.rem(z + j, NX)))
            met.append(at(lax.rem(x + i, NX), y, lax.rem(z + j, NX)))
    greet(met)

    def local(src, dst, i):
        copy = pltpu.make_async_copy(src, dst, sem_in.at[i])
        copy.start()
        return copy

    mine = rows(me, BLK)
    keep = [
        local(k.at[:, cols(x, HEAD)], kv.at[mine, 0:HEAD], 0),
        local(v.at[:, cols(x, HEAD)], kv.at[mine, HEAD:PAIR], 1),
        local(q.at[:, cols(x, DT)], q_in.at[x], 2),
        local(g.at[:, cols(x, DT)], g_in.at[x], 3),
        local(g, own_g, 4),
        local(saved, own_s, 5),
        local(hidden, own_h.at[0:BLK], 6),
        local(down_k, down.at[0:64], 7),
        local(down_v, down.at[64:128], 8),
        local(hidden_p, own_p, 9),
        local(pool_k.at[:, :, cols(x, HEAD)], pool.at[:, :, 0:HEAD], 10),
        local(pool_v.at[:, :, cols(x, HEAD)], pool.at[:, :, HEAD:PAIR], 11),
    ]
    keep[4].wait()
    keep[5].wait()
    ones = jnp.ones((8, HEAD), f32)
    for h in range(KV):
        for t in range(REP):
            cut = slice((h * REP + t) * HEAD, (h * REP + t + 1) * HEAD)
            prod = own_g[:, cut].astype(f32) * own_s[:, cut].astype(f32)
            delta_out[h, :, t * BLK : (t + 1) * BLK] = lax.dot_general(
                ones, prod, NT, preferred_element_type=f32, precision=lax.Precision.HIGHEST
            )
    delta_in[x] = delta_out[x]
    greeted(met)

    step_x, step_y, step_q, step_g = ([], []), ([], []), [], []

    def send_x(n, source, lanes):
        for i in range(1, NX):
            tx = lax.rem(x + i, NX)
            step_x[n].append(
                remote(
                    source.at[:, cols(tx, HEAD)], kv.at[mine, lanes], kvx_s.at[n, i], kvx_r.at[n, i],
                    {"seq": tx * NX + y},
                )
            )

    def send_y(n, k, lanes):
        block = rows(lax.rem(x + NX - k, NX) * NX + y, BLK)
        for i in range(1, NX):
            device = {"seq": x * NX + lax.rem(y + i, NX)}
            piece = kv.at[block, lanes]
            step_y[n].append(remote(piece, piece, kvy_s.at[n, k, i], kvy_r.at[n, k, i], device))

    def send_rows(n, source, target, steps):
        for i in range(1, NX):
            tx = lax.rem(x + i, NX)
            steps.append(
                remote(
                    source.at[:, cols(tx, DT)], target.at[x], q_s.at[n, i], q_r.at[n, i],
                    {"seq": tx * NX + y},
                )
            )

    key_lanes, value_lanes = slice(0, HEAD), slice(HEAD, PAIR)
    send_x(0, k, key_lanes)
    send_x(1, v, value_lanes)
    keep[0].wait()
    send_y(0, 0, key_lanes)
    keep[1].wait()
    send_y(1, 0, value_lanes)
    send_rows(0, q, q_in, step_q)
    for i in range(1, NX):
        tx = lax.rem(x + i, NX)
        device = {"seq": tx * NX + y}
        step_g.append(remote(delta_out.at[tx], delta_in.at[x], q_s.at[2, i], q_r.at[2, i], device))
    send_rows(1, g, g_in, step_g)
    for side, lanes in ((0, key_lanes), (1, value_lanes)):
        for n in (1, 3, 2):
            step_x[side][n - 1].wait_recv()
            send_y(side, n, lanes)

    for i in range(6, 10):
        keep[i].wait()
    own_h[BLK : BLK + SPAN, :] = own_p[...]
    own_h[BLK + SPAN : DEPTH, :] = jnp.zeros((SPAN, D), bf16)
    proj = lax.dot_general(own_h[...], down[...], NT, preferred_element_type=f32)
    proj_s[...] = proj[0:BLK].reshape(SEQ, SPAN, HEAD).astype(bf16)
    proj_all[BLK:DEPTH, :] = proj[BLK:DEPTH].astype(bf16)
    step_j = []
    for o, d in enumerate(peers):
        step_j.append(remote(proj_s.at[d], proj_r.at[me], j_s.at[o], j_r.at[o], {"seq": d}))
    proj_r[me] = proj_s[me]
    up[...] = jnp.zeros_like(up)
    up[0:64, 0:KVW] = up_k[...]
    up[64:128, KVW : 2 * KVW] = up_v[...]

    keep[10].wait()
    keep[11].wait()
    for i in range(2):
        kv[TREE + i * BLK : TREE + (i + 1) * BLK, :] = pool[listed[0, i]]
    acc[...] = jnp.zeros_like(acc)
    key_at = lax.broadcasted_iota(jnp.int32, (GROUP, BLK), 0)
    query_at = lax.broadcasted_iota(jnp.int32, (GROUP, BLK), 1)
    diag[...] = jnp.where(key_at <= y * BLK + query_at, 0.0, MASKED).astype(f32)
    keep[2].wait()
    for copy in step_q + step_y[0]:
        copy.wait_recv()

    def score_rows(kk):
        return 2 * BLK * kk * (kk + 2)

    def score_place(start, m):
        return pl.ds(pl.multiple_of(start + 2 * BLK + m * GROUP, 2 * BLK), GROUP)

    def ends_place(start):
        return pl.ds(pl.multiple_of(start, 2 * BLK), 2 * BLK)

    ends = slice(TREE, TREE + 2 * BLK)

    def scores(step, carry):
        kk = NX - 1 - step
        r = y + NX * kk
        start = score_rows(kk)
        for t in range(REP):
            span = slice(t * BLK, (t + 1) * BLK)
            qs[kk, span, :] = q_in[kk, :, span]
        top = stat.at[0, kk]
        low = stat.at[1, kk]
        top[...] = jnp.full_like(top, MASKED)
        low[...] = jnp.zeros_like(low)

        def hides(m):
            return [(mask[r, m * 4 + b].astype(f32) - 1.0) * 1e30 for b in range(4)]

        def score(place, into, hidden_by, diagonal, n):
            for lo, hi in CHUNKS:
                w = hi - lo
                s = lax.dot_general(kv[place, 0:HEAD], qs[kk, lo:hi, :], NT, preferred_element_type=f32)
                s = s * (SCALE * LOG2E)
                if diagonal:
                    s = s + jnp.concatenate([diag[...]] * (w // BLK), axis=1)
                s_ref[into, lo:hi] = s
                cut = s.reshape(n, BLK // 8, 8, w)
                before = top[:, lo:hi]
                now = before
                for b in range(n):
                    now = jnp.maximum(now, jnp.max(cut[b], axis=0) + hidden_by[b])
                part = low[:, lo:hi] * jnp.exp2(before - now)
                for b in range(n):
                    part += jnp.sum(jnp.exp2(cut[b] - (now - hidden_by[b])[None]), axis=0)
                low[:, lo:hi] = part
                top[:, lo:hi] = now

        def score_group(m, cc):
            score(rows(m, GROUP), score_place(start, m), hides(m), False, 4)
            return cc

        score(ends, ends_place(start), [0.0, 0.0], False, 2)
        lax.fori_loop(0, kk, score_group, 0)
        score(rows(kk, GROUP), score_place(start, kk), hides(kk), True, 4)
        best = jnp.max(top[...], axis=0, keepdims=True)
        total = jnp.sum(low[...] * jnp.exp2(top[...] - best), axis=0, keepdims=True)
        top[...] = jnp.broadcast_to(best + jnp.log2(total), (8, W))
        return carry

    lax.fori_loop(0, NX, scores, 0)
    keep[3].wait()
    for copy in step_g + step_y[1]:
        copy.wait_recv()

    def term(n, first_block, count, o):
        part = pl.ds(first_block, count)
        return pltpu.make_async_remote_copy(
            src_ref=tsend.at[peers[o], part], dst_ref=rt.at[me, part], send_sem=t_s.at[n, o],
            recv_sem=t_r.at[n, o], device_id={"seq": peers[o]}, device_id_type=MESH,
        )

    def rollout(step, carry):
        kk = NX - 1 - step
        r = y + NX * kk
        start = score_rows(kk)
        for t in range(REP):
            span = slice(t * BLK, (t + 1) * BLK)
            gs[span, :] = g_in[kk, :, span]
        top = stat.at[0, kk]
        low = delta_in.at[kk]

        def hides(m):
            return [(mask[r, m * 4 + b].astype(f32) - 1.0) * 1e30 for b in range(4)]

        def grads(place, into, hidden_by, n):
            for lo, hi in CHUNKS:
                w = hi - lo
                dp = lax.dot_general(kv[place, HEAD:PAIR], gs[lo:hi, :], NT, preferred_element_type=f32)
                dp = dp.reshape(n, BLK // 8, 8, w)
                cut = s_ref[into, lo:hi].reshape(n, BLK // 8, 8, w)
                for b in range(n):
                    span = slice(b * BLK, (b + 1) * BLK)
                    p = jnp.exp2(cut[b] - (top[:, lo:hi] - hidden_by[b])[None])
                    ds = p * (dp[b] - low[:, lo:hi][None])
                    pb[span, lo:hi] = p.reshape(BLK, w).astype(bf16)
                    dsb[span, lo:hi] = ds.reshape(BLK, w).astype(bf16)
            acc[place, 0:HEAD] += jnp.dot(dsb[0 : n * BLK, :], qs[kk], preferred_element_type=f32)
            acc[place, HEAD:PAIR] += jnp.dot(pb[0 : n * BLK, :], gs[...], preferred_element_type=f32)

        def grads_group(m, cc):
            grads(rows(m, GROUP), score_place(start, m), hides(m), 4)
            return cc

        grads(ends, ends_place(start), [0.0, 0.0], 2)

        @pl.when(step == NX - 1)
        def _():
            for i in range(2):
                part = acc[TREE + i * BLK : TREE + (i + 1) * BLK, :].reshape(SEQ, SPAN, PAIR)
                tsend[:, SEQ + i, :, 0:HEAD] = (part[:, :, 0:HEAD] * SCALE).astype(bf16)
                tsend[:, SEQ + i, :, HEAD:PAIR] = part[:, :, HEAD:PAIR].astype(bf16)
            for o in range(SEQ - 1):
                term(4, SEQ, 2, o).start()

        grads_group(kk, 0)
        for b in range(4):
            j = kk * 4 + b
            part = acc[rows(j, BLK), :].reshape(SEQ, SPAN, PAIR)
            tsend[:, j, :, 0:HEAD] = (part[:, :, 0:HEAD] * SCALE).astype(bf16)
            tsend[:, j, :, HEAD:PAIR] = part[:, :, HEAD:PAIR].astype(bf16)
        for o in range(SEQ - 1):
            term(kk, kk * 4, 4, o).start()
        lax.fori_loop(0, kk, grads_group, 0)
        return carry

    lax.fori_loop(0, NX, rollout, 0)
    step_e = [term(4, SEQ, 2, o) for o in range(SEQ - 1)]
    step_t = [term(kk, kk * 4, 4, o) for kk in range(NX) for o in range(SEQ - 1)]
    rt[me] = tsend[me]
    for copy in step_e:
        copy.wait_recv()
    for h in range(KV):
        for side in range(2):
            lanes = slice(side * HEAD, (side + 1) * HEAD)
            place = slice(side * KVW + h * HEAD, side * KVW + (h + 1) * HEAD)
            for i in range(2):
                part = rt[NX * h, SEQ + i, :, lanes].astype(f32)
                for a in range(1, NX):
                    part += rt[NX * h + a, SEQ + i, :, lanes].astype(f32)
                rp[i, :, place] = part
    for b in range(GRP):
        pt[b] = rp[0] * (listed[0, 0] == b).astype(f32) + rp[1] * (listed[0, 1] == b).astype(f32)
    step_p = []
    for i in range(1, GRP):
        b = lax.rem(grp + i, GRP)
        step_p.append(remote(pt.at[b], rp.at[1 + i], p_s.at[i], p_r.at[i], {"grp": b}))
    for copy in step_t:
        copy.wait_recv()
    for h in range(KV):
        for side in range(2):
            lanes = slice(side * HEAD, (side + 1) * HEAD)
            place = slice(side * KVW + h * HEAD, side * KVW + (h + 1) * HEAD)
            total = rt[NX * h, 0:SEQ, :, lanes].astype(f32)
            for a in range(1, NX):
                total += rt[NX * h + a, 0:SEQ, :, lanes].astype(f32)
            all_g[0:BLK, place] = total.reshape(BLK, HEAD).astype(bf16)
    back = lax.dot_general(all_g[0:BLK, :], up[...], NT, preferred_element_type=f32)
    back_s[...] = back.reshape(SEQ, SPAN, HEAD).astype(bf16)
    step_b = []
    for o, d in enumerate(peers):
        step_b.append(remote(back_s.at[d], back_r.at[me], b_s.at[o], b_r.at[o], {"seq": d}))
    back_r[me] = back_s[me]
    for copy in step_p:
        copy.wait_recv()
    total = pt[grp]
    for i in range(1, GRP):
        total += rp[1 + i]
    own_x[...] = total
    keep.append(local(own_x, prefix, 12))
    tail = jnp.concatenate([total, jnp.zeros_like(total)], axis=0).astype(bf16)
    all_g[BLK:DEPTH, :] = tail
    back_all[BLK:DEPTH, :] = lax.dot_general(tail, up[...], NT, preferred_element_type=f32).astype(bf16)
    keep.append(local(all_g.at[0:BLK], pair, 13))
    for copy in step_j:
        copy.wait_recv()
    proj_all[0:BLK, :] = proj_r[...].reshape(BLK, HEAD)
    same = lax.broadcasted_iota(jnp.int32, (HEAD, HEAD), 0) == lax.broadcasted_iota(jnp.int32, (HEAD, HEAD), 1)
    eye = same.astype(f32).astype(bf16)
    proj_t[...] = lax.dot_general(eye, proj_all[...], NT, preferred_element_type=f32).astype(bf16)
    for a in range(NX):
        cut = slice(a * TILE, (a + 1) * TILE)
        s0[1, 2, a] = jnp.dot(proj_t[...], all_g[:, cut], preferred_element_type=f32).astype(bf16)
    for copy in step_b:
        copy.wait_recv()

    back_all[0:BLK, :] = back_r[...].reshape(BLK, HEAD)
    back_t[...] = lax.dot_general(eye, back_all[...], NT, preferred_element_type=f32).astype(bf16)
    sibling = {"grp": grp + 1 - 2 * c}
    zero, first, second, third, fourth, fifth = [], [], [], [], [], []
    for t in range(TYPES):
        for half in range(2):
            for a in range(NX):
                n = (half * TYPES + t) * NX + a
                if n < D // TILE:
                    cut = slice(n * TILE, (n + 1) * TILE)
                    part = jnp.dot(back_t[...], own_h[:, cut], preferred_element_type=f32)
                    s0[half, t, a] = part.astype(bf16)
        zero.append(remote(s0.at[1 - c, t], r0.at[t], s0_s.at[t], s0_r.at[t], sibling))
    for t in range(TYPES):
        zero[t].wait_recv()
        for a in range(NX):
            s1[t, a] = (s0[c, t, a].astype(f32) + r0[t, a].astype(f32)).astype(bf16)
        for i in range(1, NX):
            there = lax.rem(on_line[t] + i, NX)
            first.append(remote(s1.at[t, there], r1.at[t, i - 1], s1_s.at[t, i], s1_r.at[t, i], line(t, i)))
    for t in range(TYPES):
        for copy in first[t * 3 : t * 3 + 3]:
            copy.wait_recv()
        total = s1[t, on_line[t]].astype(f32)
        for i in range(NX - 1):
            total += r1[t, i].astype(f32)
        s2[t] = total.reshape(SEQ, SPAN, TILE).astype(bf16)
        for o in range(SEQ - 1):
            e = lax.rem(on_plane[t] + o + 1, SEQ)
            second.append(remote(s2.at[t, e], r2.at[t, o], s2_s.at[t, o], s2_r.at[t, o], plane(t, e)))
    for t in range(TYPES):
        for copy in second[t * 15 : t * 15 + 15]:
            copy.wait_recv()
        total = s2[t, on_plane[t]].astype(f32)
        for o in range(SEQ - 1):
            total += r2[t, o].astype(f32)
        full[t, on_line[t], on_plane[t]] = total.astype(bf16)
        piece = full.at[t, on_line[t], on_plane[t]]
        for o in range(SEQ - 1):
            e = lax.rem(on_plane[t] + o + 1, SEQ)
            third.append(remote(piece, piece, a2_s.at[t, o], a2_r.at[t, o], plane(t, e)))
    for t in range(TYPES):
        for copy in third[t * 15 : t * 15 + 15]:
            copy.wait_recv()
        piece = full.at[t, on_line[t]]
        for i in range(1, NX):
            fourth.append(remote(piece, piece, a1_s.at[t, i], a1_r.at[t, i], line(t, i)))
    for t in range(TYPES):
        for copy in fourth[t * 3 : t * 3 + 3]:
            copy.wait_recv()
        fifth.append(remote(full.at[t], out.at[c, t], a0_s.at[t], a0_r.at[t], sibling))
        keep.append(local(full.at[t], out.at[c, t], 14 + t))
    for copy in fifth:
        copy.wait_recv()
    for copy in keep[12:]:
        copy.wait()

    for copy in (
        step_x[0] + step_x[1] + step_y[0] + step_y[1] + step_q + step_g + step_j + step_e + step_t + step_p + step_b
        + zero + first + second + third + fourth + fifth
    ):
        copy.wait_send()


def backward(*operands):
    dma = pltpu.SemaphoreType.DMA

    def low(*shape):
        return pltpu.VMEM(shape, bf16)

    def wide(*shape):
        return pltpu.VMEM(shape, f32)

    return pl.pallas_call(
        kernel,
        out_shape=(
            jax.ShapeDtypeStruct((BLK, 2 * KVW), bf16),
            jax.ShapeDtypeStruct((SPAN, 2 * KVW), f32),
            jax.ShapeDtypeStruct((2, TYPES, NX, SEQ, SPAN, TILE), bf16),
        ),
        in_specs=[smem()] * 2 + [hbm()] * 11 + [vmem()] * 2,
        out_specs=(hbm(),) * 3,
        scratch_shapes=[
            low(NX, BLK, DT), low(NX, BLK, DT), wide(NX, 8, W), low(TREE + 2 * BLK, PAIR),
            low(BLK, 4 * DT), low(BLK, 4 * DT), low(DEPTH, D), low(SPAN, D), low(HEAD, D),
            low(GRP, BLK, PAIR), low(HEAD, 2 * KVW), wide(KV, 8, W),
            low(DEPTH, 2 * KVW), low(DEPTH, HEAD), low(HEAD, DEPTH), low(DEPTH, HEAD), low(HEAD, DEPTH),
            wide(2 * BLK * NX * (NX + 2), W), wide(TREE + 2 * BLK, PAIR), low(NX, W, HEAD), low(W, HEAD),
            low(GROUP, W), low(GROUP, W), wide(2, NX, 8, W), wide(GROUP, BLK),
            low(SEQ, SEQ + 2, SPAN, PAIR), low(SEQ, SEQ + 2, SPAN, PAIR),
            low(SEQ, SPAN, HEAD), low(SEQ, SPAN, HEAD),
            wide(GRP, SPAN, 2 * KVW), wide(GRP + 1, SPAN, 2 * KVW),
            low(SEQ, SPAN, HEAD), low(SEQ, SPAN, HEAD),
            low(2, TYPES, NX, BLK, TILE), low(TYPES, NX, BLK, TILE), low(TYPES, NX, BLK, TILE),
            low(TYPES, NX - 1, BLK, TILE), low(TYPES, SEQ, SPAN, TILE), low(TYPES, SEQ - 1, SPAN, TILE),
            low(TYPES, NX, SEQ, SPAN, TILE), wide(SPAN, 2 * KVW),
            dma((17,)),
            dma((2, NX)), dma((2, NX)), dma((2, NX, NX)), dma((2, NX, NX)), dma((3, NX)), dma((3, NX)),
            dma((5, SEQ)), dma((5, SEQ)), dma((SEQ,)), dma((SEQ,)), dma((SEQ,)), dma((SEQ,)),
            dma((GRP,)), dma((GRP,)),
            dma((TYPES,)), dma((TYPES,)), dma((TYPES, NX)), dma((TYPES, NX)),
            dma((TYPES, SEQ)), dma((TYPES, SEQ)), dma((TYPES, SEQ)), dma((TYPES, SEQ)),
            dma((TYPES, NX)), dma((TYPES, NX)), dma((TYPES,)), dma((TYPES,)),
        ],
        compiler_params=pltpu.CompilerParams(
            collective_id=0, has_side_effects=True, vmem_limit_bytes=56 * 2**20
        ),
        name="backward",
    )(*operands)


def spread_kernel(summed, pair, prefix, down, rise, pair_out, prefix_out, got, made, risen, sem_got, sem_made):
    factor = 2.0 / (GRP * SEQ)
    arrive = [pltpu.make_async_copy(summed.at[i], got.at[i], sem_got.at[i]) for i in range(2 * TYPES)]
    leave = [
        pltpu.make_async_copy(pair, pair_out, sem_made.at[0]),
        pltpu.make_async_copy(prefix, prefix_out, sem_made.at[1]),
    ]
    for copy in arrive + leave:
        copy.start()
    for i in range(2 * TYPES):
        arrive[i].wait()
        for a in range(NX):
            part = got[i, a].reshape(BLK, TILE).astype(f32) * factor
            if i < 5:
                made[i, :, a * TILE : (a + 1) * TILE] = part
            else:
                side = a // 2
                risen[side, :, (a % 2) * TILE : (a % 2 + 1) * TILE] = part[side * 64 : side * 64 + 64]
        if i < 5:
            for half in range(2):
                cut = slice(half * 64, half * 64 + 64)
                leave.append(
                    pltpu.make_async_copy(
                        made.at[i, cut], down.at[cut, i * NX * TILE : (i + 1) * NX * TILE],
                        sem_made.at[2 + 2 * i + half],
                    )
                )
                leave[-1].start()
        else:
            leave.append(pltpu.make_async_copy(risen, rise, sem_made.at[12]))
            leave[-1].start()
    for copy in leave:
        copy.wait()


def spread(summed, pair, prefix):
    return pl.pallas_call(
        spread_kernel,
        out_shape=(
            jax.ShapeDtypeStruct((BLK, D), f32),
            jax.ShapeDtypeStruct((2, 64, KVW), f32),
            jax.ShapeDtypeStruct((BLK, 2 * KVW), bf16),
            jax.ShapeDtypeStruct((SPAN, 2 * KVW), f32),
        ),
        in_specs=[hbm()] * 3,
        out_specs=(hbm(),) * 4,
        scratch_shapes=[
            pltpu.VMEM((2 * TYPES, NX, SEQ, SPAN, TILE), bf16),
            pltpu.VMEM((5, BLK, NX * TILE), f32),
            pltpu.VMEM((2, 64, KVW), f32),
            pltpu.SemaphoreType.DMA((2 * TYPES,)),
            pltpu.SemaphoreType.DMA((13,)),
        ],
        compiler_params=pltpu.CompilerParams(vmem_limit_bytes=60 * 2**20),
        name="spread",
    )(summed.reshape(2 * TYPES, NX, SEQ, SPAN, TILE), pair, prefix)


def on_device(
    queries, out_grad, saved_output, key_rows, value_rows, hidden_rows, prefix_keys, prefix_values,
    prefix_hidden, block_mask, prefix_list, key_down, value_down, key_up, value_up,
):
    pair, prefix, summed = backward(
        block_mask[0], prefix_list, queries[0, 0], out_grad[0, 0], saved_output[0, 0],
        key_rows[0, 0], value_rows[0, 0], hidden_rows[0, 0], prefix_hidden[0],
        prefix_keys, prefix_values, key_down.T, value_down.T, key_up, value_up,
    )
    down, rise, pair, prefix = spread(summed, pair, prefix)
    down = jnp.swapaxes(down.reshape(2, BLK // 2, D), 1, 2)
    return pair[None], prefix[None], down, rise


def solution(mesh):
    row = P("grp", "seq", None, None)
    in_specs = (
        row, row, row, row, row, row, P(), P(),
        P("grp", "seq", None), P("grp", None, None), P("grp", None), P(), P(), P(), P(),
    )
    out_specs = (P("grp", "seq", None), P("grp", "seq", None), P(), P())
    return jax.shard_map(
        on_device, mesh=mesh, in_specs=in_specs, out_specs=out_specs, check_vma=False
    )
```

```python
import jax
import jax.numpy as jnp
from jax import lax
from jax.experimental import pallas as pl
from jax.experimental.pallas import tpu as pltpu
from jax.sharding import PartitionSpec as P

HEAD = 128
BLK = 128
NX = 4
SEQ = 16
GRP = 8
REP = 5
KV = 4
SPAN = 8
D = 5120
KVW = 512
DT = 640
TILE = 256
DEPTH = 144
TYPES = 3
W = REP * BLK
TREE = SEQ * BLK
GROUP = 4 * BLK
PAIR = 2 * HEAD
CHUNKS = ((0, 256), (256, 512), (512, 640))
MESH = pl.DeviceIdType.MESH
SCALE = HEAD ** (-0.5)
LOG2E = 1.4426950408889634
MASKED = -1e30
NT = (((1,), (1,)), ((), ()))
TN = (((0,), (0,)), ((), ()))
f32 = jnp.float32
bf16 = jnp.bfloat16


def vmem():
    return pl.BlockSpec(memory_space=pltpu.VMEM)


def hbm():
    return pl.BlockSpec(memory_space=pl.ANY)


def smem():
    return pl.BlockSpec(memory_space=pltpu.SMEM)


def remote(src, dst, send, recv, device):
    copy = pltpu.make_async_remote_copy(
        src_ref=src, dst_ref=dst, send_sem=send, recv_sem=recv, device_id=device, device_id_type=MESH
    )
    copy.start()
    return copy


def greet(devices):
    barrier = pltpu.get_barrier_semaphore()
    for device in devices:
        pl.semaphore_signal(barrier, inc=1, device_id=device, device_id_type=MESH)


def greeted(devices):
    pl.semaphore_wait(pltpu.get_barrier_semaphore(), len(devices))


def cols(i, width):
    return pl.ds(pl.multiple_of(i * width, 128), width)


def rows(i, count):
    return pl.ds(pl.multiple_of(i * count, count), count)


def kernel(
    mask, listed, q, g, saved, k, v, hidden, hidden_p, pool_k, pool_v, down_k, down_v, up_k, up_v,
    pair, prefix, out,
    q_in, g_in, delta_in, kv, own_g, own_s, own_h, own_p, down, pool, up, delta_out, all_g, back_all, back_t, proj_all, proj_t,
    s_ref, acc, qs, gs, pb, dsb, stat, diag,
    tsend, rt, proj_s, proj_r, pt, rp, back_s, back_r,
    s0, r0, s1, r1, s2, r2, full, own_x,
    sem_in, kvx_s, kvx_r, kvy_s, kvy_r, q_s, q_r, t_s, t_r, j_s, j_r, b_s, b_r, p_s, p_r,
    s0_s, s0_r, s1_s, s1_r, s2_s, s2_r, a2_s, a2_r, a1_s, a1_r, a0_s, a0_r,
):
    me, grp = lax.axis_index("seq"), lax.axis_index("grp")
    x, y = me // NX, lax.rem(me, NX)
    z, c = grp // 2, lax.rem(grp, 2)
    peers = [lax.rem(me + o, SEQ) for o in range(1, SEQ)]

    def at(xx, yy, zz):
        return {"seq": xx * NX + yy, "grp": zz * 2 + c}

    def line(t, i):
        n = [lax.rem(place + i, NX) for place in (z, x, y)]
        return (at(x, y, n[0]), at(n[1], y, z), at(x, n[2], z))[t]

    def plane(t, e):
        u, w = e // NX, lax.rem(e, NX)
        return (at(u, w, z), at(x, u, w), at(u, y, w))[t]

    on_line = (z, x, y)
    on_plane = (me, y * NX + z, x * NX + z)
    met = [{"grp": lax.rem(grp + i, GRP)} for i in range(1, GRP)]
    met += [{"seq": d} for d in peers]
    for i in range(1, NX):
        for j in range(1, NX):
            met.append(at(x, lax.rem(y + i, NX), lax.rem(z + j, NX)))
            met.append(at(lax.rem(x + i, NX), y, lax.rem(z + j, NX)))
    greet(met)

    def local(src, dst, i):
        copy = pltpu.make_async_copy(src, dst, sem_in.at[i])
        copy.start()
        return copy

    mine = rows(me, BLK)
    keep = [
        local(k.at[:, cols(x, HEAD)], kv.at[mine, 0:HEAD], 0),
        local(v.at[:, cols(x, HEAD)], kv.at[mine, HEAD:PAIR], 1),
        local(q.at[:, cols(x, DT)], q_in.at[x], 2),
        local(g.at[:, cols(x, DT)], g_in.at[x], 3),
        local(g, own_g, 4),
        local(saved, own_s, 5),
        local(hidden, own_h.at[0:BLK], 6),
        local(down_k, down.at[0:64], 7),
        local(down_v, down.at[64:128], 8),
        local(hidden_p, own_p, 9),
        local(pool_k.at[:, :, cols(x, HEAD)], pool.at[:, :, 0:HEAD], 10),
        local(pool_v.at[:, :, cols(x, HEAD)], pool.at[:, :, HEAD:PAIR], 11),
    ]
    keep[4].wait()
    keep[5].wait()
    ones = jnp.ones((8, HEAD), f32)
    for h in range(KV):
        for t in range(REP):
            cut = slice((h * REP + t) * HEAD, (h * REP + t + 1) * HEAD)
            prod = own_g[:, cut].astype(f32) * own_s[:, cut].astype(f32)
            delta_out[h, :, t * BLK : (t + 1) * BLK] = lax.dot_general(
                ones, prod, NT, preferred_element_type=f32, precision=lax.Precision.HIGHEST
            )
    delta_in[x] = delta_out[x]
    greeted(met)

    step_x, step_y, step_q, step_g = ([], []), ([], []), [], []

    def send_x(n, source, lanes):
        for i in range(1, NX):
            tx = lax.rem(x + i, NX)
            step_x[n].append(
                remote(
                    source.at[:, cols(tx, HEAD)], kv.at[mine, lanes], kvx_s.at[n, i], kvx_r.at[n, i],
                    {"seq": tx * NX + y},
                )
            )

    def send_y(n, k, lanes):
        block = rows(lax.rem(x + NX - k, NX) * NX + y, BLK)
        for i in range(1, NX):
            device = {"seq": x * NX + lax.rem(y + i, NX)}
            piece = kv.at[block, lanes]
            step_y[n].append(remote(piece, piece, kvy_s.at[n, k, i], kvy_r.at[n, k, i], device))

    def send_rows(n, source, target, steps):
        for i in range(1, NX):
            tx = lax.rem(x + i, NX)
            steps.append(
                remote(
                    source.at[:, cols(tx, DT)], target.at[x], q_s.at[n, i], q_r.at[n, i],
                    {"seq": tx * NX + y},
                )
            )

    key_lanes, value_lanes = slice(0, HEAD), slice(HEAD, PAIR)
    send_x(0, k, key_lanes)
    send_x(1, v, value_lanes)
    keep[0].wait()
    send_y(0, 0, key_lanes)
    keep[1].wait()
    send_y(1, 0, value_lanes)
    send_rows(0, q, q_in, step_q)
    for i in range(1, NX):
        tx = lax.rem(x + i, NX)
        device = {"seq": tx * NX + y}
        step_g.append(remote(delta_out.at[tx], delta_in.at[x], q_s.at[2, i], q_r.at[2, i], device))
    send_rows(1, g, g_in, step_g)
    for side, lanes in ((0, key_lanes), (1, value_lanes)):
        for n in (1, 3, 2):
            step_x[side][n - 1].wait_recv()
            send_y(side, n, lanes)

    for i in range(6, 10):
        keep[i].wait()
    own_h[BLK : BLK + SPAN, :] = own_p[...]
    own_h[BLK + SPAN : DEPTH, :] = jnp.zeros((SPAN, D), bf16)
    proj = lax.dot_general(own_h[...], down[...], NT, preferred_element_type=f32)
    proj_s[...] = proj[0:BLK].reshape(SEQ, SPAN, HEAD).astype(bf16)
    proj_all[BLK:DEPTH, :] = proj[BLK:DEPTH].astype(bf16)
    step_j = []
    for o, d in enumerate(peers):
        step_j.append(remote(proj_s.at[d], proj_r.at[me], j_s.at[o], j_r.at[o], {"seq": d}))
    proj_r[me] = proj_s[me]
    up[...] = jnp.zeros_like(up)
    up[0:64, 0:KVW] = up_k[...]
    up[64:128, KVW : 2 * KVW] = up_v[...]

    keep[10].wait()
    keep[11].wait()
    for i in range(2):
        kv[TREE + i * BLK : TREE + (i + 1) * BLK, :] = pool[listed[0, i]]
    acc[...] = jnp.zeros_like(acc)
    key_at = lax.broadcasted_iota(jnp.int32, (GROUP, BLK), 0)
    query_at = lax.broadcasted_iota(jnp.int32, (GROUP, BLK), 1)
    diag[...] = jnp.where(key_at <= y * BLK + query_at, 0.0, MASKED).astype(f32)
    keep[2].wait()
    for copy in step_q + step_y[0]:
        copy.wait_recv()

    def score_rows(kk):
        return 2 * BLK * kk * (kk + 2)

    def score_place(start, m):
        return pl.ds(pl.multiple_of(start + 2 * BLK + m * GROUP, 2 * BLK), GROUP)

    def ends_place(start):
        return pl.ds(pl.multiple_of(start, 2 * BLK), 2 * BLK)

    ends = slice(TREE, TREE + 2 * BLK)

    def scores(step, carry):
        kk = NX - 1 - step
        r = y + NX * kk
        start = score_rows(kk)
        for t in range(REP):
            span = slice(t * BLK, (t + 1) * BLK)
            qs[kk, span, :] = q_in[kk, :, span]
        top = stat.at[0, kk]
        low = stat.at[1, kk]
        top[...] = jnp.full_like(top, MASKED)
        low[...] = jnp.zeros_like(low)

        def hides(m):
            return [(mask[r, m * 4 + b].astype(f32) - 1.0) * 1e30 for b in range(4)]

        def score(place, into, hidden_by, diagonal, n):
            for lo, hi in CHUNKS:
                w = hi - lo
                s = lax.dot_general(kv[place, 0:HEAD], qs[kk, lo:hi, :], NT, preferred_element_type=f32)
                s = s * (SCALE * LOG2E)
                if diagonal:
                    s = s + jnp.concatenate([diag[...]] * (w // BLK), axis=1)
                s_ref[into, lo:hi] = s
                cut = s.reshape(n, BLK // 8, 8, w)
                before = top[:, lo:hi]
                now = before
                for b in range(n):
                    now = jnp.maximum(now, jnp.max(cut[b], axis=0) + hidden_by[b])
                part = low[:, lo:hi] * jnp.exp2(before - now)
                for b in range(n):
                    part += jnp.sum(jnp.exp2(cut[b] - (now - hidden_by[b])[None]), axis=0)
                low[:, lo:hi] = part
                top[:, lo:hi] = now

        def score_group(m, cc):
            score(rows(m, GROUP), score_place(start, m), hides(m), False, 4)
            return cc

        score(ends, ends_place(start), [0.0, 0.0], False, 2)
        lax.fori_loop(0, kk, score_group, 0)
        score(rows(kk, GROUP), score_place(start, kk), hides(kk), True, 4)
        best = jnp.max(top[...], axis=0, keepdims=True)
        total = jnp.sum(low[...] * jnp.exp2(top[...] - best), axis=0, keepdims=True)
        top[...] = jnp.broadcast_to(best + jnp.log2(total), (8, W))
        return carry

    lax.fori_loop(0, NX, scores, 0)
    keep[3].wait()
    for copy in step_g + step_y[1]:
        copy.wait_recv()

    def term(n, first_block, count, o):
        part = pl.ds(first_block, count)
        return pltpu.make_async_remote_copy(
            src_ref=tsend.at[peers[o], part], dst_ref=rt.at[me, part], send_sem=t_s.at[n, o],
            recv_sem=t_r.at[n, o], device_id={"seq": peers[o]}, device_id_type=MESH,
        )

    def rollout(step, carry):
        kk = NX - 1 - step
        r = y + NX * kk
        start = score_rows(kk)
        for t in range(REP):
            span = slice(t * BLK, (t + 1) * BLK)
            gs[span, :] = g_in[kk, :, span]
        top = stat.at[0, kk]
        low = delta_in.at[kk]

        def hides(m):
            return [(mask[r, m * 4 + b].astype(f32) - 1.0) * 1e30 for b in range(4)]

        def grads(place, into, hidden_by, n):
            for lo, hi in CHUNKS:
                w = hi - lo
                dp = lax.dot_general(kv[place, HEAD:PAIR], gs[lo:hi, :], NT, preferred_element_type=f32)
                dp = dp.reshape(n, BLK // 8, 8, w)
                cut = s_ref[into, lo:hi].reshape(n, BLK // 8, 8, w)
                for b in range(n):
                    span = slice(b * BLK, (b + 1) * BLK)
                    p = jnp.exp2(cut[b] - (top[:, lo:hi] - hidden_by[b])[None])
                    ds = p * (dp[b] - low[:, lo:hi][None])
                    pb[span, lo:hi] = p.reshape(BLK, w).astype(bf16)
                    dsb[span, lo:hi] = ds.reshape(BLK, w).astype(bf16)
            acc[place, 0:HEAD] += jnp.dot(dsb[0 : n * BLK, :], qs[kk], preferred_element_type=f32)
            acc[place, HEAD:PAIR] += jnp.dot(pb[0 : n * BLK, :], gs[...], preferred_element_type=f32)

        def grads_group(m, cc):
            grads(rows(m, GROUP), score_place(start, m), hides(m), 4)
            return cc

        grads(ends, ends_place(start), [0.0, 0.0], 2)

        @pl.when(step == NX - 1)
        def _():
            for i in range(2):
                part = acc[TREE + i * BLK : TREE + (i + 1) * BLK, :].reshape(SEQ, SPAN, PAIR)
                tsend[:, SEQ + i, :, 0:HEAD] = (part[:, :, 0:HEAD] * SCALE).astype(bf16)
                tsend[:, SEQ + i, :, HEAD:PAIR] = part[:, :, HEAD:PAIR].astype(bf16)
            for o in range(SEQ - 1):
                term(4, SEQ, 2, o).start()

        grads_group(kk, 0)
        for b in range(4):
            j = kk * 4 + b
            part = acc[rows(j, BLK), :].reshape(SEQ, SPAN, PAIR)
            tsend[:, j, :, 0:HEAD] = (part[:, :, 0:HEAD] * SCALE).astype(bf16)
            tsend[:, j, :, HEAD:PAIR] = part[:, :, HEAD:PAIR].astype(bf16)
        for o in range(SEQ - 1):
            term(kk, kk * 4, 4, o).start()
        lax.fori_loop(0, kk, grads_group, 0)
        return carry

    lax.fori_loop(0, NX, rollout, 0)
    step_e = [term(4, SEQ, 2, o) for o in range(SEQ - 1)]
    step_t = [term(kk, kk * 4, 4, o) for kk in range(NX) for o in range(SEQ - 1)]
    rt[me] = tsend[me]
    step_b = [
        pltpu.make_async_remote_copy(
            src_ref=back_s.at[peers[o]], dst_ref=back_r.at[me], send_sem=b_s.at[o], recv_sem=b_r.at[o],
            device_id={"seq": peers[o]}, device_id_type=MESH,
        )
        for o in range(SEQ - 1)
    ]

    def finish(m):
        for copy in step_t[m * 15 : m * 15 + 15]:
            copy.wait_recv()
        span = slice(m * 32, m * 32 + 32)
        for h in range(KV):
            for side in range(2):
                lanes = slice(side * HEAD, (side + 1) * HEAD)
                place = slice(side * KVW + h * HEAD, side * KVW + (h + 1) * HEAD)
                total = rt[NX * h, 4 * m : 4 * m + 4, :, lanes].astype(f32)
                for a in range(1, NX):
                    total += rt[NX * h + a, 4 * m : 4 * m + 4, :, lanes].astype(f32)
                all_g[span, place] = total.reshape(32, HEAD).astype(bf16)
        back = lax.dot_general(all_g[span, :], up[...], NT, preferred_element_type=f32)
        back_s[4 * m : 4 * m + 4] = back.reshape(4, SPAN, HEAD).astype(bf16)
        for j in range(4 * m, 4 * m + 4):

            @pl.when(me != j)
            def _():
                o = lax.rem(j - me + 2 * SEQ - 1, SEQ)
                remote(back_s.at[j], back_r.at[me], b_s.at[o], b_r.at[o], {"seq": j})

    for m in (3, 2, 1):
        finish(m)
    for copy in step_e:
        copy.wait_recv()
    for h in range(KV):
        for side in range(2):
            lanes = slice(side * HEAD, (side + 1) * HEAD)
            place = slice(side * KVW + h * HEAD, side * KVW + (h + 1) * HEAD)
            for i in range(2):
                part = rt[NX * h, SEQ + i, :, lanes].astype(f32)
                for a in range(1, NX):
                    part += rt[NX * h + a, SEQ + i, :, lanes].astype(f32)
                rp[i, :, place] = part
    for b in range(GRP):
        pt[b] = rp[0] * (listed[0, 0] == b).astype(f32) + rp[1] * (listed[0, 1] == b).astype(f32)
    step_p = []
    for i in range(1, GRP):
        b = lax.rem(grp + i, GRP)
        step_p.append(remote(pt.at[b], rp.at[1 + i], p_s.at[i], p_r.at[i], {"grp": b}))
    finish(0)
    back_r[me] = back_s[me]
    for copy in step_p:
        copy.wait_recv()
    total = pt[grp]
    for i in range(1, GRP):
        total += rp[1 + i]
    own_x[...] = total
    keep.append(local(own_x, prefix, 12))
    tail = jnp.concatenate([total, jnp.zeros_like(total)], axis=0).astype(bf16)
    all_g[BLK:DEPTH, :] = tail
    back_all[BLK:DEPTH, :] = lax.dot_general(tail, up[...], NT, preferred_element_type=f32).astype(bf16)
    keep.append(local(all_g.at[0:BLK], pair, 13))
    for copy in step_j:
        copy.wait_recv()
    proj_all[0:BLK, :] = proj_r[...].reshape(BLK, HEAD)
    same = lax.broadcasted_iota(jnp.int32, (HEAD, HEAD), 0) == lax.broadcasted_iota(jnp.int32, (HEAD, HEAD), 1)
    eye = same.astype(f32).astype(bf16)
    proj_t[...] = lax.dot_general(eye, proj_all[...], NT, preferred_element_type=f32).astype(bf16)
    for a in range(NX):
        cut = slice(a * TILE, (a + 1) * TILE)
        s0[1, 2, a] = jnp.dot(proj_t[...], all_g[:, cut], preferred_element_type=f32).astype(bf16)
    for copy in step_b:
        copy.wait_recv()

    back_all[0:BLK, :] = back_r[...].reshape(BLK, HEAD)
    back_t[...] = lax.dot_general(eye, back_all[...], NT, preferred_element_type=f32).astype(bf16)
    sibling = {"grp": grp + 1 - 2 * c}
    zero, first, second, third, fourth, fifth = [], [], [], [], [], []
    for t in range(TYPES):
        for half in range(2):
            for a in range(NX):
                n = (half * TYPES + t) * NX + a
                if n < D // TILE:
                    cut = slice(n * TILE, (n + 1) * TILE)
                    part = jnp.dot(back_t[...], own_h[:, cut], preferred_element_type=f32)
                    s0[half, t, a] = part.astype(bf16)
        zero.append(remote(s0.at[1 - c, t], r0.at[t], s0_s.at[t], s0_r.at[t], sibling))
    for t in range(TYPES):
        zero[t].wait_recv()
        for a in range(NX):
            s1[t, a] = (s0[c, t, a].astype(f32) + r0[t, a].astype(f32)).astype(bf16)
        for i in range(1, NX):
            there = lax.rem(on_line[t] + i, NX)
            first.append(remote(s1.at[t, there], r1.at[t, i - 1], s1_s.at[t, i], s1_r.at[t, i], line(t, i)))
    for t in range(TYPES):
        for copy in first[t * 3 : t * 3 + 3]:
            copy.wait_recv()
        total = s1[t, on_line[t]].astype(f32)
        for i in range(NX - 1):
            total += r1[t, i].astype(f32)
        s2[t] = total.reshape(SEQ, SPAN, TILE).astype(bf16)
        for o in range(SEQ - 1):
            e = lax.rem(on_plane[t] + o + 1, SEQ)
            second.append(remote(s2.at[t, e], r2.at[t, o], s2_s.at[t, o], s2_r.at[t, o], plane(t, e)))
    for t in range(TYPES):
        for copy in second[t * 15 : t * 15 + 15]:
            copy.wait_recv()
        total = s2[t, on_plane[t]].astype(f32)
        for o in range(SEQ - 1):
            total += r2[t, o].astype(f32)
        full[t, on_line[t], on_plane[t]] = total.astype(bf16)
        piece = full.at[t, on_line[t], on_plane[t]]
        for o in range(SEQ - 1):
            e = lax.rem(on_plane[t] + o + 1, SEQ)
            third.append(remote(piece, piece, a2_s.at[t, o], a2_r.at[t, o], plane(t, e)))
    for t in range(TYPES):
        for copy in third[t * 15 : t * 15 + 15]:
            copy.wait_recv()
        piece = full.at[t, on_line[t]]
        for i in range(1, NX):
            fourth.append(remote(piece, piece, a1_s.at[t, i], a1_r.at[t, i], line(t, i)))
    for t in range(TYPES):
        for copy in fourth[t * 3 : t * 3 + 3]:
            copy.wait_recv()
        fifth.append(remote(full.at[t], out.at[c, t], a0_s.at[t], a0_r.at[t], sibling))
        keep.append(local(full.at[t], out.at[c, t], 14 + t))
    for copy in fifth:
        copy.wait_recv()
    for copy in keep[12:]:
        copy.wait()

    for copy in (
        step_x[0] + step_x[1] + step_y[0] + step_y[1] + step_q + step_g + step_j + step_e + step_t + step_p + step_b
        + zero + first + second + third + fourth + fifth
    ):
        copy.wait_send()


def backward(*operands):
    dma = pltpu.SemaphoreType.DMA

    def low(*shape):
        return pltpu.VMEM(shape, bf16)

    def wide(*shape):
        return pltpu.VMEM(shape, f32)

    return pl.pallas_call(
        kernel,
        out_shape=(
            jax.ShapeDtypeStruct((BLK, 2 * KVW), bf16),
            jax.ShapeDtypeStruct((SPAN, 2 * KVW), f32),
            jax.ShapeDtypeStruct((2, TYPES, NX, SEQ, SPAN, TILE), bf16),
        ),
        in_specs=[smem()] * 2 + [hbm()] * 11 + [vmem()] * 2,
        out_specs=(hbm(),) * 3,
        scratch_shapes=[
            low(NX, BLK, DT), low(NX, BLK, DT), wide(NX, 8, W), low(TREE + 2 * BLK, PAIR),
            low(BLK, 4 * DT), low(BLK, 4 * DT), low(DEPTH, D), low(SPAN, D), low(HEAD, D),
            low(GRP, BLK, PAIR), low(HEAD, 2 * KVW), wide(KV, 8, W),
            low(DEPTH, 2 * KVW), low(DEPTH, HEAD), low(HEAD, DEPTH), low(DEPTH, HEAD), low(HEAD, DEPTH),
            wide(2 * BLK * NX * (NX + 2), W), wide(TREE + 2 * BLK, PAIR), low(NX, W, HEAD), low(W, HEAD),
            low(GROUP, W), low(GROUP, W), wide(2, NX, 8, W), wide(GROUP, BLK),
            low(SEQ, SEQ + 2, SPAN, PAIR), low(SEQ, SEQ + 2, SPAN, PAIR),
            low(SEQ, SPAN, HEAD), low(SEQ, SPAN, HEAD),
            wide(GRP, SPAN, 2 * KVW), wide(GRP + 1, SPAN, 2 * KVW),
            low(SEQ, SPAN, HEAD), low(SEQ, SPAN, HEAD),
            low(2, TYPES, NX, BLK, TILE), low(TYPES, NX, BLK, TILE), low(TYPES, NX, BLK, TILE),
            low(TYPES, NX - 1, BLK, TILE), low(TYPES, SEQ, SPAN, TILE), low(TYPES, SEQ - 1, SPAN, TILE),
            low(TYPES, NX, SEQ, SPAN, TILE), wide(SPAN, 2 * KVW),
            dma((17,)),
            dma((2, NX)), dma((2, NX)), dma((2, NX, NX)), dma((2, NX, NX)), dma((3, NX)), dma((3, NX)),
            dma((5, SEQ)), dma((5, SEQ)), dma((SEQ,)), dma((SEQ,)), dma((SEQ,)), dma((SEQ,)),
            dma((GRP,)), dma((GRP,)),
            dma((TYPES,)), dma((TYPES,)), dma((TYPES, NX)), dma((TYPES, NX)),
            dma((TYPES, SEQ)), dma((TYPES, SEQ)), dma((TYPES, SEQ)), dma((TYPES, SEQ)),
            dma((TYPES, NX)), dma((TYPES, NX)), dma((TYPES,)), dma((TYPES,)),
        ],
        compiler_params=pltpu.CompilerParams(
            collective_id=0, has_side_effects=True, vmem_limit_bytes=56 * 2**20
        ),
        name="backward",
    )(*operands)


def spread_kernel(summed, pair, prefix, down, rise, pair_out, prefix_out, got, made, risen, pair_got, prefix_got, sem_got, sem_made):
    factor = 2.0 / (GRP * SEQ)
    arrive = [pltpu.make_async_copy(summed.at[i], got.at[i], sem_got.at[i]) for i in range(2 * TYPES)]
    through = [
        pltpu.make_async_copy(pair, pair_got, sem_got.at[6]),
        pltpu.make_async_copy(prefix, prefix_got, sem_got.at[7]),
    ]
    for copy in arrive + through:
        copy.start()
    leave = []
    for i in range(2 * TYPES):
        arrive[i].wait()
        for a in range(NX):
            part = got[i, a].reshape(BLK, TILE).astype(f32) * factor
            if i < 5:
                made[i, :, a * TILE : (a + 1) * TILE] = part
            else:
                side = a // 2
                risen[side, :, (a % 2) * TILE : (a % 2 + 1) * TILE] = part[side * 64 : side * 64 + 64]
        if i < 5:
            for half in range(2):
                cut = slice(half * 64, half * 64 + 64)
                leave.append(
                    pltpu.make_async_copy(
                        made.at[i, cut], down.at[cut, i * NX * TILE : (i + 1) * NX * TILE],
                        sem_made.at[2 + 2 * i + half],
                    )
                )
                leave[-1].start()
        else:
            leave.append(pltpu.make_async_copy(risen, rise, sem_made.at[12]))
            leave[-1].start()
    for i, (source, target) in enumerate(((pair_got, pair_out), (prefix_got, prefix_out))):
        through[i].wait()
        leave.append(pltpu.make_async_copy(source, target, sem_made.at[i]))
        leave[-1].start()
    for copy in leave:
        copy.wait()


def spread(summed, pair, prefix):
    return pl.pallas_call(
        spread_kernel,
        out_shape=(
            jax.ShapeDtypeStruct((BLK, D), f32),
            jax.ShapeDtypeStruct((2, 64, KVW), f32),
            jax.ShapeDtypeStruct((BLK, 2 * KVW), bf16),
            jax.ShapeDtypeStruct((SPAN, 2 * KVW), f32),
        ),
        in_specs=[hbm()] * 3,
        out_specs=(hbm(),) * 4,
        scratch_shapes=[
            pltpu.VMEM((2 * TYPES, NX, SEQ, SPAN, TILE), bf16),
            pltpu.VMEM((5, BLK, NX * TILE), f32),
            pltpu.VMEM((2, 64, KVW), f32),
            pltpu.VMEM((BLK, 2 * KVW), bf16),
            pltpu.VMEM((SPAN, 2 * KVW), f32),
            pltpu.SemaphoreType.DMA((2 * TYPES + 2,)),
            pltpu.SemaphoreType.DMA((13,)),
        ],
        compiler_params=pltpu.CompilerParams(vmem_limit_bytes=60 * 2**20),
        name="spread",
    )(summed.reshape(2 * TYPES, NX, SEQ, SPAN, TILE), pair, prefix)


def on_device(
    queries, out_grad, saved_output, key_rows, value_rows, hidden_rows, prefix_keys, prefix_values,
    prefix_hidden, block_mask, prefix_list, key_down, value_down, key_up, value_up,
):
    pair, prefix, summed = backward(
        block_mask[0], prefix_list, queries[0, 0], out_grad[0, 0], saved_output[0, 0],
        key_rows[0, 0], value_rows[0, 0], hidden_rows[0, 0], prefix_hidden[0],
        prefix_keys, prefix_values, key_down.T, value_down.T, key_up, value_up,
    )
    down, rise, pair, prefix = spread(summed, pair, prefix)
    down = jnp.swapaxes(down.reshape(2, BLK // 2, D), 1, 2)
    return pair[None], prefix[None], down, rise


def solution(mesh):
    row = P("grp", "seq", None, None)
    in_specs = (
        row, row, row, row, row, row, P(), P(),
        P("grp", "seq", None), P("grp", None, None), P("grp", None), P(), P(), P(), P(),
    )
    out_specs = (P("grp", "seq", None), P("grp", "seq", None), P(), P())
    return jax.shard_map(
        on_device, mesh=mesh, in_specs=in_specs, out_specs=out_specs, check_vma=False
    )
```

```python
import jax
import jax.numpy as jnp
from jax import lax
from jax.experimental import pallas as pl
from jax.experimental.pallas import tpu as pltpu
from jax.sharding import PartitionSpec as P

HEAD = 128
BLK = 128
NX = 4
SEQ = 16
GRP = 8
REP = 5
KV = 4
SPAN = 8
D = 5120
KVW = 512
DT = 640
TILE = 256
DEPTH = 144
TYPES = 3
W = REP * BLK
TREE = SEQ * BLK
GROUP = 4 * BLK
PAIR = 2 * HEAD
CHUNKS = ((0, 256), (256, 512), (512, 640))
MESH = pl.DeviceIdType.MESH
SCALE = HEAD ** (-0.5)
LOG2E = 1.4426950408889634
MASKED = -1e30
NT = (((1,), (1,)), ((), ()))
TN = (((0,), (0,)), ((), ()))
f32 = jnp.float32
bf16 = jnp.bfloat16


def vmem():
    return pl.BlockSpec(memory_space=pltpu.VMEM)


def hbm():
    return pl.BlockSpec(memory_space=pl.ANY)


def smem():
    return pl.BlockSpec(memory_space=pltpu.SMEM)


def remote(src, dst, send, recv, device):
    copy = pltpu.make_async_remote_copy(
        src_ref=src, dst_ref=dst, send_sem=send, recv_sem=recv, device_id=device, device_id_type=MESH
    )
    copy.start()
    return copy


def greet(devices):
    barrier = pltpu.get_barrier_semaphore()
    for device in devices:
        pl.semaphore_signal(barrier, inc=1, device_id=device, device_id_type=MESH)


def greeted(devices):
    pl.semaphore_wait(pltpu.get_barrier_semaphore(), len(devices))


def cols(i, width):
    return pl.ds(pl.multiple_of(i * width, 128), width)


def rows(i, count):
    return pl.ds(pl.multiple_of(i * count, count), count)


def kernel(
    mask, listed, q, g, saved, k, v, hidden, hidden_p, pool_k, pool_v, down_k, down_v, up_k, up_v,
    pair, prefix, out,
    q_in, g_in, delta_in, kv, own_g, own_s, own_h, own_p, down, pool, up, delta_out, all_g, back_all, back_t, proj_all, proj_t,
    s_ref, acc, qs, gs, pb, dsb, stat, diag,
    tsend, rt, proj_s, proj_r, pt, rp, back_s, back_r,
    s0, r0, s1, r1, s2, r2, full, own_x,
    sem_in, kvx_s, kvx_r, kvy_s, kvy_r, q_s, q_r, t_s, t_r, j_s, j_r, b_s, b_r, p_s, p_r,
    s0_s, s0_r, s1_s, s1_r, s2_s, s2_r, a2_s, a2_r, a1_s, a1_r, a0_s, a0_r,
):
    me, grp = lax.axis_index("seq"), lax.axis_index("grp")
    x, y = me // NX, lax.rem(me, NX)
    z, c = grp // 2, lax.rem(grp, 2)
    peers = [lax.rem(me + o, SEQ) for o in range(1, SEQ)]

    def at(xx, yy, zz):
        return {"seq": xx * NX + yy, "grp": zz * 2 + c}

    def line(t, i):
        n = [lax.rem(place + i, NX) for place in (z, x, y)]
        return (at(x, y, n[0]), at(n[1], y, z), at(x, n[2], z))[t]

    def plane(t, e):
        u, w = e // NX, lax.rem(e, NX)
        return (at(u, w, z), at(x, u, w), at(u, y, w))[t]

    on_line = (z, x, y)
    on_plane = (me, y * NX + z, x * NX + z)
    met = [{"grp": lax.rem(grp + i, GRP)} for i in range(1, GRP)]
    met += [{"seq": d} for d in peers]
    for i in range(1, NX):
        for j in range(1, NX):
            met.append(at(x, lax.rem(y + i, NX), lax.rem(z + j, NX)))
            met.append(at(lax.rem(x + i, NX), y, lax.rem(z + j, NX)))
    greet(met)

    def local(src, dst, i):
        copy = pltpu.make_async_copy(src, dst, sem_in.at[i])
        copy.start()
        return copy

    mine = rows(me, BLK)
    keep = [
        local(k.at[:, cols(x, HEAD)], kv.at[mine, 0:HEAD], 0),
        local(v.at[:, cols(x, HEAD)], kv.at[mine, HEAD:PAIR], 1),
        local(q.at[:, cols(x, DT)], q_in.at[x], 2),
        local(g.at[:, cols(x, DT)], g_in.at[x], 3),
        local(g, own_g, 4),
        local(saved, own_s, 5),
        local(hidden, own_h.at[0:BLK], 6),
        local(down_k, down.at[0:64], 7),
        local(down_v, down.at[64:128], 8),
        local(hidden_p, own_p, 9),
        local(pool_k.at[:, :, cols(x, HEAD)], pool.at[:, :, 0:HEAD], 10),
        local(pool_v.at[:, :, cols(x, HEAD)], pool.at[:, :, HEAD:PAIR], 11),
    ]
    keep[4].wait()
    keep[5].wait()
    ones = jnp.ones((8, HEAD), f32)
    for h in range(KV):
        for t in range(REP):
            cut = slice((h * REP + t) * HEAD, (h * REP + t + 1) * HEAD)
            prod = own_g[:, cut].astype(f32) * own_s[:, cut].astype(f32)
            delta_out[h, :, t * BLK : (t + 1) * BLK] = lax.dot_general(
                ones, prod, NT, preferred_element_type=f32, precision=lax.Precision.HIGHEST
            )
    delta_in[x] = delta_out[x]
    greeted(met)

    step_x, step_y, step_q, step_g = ([], []), ([], []), [], []

    def send_x(n, source, lanes):
        for i in range(1, NX):
            tx = lax.rem(x + i, NX)
            step_x[n].append(
                remote(
                    source.at[:, cols(tx, HEAD)], kv.at[mine, lanes], kvx_s.at[n, i], kvx_r.at[n, i],
                    {"seq": tx * NX + y},
                )
            )

    def send_y(n, k, lanes):
        block = rows(lax.rem(x + NX - k, NX) * NX + y, BLK)
        for i in range(1, NX):
            device = {"seq": x * NX + lax.rem(y + i, NX)}
            piece = kv.at[block, lanes]
            step_y[n].append(remote(piece, piece, kvy_s.at[n, k, i], kvy_r.at[n, k, i], device))

    def send_rows(n, source, target, steps):
        for i in range(1, NX):
            tx = lax.rem(x + i, NX)
            steps.append(
                remote(
                    source.at[:, cols(tx, DT)], target.at[x], q_s.at[n, i], q_r.at[n, i],
                    {"seq": tx * NX + y},
                )
            )

    key_lanes, value_lanes = slice(0, HEAD), slice(HEAD, PAIR)
    send_x(0, k, key_lanes)
    send_x(1, v, value_lanes)
    keep[0].wait()
    send_y(0, 0, key_lanes)
    keep[1].wait()
    send_y(1, 0, value_lanes)
    send_rows(0, q, q_in, step_q)
    for i in range(1, NX):
        tx = lax.rem(x + i, NX)
        device = {"seq": tx * NX + y}
        step_g.append(remote(delta_out.at[tx], delta_in.at[x], q_s.at[2, i], q_r.at[2, i], device))
    send_rows(1, g, g_in, step_g)
    for side, lanes in ((0, key_lanes), (1, value_lanes)):
        for n in (1, 3, 2):
            step_x[side][n - 1].wait_recv()
            send_y(side, n, lanes)

    for i in range(6, 10):
        keep[i].wait()
    own_h[BLK : BLK + SPAN, :] = own_p[...]
    own_h[BLK + SPAN : DEPTH, :] = jnp.zeros((SPAN, D), bf16)
    proj = lax.dot_general(own_h[...], down[...], NT, preferred_element_type=f32)
    proj_s[...] = proj[0:BLK].reshape(SEQ, SPAN, HEAD).astype(bf16)
    proj_all[BLK:DEPTH, :] = proj[BLK:DEPTH].astype(bf16)
    step_j = []
    for o, d in enumerate(peers):
        step_j.append(remote(proj_s.at[d], proj_r.at[me], j_s.at[o], j_r.at[o], {"seq": d}))
    proj_r[me] = proj_s[me]
    up[...] = jnp.zeros_like(up)
    up[0:64, 0:KVW] = up_k[...]
    up[64:128, KVW : 2 * KVW] = up_v[...]

    keep[10].wait()
    keep[11].wait()
    for i in range(2):
        kv[TREE + i * BLK : TREE + (i + 1) * BLK, :] = pool[listed[0, i]]
    acc[...] = jnp.zeros_like(acc)
    key_at = lax.broadcasted_iota(jnp.int32, (GROUP, BLK), 0)
    query_at = lax.broadcasted_iota(jnp.int32, (GROUP, BLK), 1)
    diag[...] = jnp.where(key_at <= y * BLK + query_at, 0.0, MASKED).astype(f32)
    keep[2].wait()
    for copy in step_q + step_y[0]:
        copy.wait_recv()

    def score_rows(kk):
        return 2 * BLK * kk * (kk + 2)

    def score_place(start, m):
        return pl.ds(pl.multiple_of(start + 2 * BLK + m * GROUP, 2 * BLK), GROUP)

    def ends_place(start):
        return pl.ds(pl.multiple_of(start, 2 * BLK), 2 * BLK)

    ends = slice(TREE, TREE + 2 * BLK)

    def scores(step, carry):
        kk = NX - 1 - step
        r = y + NX * kk
        start = score_rows(kk)
        for t in range(REP):
            span = slice(t * BLK, (t + 1) * BLK)
            qs[kk, span, :] = q_in[kk, :, span]
        top = stat.at[0, kk]
        low = stat.at[1, kk]
        top[...] = jnp.full_like(top, MASKED)
        low[...] = jnp.zeros_like(low)

        def hides(m):
            return [(mask[r, m * 4 + b].astype(f32) - 1.0) * 1e30 for b in range(4)]

        def score(place, into, hidden_by, diagonal, n):
            for lo, hi in CHUNKS:
                w = hi - lo
                s = lax.dot_general(kv[place, 0:HEAD], qs[kk, lo:hi, :], NT, preferred_element_type=f32)
                s = s * (SCALE * LOG2E)
                if diagonal:
                    s = s + jnp.concatenate([diag[...]] * (w // BLK), axis=1)
                s_ref[into, lo:hi] = s
                cut = s.reshape(n, BLK // 8, 8, w)
                before = top[:, lo:hi]
                now = before
                for b in range(n):
                    now = jnp.maximum(now, jnp.max(cut[b], axis=0) + hidden_by[b])
                part = low[:, lo:hi] * jnp.exp2(before - now)
                for b in range(n):
                    part += jnp.sum(jnp.exp2(cut[b] - (now - hidden_by[b])[None]), axis=0)
                low[:, lo:hi] = part
                top[:, lo:hi] = now

        def score_group(m, cc):
            score(rows(m, GROUP), score_place(start, m), hides(m), False, 4)
            return cc

        score(ends, ends_place(start), [0.0, 0.0], False, 2)
        lax.fori_loop(0, kk, score_group, 0)
        score(rows(kk, GROUP), score_place(start, kk), hides(kk), True, 4)
        best = jnp.max(top[...], axis=0, keepdims=True)
        total = jnp.sum(low[...] * jnp.exp2(top[...] - best), axis=0, keepdims=True)
        top[...] = jnp.broadcast_to(best + jnp.log2(total), (8, W))
        return carry

    lax.fori_loop(0, NX, scores, 0)
    keep[3].wait()
    for copy in step_g + step_y[1]:
        copy.wait_recv()

    def term(n, first_block, count, o):
        part = pl.ds(first_block, count)
        return pltpu.make_async_remote_copy(
            src_ref=tsend.at[peers[o], part], dst_ref=rt.at[me, part], send_sem=t_s.at[n, o],
            recv_sem=t_r.at[n, o], device_id={"seq": peers[o]}, device_id_type=MESH,
        )

    def rollout(step, carry):
        kk = NX - 1 - step
        r = y + NX * kk
        start = score_rows(kk)
        for t in range(REP):
            span = slice(t * BLK, (t + 1) * BLK)
            gs[span, :] = g_in[kk, :, span]
        top = stat.at[0, kk]
        low = delta_in.at[kk]

        def hides(m):
            return [(mask[r, m * 4 + b].astype(f32) - 1.0) * 1e30 for b in range(4)]

        def grads(place, into, hidden_by, n):
            for lo, hi in CHUNKS:
                w = hi - lo
                dp = lax.dot_general(kv[place, HEAD:PAIR], gs[lo:hi, :], NT, preferred_element_type=f32)
                dp = dp.reshape(n, BLK // 8, 8, w)
                cut = s_ref[into, lo:hi].reshape(n, BLK // 8, 8, w)
                for b in range(n):
                    span = slice(b * BLK, (b + 1) * BLK)
                    p = jnp.exp2(cut[b] - (top[:, lo:hi] - hidden_by[b])[None])
                    ds = p * (dp[b] - low[:, lo:hi][None])
                    pb[span, lo:hi] = p.reshape(BLK, w).astype(bf16)
                    dsb[span, lo:hi] = ds.reshape(BLK, w).astype(bf16)
            acc[place, 0:HEAD] += jnp.dot(dsb[0 : n * BLK, :], qs[kk], preferred_element_type=f32)
            acc[place, HEAD:PAIR] += jnp.dot(pb[0 : n * BLK, :], gs[...], preferred_element_type=f32)

        def grads_group(m, cc):
            grads(rows(m, GROUP), score_place(start, m), hides(m), 4)
            return cc

        grads_group(kk, 0)
        for b in range(4):
            j = kk * 4 + b
            part = acc[rows(j, BLK), :].reshape(SEQ, SPAN, PAIR)
            tsend[:, j, :, 0:HEAD] = (part[:, :, 0:HEAD] * SCALE).astype(bf16)
            tsend[:, j, :, HEAD:PAIR] = part[:, :, HEAD:PAIR].astype(bf16)
        for o in range(SEQ - 1):
            term(kk, kk * 4, 4, o).start()
        lax.fori_loop(0, kk, grads_group, 0)
        grads(ends, ends_place(start), [0.0, 0.0], 2)

        @pl.when(step == NX - 1)
        def _():
            for i in range(2):
                part = acc[TREE + i * BLK : TREE + (i + 1) * BLK, :].reshape(SEQ, SPAN, PAIR)
                tsend[:, SEQ + i, :, 0:HEAD] = (part[:, :, 0:HEAD] * SCALE).astype(bf16)
                tsend[:, SEQ + i, :, HEAD:PAIR] = part[:, :, HEAD:PAIR].astype(bf16)
            for o in range(SEQ - 1):
                term(4, SEQ, 2, o).start()

        return carry

    lax.fori_loop(0, NX, rollout, 0)
    step_e = [term(4, SEQ, 2, o) for o in range(SEQ - 1)]
    step_t = [term(kk, kk * 4, 4, o) for kk in range(NX) for o in range(SEQ - 1)]
    rt[me] = tsend[me]
    step_b = [
        pltpu.make_async_remote_copy(
            src_ref=back_s.at[peers[o]], dst_ref=back_r.at[me], send_sem=b_s.at[o], recv_sem=b_r.at[o],
            device_id={"seq": peers[o]}, device_id_type=MESH,
        )
        for o in range(SEQ - 1)
    ]

    def finish(m):
        for copy in step_t[m * 15 : m * 15 + 15]:
            copy.wait_recv()
        span = slice(m * 32, m * 32 + 32)
        for h in range(KV):
            for side in range(2):
                lanes = slice(side * HEAD, (side + 1) * HEAD)
                place = slice(side * KVW + h * HEAD, side * KVW + (h + 1) * HEAD)
                total = rt[NX * h, 4 * m : 4 * m + 4, :, lanes].astype(f32)
                for a in range(1, NX):
                    total += rt[NX * h + a, 4 * m : 4 * m + 4, :, lanes].astype(f32)
                all_g[span, place] = total.reshape(32, HEAD).astype(bf16)
        back = lax.dot_general(all_g[span, :], up[...], NT, preferred_element_type=f32)
        back_s[4 * m : 4 * m + 4] = back.reshape(4, SPAN, HEAD).astype(bf16)
        for j in range(4 * m, 4 * m + 4):

            @pl.when(me != j)
            def _():
                o = lax.rem(j - me + 2 * SEQ - 1, SEQ)
                remote(back_s.at[j], back_r.at[me], b_s.at[o], b_r.at[o], {"seq": j})

    for m in (3, 2, 1, 0):
        finish(m)
    back_r[me] = back_s[me]
    for copy in step_e:
        copy.wait_recv()
    for h in range(KV):
        for side in range(2):
            lanes = slice(side * HEAD, (side + 1) * HEAD)
            place = slice(side * KVW + h * HEAD, side * KVW + (h + 1) * HEAD)
            for i in range(2):
                part = rt[NX * h, SEQ + i, :, lanes].astype(f32)
                for a in range(1, NX):
                    part += rt[NX * h + a, SEQ + i, :, lanes].astype(f32)
                rp[i, :, place] = part
    for b in range(GRP):
        pt[b] = rp[0] * (listed[0, 0] == b).astype(f32) + rp[1] * (listed[0, 1] == b).astype(f32)
    step_p = []
    for i in range(1, GRP):
        b = lax.rem(grp + i, GRP)
        step_p.append(remote(pt.at[b], rp.at[1 + i], p_s.at[i], p_r.at[i], {"grp": b}))
    for copy in step_p:
        copy.wait_recv()
    total = pt[grp]
    for i in range(1, GRP):
        total += rp[1 + i]
    own_x[...] = total
    keep.append(local(own_x, prefix, 12))
    tail = jnp.concatenate([total, jnp.zeros_like(total)], axis=0).astype(bf16)
    all_g[BLK:DEPTH, :] = tail
    back_all[BLK:DEPTH, :] = lax.dot_general(tail, up[...], NT, preferred_element_type=f32).astype(bf16)
    keep.append(local(all_g.at[0:BLK], pair, 13))
    for copy in step_j:
        copy.wait_recv()
    proj_all[0:BLK, :] = proj_r[...].reshape(BLK, HEAD)
    same = lax.broadcasted_iota(jnp.int32, (HEAD, HEAD), 0) == lax.broadcasted_iota(jnp.int32, (HEAD, HEAD), 1)
    eye = same.astype(f32).astype(bf16)
    proj_t[...] = lax.dot_general(eye, proj_all[...], NT, preferred_element_type=f32).astype(bf16)
    for a in range(NX):
        cut = slice(a * TILE, (a + 1) * TILE)
        s0[1, 2, a] = jnp.dot(proj_t[...], all_g[:, cut], preferred_element_type=f32).astype(bf16)
    for copy in step_b:
        copy.wait_recv()

    back_all[0:BLK, :] = back_r[...].reshape(BLK, HEAD)
    back_t[...] = lax.dot_general(eye, back_all[...], NT, preferred_element_type=f32).astype(bf16)
    sibling = {"grp": grp + 1 - 2 * c}
    zero, first, second, third, fourth, fifth = [], [], [], [], [], []

    def down_terms(half, t):
        for a in range(NX):
            cut = cols((half * TYPES + t) * NX + a, TILE)
            s0[half, t, a] = jnp.dot(back_t[...], own_h[:, cut], preferred_element_type=f32).astype(bf16)

    for t in range(TYPES):
        if t < 2:
            down_terms(1 - c, t)
        else:
            down_terms(0, t)
        zero.append(remote(s0.at[1 - c, t], r0.at[t], s0_s.at[t], s0_r.at[t], sibling))
    for t in range(2):
        down_terms(c, t)
    for t in range(TYPES):
        zero[t].wait_recv()
        for a in range(NX):
            s1[t, a] = (s0[c, t, a].astype(f32) + r0[t, a].astype(f32)).astype(bf16)
        for i in range(1, NX):
            there = lax.rem(on_line[t] + i, NX)
            first.append(remote(s1.at[t, there], r1.at[t, i - 1], s1_s.at[t, i], s1_r.at[t, i], line(t, i)))
    for t in range(TYPES):
        for copy in first[t * 3 : t * 3 + 3]:
            copy.wait_recv()
        total = s1[t, on_line[t]].astype(f32)
        for i in range(NX - 1):
            total += r1[t, i].astype(f32)
        s2[t] = total.reshape(SEQ, SPAN, TILE).astype(bf16)
        for o in range(SEQ - 1):
            e = lax.rem(on_plane[t] + o + 1, SEQ)
            second.append(remote(s2.at[t, e], r2.at[t, o], s2_s.at[t, o], s2_r.at[t, o], plane(t, e)))
    for t in range(TYPES):
        for copy in second[t * 15 : t * 15 + 15]:
            copy.wait_recv()
        total = s2[t, on_plane[t]].astype(f32)
        for o in range(SEQ - 1):
            total += r2[t, o].astype(f32)
        full[t, on_line[t], on_plane[t]] = total.astype(bf16)
        piece = full.at[t, on_line[t], on_plane[t]]
        for o in range(SEQ - 1):
            e = lax.rem(on_plane[t] + o + 1, SEQ)
            third.append(remote(piece, piece, a2_s.at[t, o], a2_r.at[t, o], plane(t, e)))
    for t in range(TYPES):
        for copy in third[t * 15 : t * 15 + 15]:
            copy.wait_recv()
        piece = full.at[t, on_line[t]]
        for i in range(1, NX):
            fourth.append(remote(piece, piece, a1_s.at[t, i], a1_r.at[t, i], line(t, i)))
    for t in range(TYPES):
        for copy in fourth[t * 3 : t * 3 + 3]:
            copy.wait_recv()
        fifth.append(remote(full.at[t], out.at[c, t], a0_s.at[t], a0_r.at[t], sibling))
        keep.append(local(full.at[t], out.at[c, t], 14 + t))
    for copy in fifth:
        copy.wait_recv()
    for copy in keep[12:]:
        copy.wait()

    for copy in (
        step_x[0] + step_x[1] + step_y[0] + step_y[1] + step_q + step_g + step_j + step_e + step_t + step_p + step_b
        + zero + first + second + third + fourth + fifth
    ):
        copy.wait_send()


def backward(*operands):
    dma = pltpu.SemaphoreType.DMA

    def low(*shape):
        return pltpu.VMEM(shape, bf16)

    def wide(*shape):
        return pltpu.VMEM(shape, f32)

    return pl.pallas_call(
        kernel,
        out_shape=(
            jax.ShapeDtypeStruct((BLK, 2 * KVW), bf16),
            jax.ShapeDtypeStruct((SPAN, 2 * KVW), f32),
            jax.ShapeDtypeStruct((2, TYPES, NX, SEQ, SPAN, TILE), bf16),
        ),
        in_specs=[smem()] * 2 + [hbm()] * 11 + [vmem()] * 2,
        out_specs=(hbm(),) * 3,
        scratch_shapes=[
            low(NX, BLK, DT), low(NX, BLK, DT), wide(NX, 8, W), low(TREE + 2 * BLK, PAIR),
            low(BLK, 4 * DT), low(BLK, 4 * DT), low(DEPTH, D), low(SPAN, D), low(HEAD, D),
            low(GRP, BLK, PAIR), low(HEAD, 2 * KVW), wide(KV, 8, W),
            low(DEPTH, 2 * KVW), low(DEPTH, HEAD), low(HEAD, DEPTH), low(DEPTH, HEAD), low(HEAD, DEPTH),
            wide(2 * BLK * NX * (NX + 2), W), wide(TREE + 2 * BLK, PAIR), low(NX, W, HEAD), low(W, HEAD),
            low(GROUP, W), low(GROUP, W), wide(2, NX, 8, W), wide(GROUP, BLK),
            low(SEQ, SEQ + 2, SPAN, PAIR), low(SEQ, SEQ + 2, SPAN, PAIR),
            low(SEQ, SPAN, HEAD), low(SEQ, SPAN, HEAD),
            wide(GRP, SPAN, 2 * KVW), wide(GRP + 1, SPAN, 2 * KVW),
            low(SEQ, SPAN, HEAD), low(SEQ, SPAN, HEAD),
            low(2, TYPES, NX, BLK, TILE), low(TYPES, NX, BLK, TILE), low(TYPES, NX, BLK, TILE),
            low(TYPES, NX - 1, BLK, TILE), low(TYPES, SEQ, SPAN, TILE), low(TYPES, SEQ - 1, SPAN, TILE),
            low(TYPES, NX, SEQ, SPAN, TILE), wide(SPAN, 2 * KVW),
            dma((17,)),
            dma((2, NX)), dma((2, NX)), dma((2, NX, NX)), dma((2, NX, NX)), dma((3, NX)), dma((3, NX)),
            dma((5, SEQ)), dma((5, SEQ)), dma((SEQ,)), dma((SEQ,)), dma((SEQ,)), dma((SEQ,)),
            dma((GRP,)), dma((GRP,)),
            dma((TYPES,)), dma((TYPES,)), dma((TYPES, NX)), dma((TYPES, NX)),
            dma((TYPES, SEQ)), dma((TYPES, SEQ)), dma((TYPES, SEQ)), dma((TYPES, SEQ)),
            dma((TYPES, NX)), dma((TYPES, NX)), dma((TYPES,)), dma((TYPES,)),
        ],
        compiler_params=pltpu.CompilerParams(
            collective_id=0, has_side_effects=True, vmem_limit_bytes=56 * 2**20
        ),
        name="backward",
    )(*operands)


def spread_kernel(summed, pair, prefix, down, rise, pair_out, prefix_out, got, made, risen, pair_got, prefix_got, sem_got, sem_made):
    factor = 2.0 / (GRP * SEQ)
    arrive = [pltpu.make_async_copy(summed.at[i], got.at[i], sem_got.at[i]) for i in range(2 * TYPES)]
    through = [
        pltpu.make_async_copy(pair, pair_got, sem_got.at[6]),
        pltpu.make_async_copy(prefix, prefix_got, sem_got.at[7]),
    ]
    for copy in arrive + through:
        copy.start()
    leave = []
    for i in range(2 * TYPES):
        arrive[i].wait()
        for a in range(NX):
            part = got[i, a].reshape(BLK, TILE).astype(f32) * factor
            if i < 5:
                made[i, :, a * TILE : (a + 1) * TILE] = part
            else:
                side = a // 2
                risen[side, :, (a % 2) * TILE : (a % 2 + 1) * TILE] = part[side * 64 : side * 64 + 64]
        if i < 5:
            for half in range(2):
                cut = slice(half * 64, half * 64 + 64)
                leave.append(
                    pltpu.make_async_copy(
                        made.at[i, cut], down.at[cut, i * NX * TILE : (i + 1) * NX * TILE],
                        sem_made.at[2 + 2 * i + half],
                    )
                )
                leave[-1].start()
        else:
            leave.append(pltpu.make_async_copy(risen, rise, sem_made.at[12]))
            leave[-1].start()
    for i, (source, target) in enumerate(((pair_got, pair_out), (prefix_got, prefix_out))):
        through[i].wait()
        leave.append(pltpu.make_async_copy(source, target, sem_made.at[i]))
        leave[-1].start()
    for copy in leave:
        copy.wait()


def spread(summed, pair, prefix):
    return pl.pallas_call(
        spread_kernel,
        out_shape=(
            jax.ShapeDtypeStruct((BLK, D), f32),
            jax.ShapeDtypeStruct((2, 64, KVW), f32),
            jax.ShapeDtypeStruct((BLK, 2 * KVW), bf16),
            jax.ShapeDtypeStruct((SPAN, 2 * KVW), f32),
        ),
        in_specs=[hbm()] * 3,
        out_specs=(hbm(),) * 4,
        scratch_shapes=[
            pltpu.VMEM((2 * TYPES, NX, SEQ, SPAN, TILE), bf16),
            pltpu.VMEM((5, BLK, NX * TILE), f32),
            pltpu.VMEM((2, 64, KVW), f32),
            pltpu.VMEM((BLK, 2 * KVW), bf16),
            pltpu.VMEM((SPAN, 2 * KVW), f32),
            pltpu.SemaphoreType.DMA((2 * TYPES + 2,)),
            pltpu.SemaphoreType.DMA((13,)),
        ],
        compiler_params=pltpu.CompilerParams(vmem_limit_bytes=60 * 2**20),
        name="spread",
    )(summed.reshape(2 * TYPES, NX, SEQ, SPAN, TILE), pair, prefix)


def on_device(
    queries, out_grad, saved_output, key_rows, value_rows, hidden_rows, prefix_keys, prefix_values,
    prefix_hidden, block_mask, prefix_list, key_down, value_down, key_up, value_up,
):
    pair, prefix, summed = backward(
        block_mask[0], prefix_list, queries[0, 0], out_grad[0, 0], saved_output[0, 0],
        key_rows[0, 0], value_rows[0, 0], hidden_rows[0, 0], prefix_hidden[0],
        prefix_keys, prefix_values, key_down.T, value_down.T, key_up, value_up,
    )
    down, rise, pair, prefix = spread(summed, pair, prefix)
    down = jnp.swapaxes(down.reshape(2, BLK // 2, D), 1, 2)
    return pair[None], prefix[None], down, rise


def solution(mesh):
    row = P("grp", "seq", None, None)
    in_specs = (
        row, row, row, row, row, row, P(), P(),
        P("grp", "seq", None), P("grp", None, None), P("grp", None), P(), P(), P(), P(),
    )
    out_specs = (P("grp", "seq", None), P("grp", "seq", None), P(), P())
    return jax.shard_map(
        on_device, mesh=mesh, in_specs=in_specs, out_specs=out_specs, check_vma=False
    )
```

```python
import jax
import jax.numpy as jnp
from jax import lax
from jax.experimental import pallas as pl
from jax.experimental.pallas import tpu as pltpu
from jax.sharding import PartitionSpec as P

HEAD = 128
BLK = 128
NX = 4
SEQ = 16
GRP = 8
REP = 5
KV = 4
SPAN = 8
D = 5120
KVW = 512
DT = 640
TILE = 256
DEPTH = 144
TYPES = 3
W = REP * BLK
TREE = SEQ * BLK
GROUP = 4 * BLK
PAIR = 2 * HEAD
CHUNKS = ((0, 256), (256, 512), (512, 640))
MESH = pl.DeviceIdType.MESH
SCALE = HEAD ** (-0.5)
LOG2E = 1.4426950408889634
MASKED = -1e30
NT = (((1,), (1,)), ((), ()))
TN = (((0,), (0,)), ((), ()))
f32 = jnp.float32
bf16 = jnp.bfloat16


def vmem():
    return pl.BlockSpec(memory_space=pltpu.VMEM)


def hbm():
    return pl.BlockSpec(memory_space=pl.ANY)


def smem():
    return pl.BlockSpec(memory_space=pltpu.SMEM)


def remote(src, dst, send, recv, device):
    copy = pltpu.make_async_remote_copy(
        src_ref=src, dst_ref=dst, send_sem=send, recv_sem=recv, device_id=device, device_id_type=MESH
    )
    copy.start()
    return copy


def greet(devices):
    barrier = pltpu.get_barrier_semaphore()
    for device in devices:
        pl.semaphore_signal(barrier, inc=1, device_id=device, device_id_type=MESH)


def greeted(devices):
    pl.semaphore_wait(pltpu.get_barrier_semaphore(), len(devices))


def cols(i, width):
    return pl.ds(pl.multiple_of(i * width, 128), width)


def rows(i, count):
    return pl.ds(pl.multiple_of(i * count, count), count)


def kernel(
    mask, listed, q, g, saved, k, v, hidden, hidden_p, pool_k, pool_v, down_k, down_v, up_k, up_v,
    pair, prefix, out,
    q_in, g_in, delta_in, kv, own_g, own_s, own_h, own_p, down, pool, up, delta_out, all_g, back_all, back_t, proj_all, proj_t,
    s_ref, acc, qs, gs, pb, dsb, stat, diag,
    tsend, rt, proj_s, proj_r, pt, rp, rq, back_s, back_r,
    s0, r0, s1, r1, s2, r2, full, own_x,
    sem_in, kvx_s, kvx_r, kvy_s, kvy_r, q_s, q_r, t_s, t_r, j_s, j_r, b_s, b_r, p_s, p_r,
    s0_s, s0_r, s1_s, s1_r, s2_s, s2_r, a2_s, a2_r, a1_s, a1_r, a0_s, a0_r,
):
    me, grp = lax.axis_index("seq"), lax.axis_index("grp")
    x, y = me // NX, lax.rem(me, NX)
    z, c = grp // 2, lax.rem(grp, 2)
    peers = [lax.rem(me + o, SEQ) for o in range(1, SEQ)]

    def at(xx, yy, zz):
        return {"seq": xx * NX + yy, "grp": zz * 2 + c}

    def line(t, i):
        n = [lax.rem(place + i, NX) for place in (z, x, y)]
        return (at(x, y, n[0]), at(n[1], y, z), at(x, n[2], z))[t]

    def plane(t, e):
        u, w = e // NX, lax.rem(e, NX)
        return (at(u, w, z), at(x, u, w), at(u, y, w))[t]

    on_line = (z, x, y)
    on_plane = (me, y * NX + z, x * NX + z)
    met = [{"grp": lax.rem(grp + i, GRP)} for i in range(1, GRP)]
    met += [{"seq": d} for d in peers]
    for i in range(1, NX):
        for j in range(1, NX):
            met.append(at(x, lax.rem(y + i, NX), lax.rem(z + j, NX)))
            met.append(at(lax.rem(x + i, NX), y, lax.rem(z + j, NX)))
    greet(met)

    def local(src, dst, i):
        copy = pltpu.make_async_copy(src, dst, sem_in.at[i])
        copy.start()
        return copy

    mine = rows(me, BLK)
    keep = [
        local(k.at[:, cols(x, HEAD)], kv.at[mine, 0:HEAD], 0),
        local(v.at[:, cols(x, HEAD)], kv.at[mine, HEAD:PAIR], 1),
        local(q.at[:, cols(x, DT)], q_in.at[x], 2),
        local(g.at[:, cols(x, DT)], g_in.at[x], 3),
        local(g, own_g, 4),
        local(saved, own_s, 5),
        local(hidden, own_h.at[0:BLK], 6),
        local(down_k, down.at[0:64], 7),
        local(down_v, down.at[64:128], 8),
        local(hidden_p, own_p, 9),
        local(pool_k.at[:, :, cols(x, HEAD)], pool.at[:, :, 0:HEAD], 10),
        local(pool_v.at[:, :, cols(x, HEAD)], pool.at[:, :, HEAD:PAIR], 11),
    ]
    keep[4].wait()
    keep[5].wait()
    ones = jnp.ones((8, HEAD), f32)
    for h in range(KV):
        for t in range(REP):
            cut = slice((h * REP + t) * HEAD, (h * REP + t + 1) * HEAD)
            prod = own_g[:, cut].astype(f32) * own_s[:, cut].astype(f32)
            delta_out[h, :, t * BLK : (t + 1) * BLK] = lax.dot_general(
                ones, prod, NT, preferred_element_type=f32, precision=lax.Precision.HIGHEST
            )
    delta_in[x] = delta_out[x]
    greeted(met)

    step_x, step_y, step_q, step_g = ([], []), ([], []), [], []

    def send_x(n, source, lanes):
        for i in range(1, NX):
            tx = lax.rem(x + i, NX)
            step_x[n].append(
                remote(
                    source.at[:, cols(tx, HEAD)], kv.at[mine, lanes], kvx_s.at[n, i], kvx_r.at[n, i],
                    {"seq": tx * NX + y},
                )
            )

    def send_y(n, k, lanes):
        block = rows(lax.rem(x + NX - k, NX) * NX + y, BLK)
        for i in range(1, NX):
            device = {"seq": x * NX + lax.rem(y + i, NX)}
            piece = kv.at[block, lanes]
            step_y[n].append(remote(piece, piece, kvy_s.at[n, k, i], kvy_r.at[n, k, i], device))

    def send_rows(n, source, target, steps):
        for i in range(1, NX):
            tx = lax.rem(x + i, NX)
            steps.append(
                remote(
                    source.at[:, cols(tx, DT)], target.at[x], q_s.at[n, i], q_r.at[n, i],
                    {"seq": tx * NX + y},
                )
            )

    key_lanes, value_lanes = slice(0, HEAD), slice(HEAD, PAIR)
    send_x(0, k, key_lanes)
    send_x(1, v, value_lanes)
    keep[0].wait()
    send_y(0, 0, key_lanes)
    keep[1].wait()
    send_y(1, 0, value_lanes)
    send_rows(0, q, q_in, step_q)
    for i in range(1, NX):
        tx = lax.rem(x + i, NX)
        device = {"seq": tx * NX + y}
        step_g.append(remote(delta_out.at[tx], delta_in.at[x], q_s.at[2, i], q_r.at[2, i], device))
    send_rows(1, g, g_in, step_g)
    for side, lanes in ((0, key_lanes), (1, value_lanes)):
        for n in (1, 3, 2):
            step_x[side][n - 1].wait_recv()
            send_y(side, n, lanes)

    for i in range(6, 10):
        keep[i].wait()
    own_h[BLK : BLK + SPAN, :] = own_p[...]
    own_h[BLK + SPAN : DEPTH, :] = jnp.zeros((SPAN, D), bf16)
    proj = lax.dot_general(own_h[...], down[...], NT, preferred_element_type=f32)
    proj_s[...] = proj[0:BLK].reshape(SEQ, SPAN, HEAD).astype(bf16)
    proj_all[BLK:DEPTH, :] = proj[BLK:DEPTH].astype(bf16)
    step_j = []
    for o, d in enumerate(peers):
        step_j.append(remote(proj_s.at[d], proj_r.at[me], j_s.at[o], j_r.at[o], {"seq": d}))
    proj_r[me] = proj_s[me]
    up[...] = jnp.zeros_like(up)
    up[0:64, 0:KVW] = up_k[...]
    up[64:128, KVW : 2 * KVW] = up_v[...]

    keep[10].wait()
    keep[11].wait()
    for i in range(2):
        kv[TREE + i * BLK : TREE + (i + 1) * BLK, :] = pool[listed[0, i]]
    acc[...] = jnp.zeros_like(acc)
    key_at = lax.broadcasted_iota(jnp.int32, (GROUP, BLK), 0)
    query_at = lax.broadcasted_iota(jnp.int32, (GROUP, BLK), 1)
    diag[...] = jnp.where(key_at <= y * BLK + query_at, 0.0, MASKED).astype(f32)
    keep[2].wait()
    for copy in step_q + step_y[0]:
        copy.wait_recv()

    def score_rows(kk):
        return 2 * BLK * kk * (kk + 2)

    def score_place(start, m):
        return pl.ds(pl.multiple_of(start + 2 * BLK + m * GROUP, 2 * BLK), GROUP)

    def ends_place(start):
        return pl.ds(pl.multiple_of(start, 2 * BLK), 2 * BLK)

    ends = slice(TREE, TREE + 2 * BLK)

    def scores(step, carry):
        kk = NX - 1 - step
        r = y + NX * kk
        start = score_rows(kk)
        for t in range(REP):
            span = slice(t * BLK, (t + 1) * BLK)
            qs[kk, span, :] = q_in[kk, :, span]
        top = stat.at[0, kk]
        low = stat.at[1, kk]
        top[...] = jnp.full_like(top, MASKED)
        low[...] = jnp.zeros_like(low)

        def hides(m):
            return [(mask[r, m * 4 + b].astype(f32) - 1.0) * 1e30 for b in range(4)]

        def score(place, into, hidden_by, diagonal, n):
            for lo, hi in CHUNKS:
                w = hi - lo
                s = lax.dot_general(kv[place, 0:HEAD], qs[kk, lo:hi, :], NT, preferred_element_type=f32)
                s = s * (SCALE * LOG2E)
                if diagonal:
                    s = s + jnp.concatenate([diag[...]] * (w // BLK), axis=1)
                s_ref[into, lo:hi] = s
                cut = s.reshape(n, BLK // 8, 8, w)
                before = top[:, lo:hi]
                now = before
                for b in range(n):
                    now = jnp.maximum(now, jnp.max(cut[b], axis=0) + hidden_by[b])
                part = low[:, lo:hi] * jnp.exp2(before - now)
                for b in range(n):
                    part += jnp.sum(jnp.exp2(cut[b] - (now - hidden_by[b])[None]), axis=0)
                low[:, lo:hi] = part
                top[:, lo:hi] = now

        def score_group(m, cc):
            score(rows(m, GROUP), score_place(start, m), hides(m), False, 4)
            return cc

        score(ends, ends_place(start), [0.0, 0.0], False, 2)
        lax.fori_loop(0, kk, score_group, 0)
        score(rows(kk, GROUP), score_place(start, kk), hides(kk), True, 4)
        best = jnp.max(top[...], axis=0, keepdims=True)
        total = jnp.sum(low[...] * jnp.exp2(top[...] - best), axis=0, keepdims=True)
        top[...] = jnp.broadcast_to(best + jnp.log2(total), (8, W))
        return carry

    lax.fori_loop(0, NX, scores, 0)
    keep[3].wait()
    for copy in step_g + step_y[1]:
        copy.wait_recv()

    def term(n, first_block, count, o):
        part = pl.ds(first_block, count)
        return pltpu.make_async_remote_copy(
            src_ref=tsend.at[peers[o], part], dst_ref=rt.at[me, part], send_sem=t_s.at[n, o],
            recv_sem=t_r.at[n, o], device_id={"seq": peers[o]}, device_id_type=MESH,
        )

    def rollout(step, carry):
        kk = NX - 1 - step
        r = y + NX * kk
        start = score_rows(kk)
        for t in range(REP):
            span = slice(t * BLK, (t + 1) * BLK)
            gs[span, :] = g_in[kk, :, span]
        top = stat.at[0, kk]
        low = delta_in.at[kk]

        def hides(m):
            return [(mask[r, m * 4 + b].astype(f32) - 1.0) * 1e30 for b in range(4)]

        def grads(place, into, hidden_by, n):
            for lo, hi in CHUNKS:
                w = hi - lo
                dp = lax.dot_general(kv[place, HEAD:PAIR], gs[lo:hi, :], NT, preferred_element_type=f32)
                dp = dp.reshape(n, BLK // 8, 8, w)
                cut = s_ref[into, lo:hi].reshape(n, BLK // 8, 8, w)
                for b in range(n):
                    span = slice(b * BLK, (b + 1) * BLK)
                    p = jnp.exp2(cut[b] - (top[:, lo:hi] - hidden_by[b])[None])
                    ds = p * (dp[b] - low[:, lo:hi][None])
                    pb[span, lo:hi] = p.reshape(BLK, w).astype(bf16)
                    dsb[span, lo:hi] = ds.reshape(BLK, w).astype(bf16)
            acc[place, 0:HEAD] += jnp.dot(dsb[0 : n * BLK, :], qs[kk], preferred_element_type=f32)
            acc[place, HEAD:PAIR] += jnp.dot(pb[0 : n * BLK, :], gs[...], preferred_element_type=f32)

        def grads_group(m, cc):
            grads(rows(m, GROUP), score_place(start, m), hides(m), 4)
            return cc

        grads(ends, ends_place(start), [0.0, 0.0], 2)

        @pl.when(step == NX - 1)
        def _():
            for i in range(2):
                part = acc[TREE + i * BLK : TREE + (i + 1) * BLK, :].reshape(SEQ, SPAN, PAIR)
                tsend[:, SEQ + i, :, 0:HEAD] = (part[:, :, 0:HEAD] * SCALE).astype(bf16)
                tsend[:, SEQ + i, :, HEAD:PAIR] = part[:, :, HEAD:PAIR].astype(bf16)
            for o in range(SEQ - 1):
                term(4, SEQ, 2, o).start()

        grads_group(kk, 0)
        for b in range(4):
            j = kk * 4 + b
            part = acc[rows(j, BLK), :].reshape(SEQ, SPAN, PAIR)
            tsend[:, j, :, 0:HEAD] = (part[:, :, 0:HEAD] * SCALE).astype(bf16)
            tsend[:, j, :, HEAD:PAIR] = part[:, :, HEAD:PAIR].astype(bf16)
        for o in range(SEQ - 1):
            term(kk, kk * 4, 4, o).start()
        lax.fori_loop(0, kk, grads_group, 0)
        return carry

    lax.fori_loop(0, NX, rollout, 0)
    step_e = [term(4, SEQ, 2, o) for o in range(SEQ - 1)]
    step_t = [term(kk, kk * 4, 4, o) for kk in range(NX) for o in range(SEQ - 1)]
    rt[me] = tsend[me]
    step_b = [
        pltpu.make_async_remote_copy(
            src_ref=back_s.at[peers[o]], dst_ref=back_r.at[me], send_sem=b_s.at[o], recv_sem=b_r.at[o],
            device_id={"seq": peers[o]}, device_id_type=MESH,
        )
        for o in range(SEQ - 1)
    ]

    def finish(m):
        for copy in step_t[m * 15 : m * 15 + 15]:
            copy.wait_recv()
        span = slice(m * 32, m * 32 + 32)
        for h in range(KV):
            for side in range(2):
                lanes = slice(side * HEAD, (side + 1) * HEAD)
                place = slice(side * KVW + h * HEAD, side * KVW + (h + 1) * HEAD)
                total = rt[NX * h, 4 * m : 4 * m + 4, :, lanes].astype(f32)
                for a in range(1, NX):
                    total += rt[NX * h + a, 4 * m : 4 * m + 4, :, lanes].astype(f32)
                all_g[span, place] = total.reshape(32, HEAD).astype(bf16)
        back = lax.dot_general(all_g[span, :], up[...], NT, preferred_element_type=f32)
        back_s[4 * m : 4 * m + 4] = back.reshape(4, SPAN, HEAD).astype(bf16)
        for j in range(4 * m, 4 * m + 4):

            @pl.when(me != j)
            def _():
                o = lax.rem(j - me + 2 * SEQ - 1, SEQ)
                remote(back_s.at[j], back_r.at[me], b_s.at[o], b_r.at[o], {"seq": j})

    for m in (3, 2, 1):
        finish(m)
    for copy in step_e:
        copy.wait_recv()
    for h in range(KV):
        for side in range(2):
            lanes = slice(side * HEAD, (side + 1) * HEAD)
            place = slice(side * KVW + h * HEAD, side * KVW + (h + 1) * HEAD)
            for i in range(2):
                part = rt[NX * h, SEQ + i, :, lanes].astype(f32)
                for a in range(1, NX):
                    part += rt[NX * h + a, SEQ + i, :, lanes].astype(f32)
                rp[i, :, place] = part
    for b in range(GRP):
        part = rp[0] * (listed[0, 0] == b).astype(f32) + rp[1] * (listed[0, 1] == b).astype(f32)
        pt[b] = part.astype(bf16)
    step_p = []
    for i in range(1, GRP):
        b = lax.rem(grp + i, GRP)
        step_p.append(remote(pt.at[b], rq.at[i], p_s.at[i], p_r.at[i], {"grp": b}))
    finish(0)
    back_r[me] = back_s[me]
    for copy in step_p:
        copy.wait_recv()
    total = pt[grp].astype(f32)
    for i in range(1, GRP):
        total += rq[i].astype(f32)
    own_x[...] = total
    keep.append(local(own_x, prefix, 12))
    tail = jnp.concatenate([total, jnp.zeros_like(total)], axis=0).astype(bf16)
    all_g[BLK:DEPTH, :] = tail
    back_all[BLK:DEPTH, :] = lax.dot_general(tail, up[...], NT, preferred_element_type=f32).astype(bf16)
    keep.append(local(all_g.at[0:BLK], pair, 13))
    for copy in step_j:
        copy.wait_recv()
    proj_all[0:BLK, :] = proj_r[...].reshape(BLK, HEAD)
    same = lax.broadcasted_iota(jnp.int32, (HEAD, HEAD), 0) == lax.broadcasted_iota(jnp.int32, (HEAD, HEAD), 1)
    eye = same.astype(f32).astype(bf16)
    proj_t[...] = lax.dot_general(eye, proj_all[...], NT, preferred_element_type=f32).astype(bf16)
    for a in range(NX):
        cut = slice(a * TILE, (a + 1) * TILE)
        s0[1, 2, a] = jnp.dot(proj_t[...], all_g[:, cut], preferred_element_type=f32).astype(bf16)
    for copy in step_b:
        copy.wait_recv()

    back_all[0:BLK, :] = back_r[...].reshape(BLK, HEAD)
    back_t[...] = lax.dot_general(eye, back_all[...], NT, preferred_element_type=f32).astype(bf16)
    sibling = {"grp": grp + 1 - 2 * c}
    zero, first, second, third, fourth, fifth = [], [], [], [], [], []

    def down_terms(half, t):
        for a in range(NX):
            cut = cols((half * TYPES + t) * NX + a, TILE)
            s0[half, t, a] = jnp.dot(back_t[...], own_h[:, cut], preferred_element_type=f32).astype(bf16)

    for t in range(TYPES):
        if t < 2:
            down_terms(1 - c, t)
        else:
            down_terms(0, t)
        zero.append(remote(s0.at[1 - c, t], r0.at[t], s0_s.at[t], s0_r.at[t], sibling))
    for t in range(2):
        down_terms(c, t)
    for t in range(TYPES):
        zero[t].wait_recv()
        for a in range(NX):
            s1[t, a] = (s0[c, t, a].astype(f32) + r0[t, a].astype(f32)).astype(bf16)
        for i in range(1, NX):
            there = lax.rem(on_line[t] + i, NX)
            first.append(remote(s1.at[t, there], r1.at[t, i - 1], s1_s.at[t, i], s1_r.at[t, i], line(t, i)))
    for t in range(TYPES):
        for copy in first[t * 3 : t * 3 + 3]:
            copy.wait_recv()
        total = s1[t, on_line[t]].astype(f32)
        for i in range(NX - 1):
            total += r1[t, i].astype(f32)
        s2[t] = total.reshape(SEQ, SPAN, TILE).astype(bf16)
        for o in range(SEQ - 1):
            e = lax.rem(on_plane[t] + o + 1, SEQ)
            second.append(remote(s2.at[t, e], r2.at[t, o], s2_s.at[t, o], s2_r.at[t, o], plane(t, e)))
    for t in range(TYPES):
        for copy in second[t * 15 : t * 15 + 15]:
            copy.wait_recv()
        total = s2[t, on_plane[t]].astype(f32)
        for o in range(SEQ - 1):
            total += r2[t, o].astype(f32)
        full[t, on_line[t], on_plane[t]] = total.astype(bf16)
        piece = full.at[t, on_line[t], on_plane[t]]
        for o in range(SEQ - 1):
            e = lax.rem(on_plane[t] + o + 1, SEQ)
            third.append(remote(piece, piece, a2_s.at[t, o], a2_r.at[t, o], plane(t, e)))
    for t in range(TYPES):
        for copy in third[t * 15 : t * 15 + 15]:
            copy.wait_recv()
        piece = full.at[t, on_line[t]]
        for i in range(1, NX):
            fourth.append(remote(piece, piece, a1_s.at[t, i], a1_r.at[t, i], line(t, i)))
    for t in range(TYPES):
        for copy in fourth[t * 3 : t * 3 + 3]:
            copy.wait_recv()
        fifth.append(remote(full.at[t], out.at[c, t], a0_s.at[t], a0_r.at[t], sibling))
        keep.append(local(full.at[t], out.at[c, t], 14 + t))
    for copy in fifth:
        copy.wait_recv()
    for copy in keep[12:]:
        copy.wait()

    for copy in (
        step_x[0] + step_x[1] + step_y[0] + step_y[1] + step_q + step_g + step_j + step_e + step_t + step_p + step_b
        + zero + first + second + third + fourth + fifth
    ):
        copy.wait_send()


def backward(*operands):
    dma = pltpu.SemaphoreType.DMA

    def low(*shape):
        return pltpu.VMEM(shape, bf16)

    def wide(*shape):
        return pltpu.VMEM(shape, f32)

    return pl.pallas_call(
        kernel,
        out_shape=(
            jax.ShapeDtypeStruct((BLK, 2 * KVW), bf16),
            jax.ShapeDtypeStruct((SPAN, 2 * KVW), f32),
            jax.ShapeDtypeStruct((2, TYPES, NX, SEQ, SPAN, TILE), bf16),
        ),
        in_specs=[smem()] * 2 + [hbm()] * 11 + [vmem()] * 2,
        out_specs=(hbm(),) * 3,
        scratch_shapes=[
            low(NX, BLK, DT), low(NX, BLK, DT), wide(NX, 8, W), low(TREE + 2 * BLK, PAIR),
            low(BLK, 4 * DT), low(BLK, 4 * DT), low(DEPTH, D), low(SPAN, D), low(HEAD, D),
            low(GRP, BLK, PAIR), low(HEAD, 2 * KVW), wide(KV, 8, W),
            low(DEPTH, 2 * KVW), low(DEPTH, HEAD), low(HEAD, DEPTH), low(DEPTH, HEAD), low(HEAD, DEPTH),
            wide(2 * BLK * NX * (NX + 2), W), wide(TREE + 2 * BLK, PAIR), low(NX, W, HEAD), low(W, HEAD),
            low(GROUP, W), low(GROUP, W), wide(2, NX, 8, W), wide(GROUP, BLK),
            low(SEQ, SEQ + 2, SPAN, PAIR), low(SEQ, SEQ + 2, SPAN, PAIR),
            low(SEQ, SPAN, HEAD), low(SEQ, SPAN, HEAD),
            low(GRP, SPAN, 2 * KVW), wide(2, SPAN, 2 * KVW), low(GRP, SPAN, 2 * KVW),
            low(SEQ, SPAN, HEAD), low(SEQ, SPAN, HEAD),
            low(2, TYPES, NX, BLK, TILE), low(TYPES, NX, BLK, TILE), low(TYPES, NX, BLK, TILE),
            low(TYPES, NX - 1, BLK, TILE), low(TYPES, SEQ, SPAN, TILE), low(TYPES, SEQ - 1, SPAN, TILE),
            low(TYPES, NX, SEQ, SPAN, TILE), wide(SPAN, 2 * KVW),
            dma((17,)),
            dma((2, NX)), dma((2, NX)), dma((2, NX, NX)), dma((2, NX, NX)), dma((3, NX)), dma((3, NX)),
            dma((5, SEQ)), dma((5, SEQ)), dma((SEQ,)), dma((SEQ,)), dma((SEQ,)), dma((SEQ,)),
            dma((GRP,)), dma((GRP,)),
            dma((TYPES,)), dma((TYPES,)), dma((TYPES, NX)), dma((TYPES, NX)),
            dma((TYPES, SEQ)), dma((TYPES, SEQ)), dma((TYPES, SEQ)), dma((TYPES, SEQ)),
            dma((TYPES, NX)), dma((TYPES, NX)), dma((TYPES,)), dma((TYPES,)),
        ],
        compiler_params=pltpu.CompilerParams(
            collective_id=0, has_side_effects=True, vmem_limit_bytes=56 * 2**20
        ),
        name="backward",
    )(*operands)


def spread_kernel(summed, pair, prefix, down, rise, pair_out, prefix_out, got, made, risen, pair_got, prefix_got, sem_got, sem_made):
    factor = 2.0 / (GRP * SEQ)
    arrive = [pltpu.make_async_copy(summed.at[i], got.at[i], sem_got.at[i]) for i in range(2 * TYPES)]
    through = [
        pltpu.make_async_copy(pair, pair_got, sem_got.at[6]),
        pltpu.make_async_copy(prefix, prefix_got, sem_got.at[7]),
    ]
    for copy in arrive + through:
        copy.start()
    leave = []
    for i in range(2 * TYPES):
        arrive[i].wait()
        for a in range(NX):
            part = got[i, a].reshape(BLK, TILE).astype(f32) * factor
            if i < 5:
                made[i, :, a * TILE : (a + 1) * TILE] = part
            else:
                side = a // 2
                risen[side, :, (a % 2) * TILE : (a % 2 + 1) * TILE] = part[side * 64 : side * 64 + 64]
        if i < 5:
            for half in range(2):
                cut = slice(half * 64, half * 64 + 64)
                leave.append(
                    pltpu.make_async_copy(
                        made.at[i, cut], down.at[cut, i * NX * TILE : (i + 1) * NX * TILE],
                        sem_made.at[2 + 2 * i + half],
                    )
                )
                leave[-1].start()
        else:
            leave.append(pltpu.make_async_copy(risen, rise, sem_made.at[12]))
            leave[-1].start()
    for i, (source, target) in enumerate(((pair_got, pair_out), (prefix_got, prefix_out))):
        through[i].wait()
        leave.append(pltpu.make_async_copy(source, target, sem_made.at[i]))
        leave[-1].start()
    for copy in leave:
        copy.wait()


def spread(summed, pair, prefix):
    return pl.pallas_call(
        spread_kernel,
        out_shape=(
            jax.ShapeDtypeStruct((BLK, D), f32),
            jax.ShapeDtypeStruct((2, 64, KVW), f32),
            jax.ShapeDtypeStruct((BLK, 2 * KVW), bf16),
            jax.ShapeDtypeStruct((SPAN, 2 * KVW), f32),
        ),
        in_specs=[hbm()] * 3,
        out_specs=(hbm(),) * 4,
        scratch_shapes=[
            pltpu.VMEM((2 * TYPES, NX, SEQ, SPAN, TILE), bf16),
            pltpu.VMEM((5, BLK, NX * TILE), f32),
            pltpu.VMEM((2, 64, KVW), f32),
            pltpu.VMEM((BLK, 2 * KVW), bf16),
            pltpu.VMEM((SPAN, 2 * KVW), f32),
            pltpu.SemaphoreType.DMA((2 * TYPES + 2,)),
            pltpu.SemaphoreType.DMA((13,)),
        ],
        compiler_params=pltpu.CompilerParams(vmem_limit_bytes=60 * 2**20),
        name="spread",
    )(summed.reshape(2 * TYPES, NX, SEQ, SPAN, TILE), pair, prefix)


def on_device(
    queries, out_grad, saved_output, key_rows, value_rows, hidden_rows, prefix_keys, prefix_values,
    prefix_hidden, block_mask, prefix_list, key_down, value_down, key_up, value_up,
):
    pair, prefix, summed = backward(
        block_mask[0], prefix_list, queries[0, 0], out_grad[0, 0], saved_output[0, 0],
        key_rows[0, 0], value_rows[0, 0], hidden_rows[0, 0], prefix_hidden[0],
        prefix_keys, prefix_values, key_down.T, value_down.T, key_up, value_up,
    )
    down, rise, pair, prefix = spread(summed, pair, prefix)
    down = jnp.swapaxes(down.reshape(2, BLK // 2, D), 1, 2)
    return pair[None], prefix[None], down, rise


def solution(mesh):
    row = P("grp", "seq", None, None)
    in_specs = (
        row, row, row, row, row, row, P(), P(),
        P("grp", "seq", None), P("grp", None, None), P("grp", None), P(), P(), P(), P(),
    )
    out_specs = (P("grp", "seq", None), P("grp", "seq", None), P(), P())
    return jax.shard_map(
        on_device, mesh=mesh, in_specs=in_specs, out_specs=out_specs, check_vma=False
    )
```

```python
import jax
import jax.numpy as jnp
from jax import lax
from jax.experimental import pallas as pl
from jax.experimental.pallas import tpu as pltpu
from jax.sharding import PartitionSpec as P

HEAD = 128
BLK = 128
NX = 4
SEQ = 16
GRP = 8
REP = 5
KV = 4
SPAN = 8
D = 5120
KVW = 512
DT = 640
TILE = 256
DEPTH = 144
TYPES = 3
W = REP * BLK
TREE = SEQ * BLK
GROUP = 4 * BLK
PAIR = 2 * HEAD
CHUNKS = ((0, 256), (256, 512), (512, 640))
MESH = pl.DeviceIdType.MESH
SCALE = HEAD ** (-0.5)
LOG2E = 1.4426950408889634
MASKED = -1e30
NT = (((1,), (1,)), ((), ()))
TN = (((0,), (0,)), ((), ()))
f32 = jnp.float32
bf16 = jnp.bfloat16


def vmem():
    return pl.BlockSpec(memory_space=pltpu.VMEM)


def hbm():
    return pl.BlockSpec(memory_space=pl.ANY)


def smem():
    return pl.BlockSpec(memory_space=pltpu.SMEM)


def remote(src, dst, send, recv, device):
    copy = pltpu.make_async_remote_copy(
        src_ref=src, dst_ref=dst, send_sem=send, recv_sem=recv, device_id=device, device_id_type=MESH
    )
    copy.start()
    return copy


def greet(devices):
    barrier = pltpu.get_barrier_semaphore()
    for device in devices:
        pl.semaphore_signal(barrier, inc=1, device_id=device, device_id_type=MESH)


def greeted(devices):
    pl.semaphore_wait(pltpu.get_barrier_semaphore(), len(devices))


def cols(i, width):
    return pl.ds(pl.multiple_of(i * width, 128), width)


def rows(i, count):
    return pl.ds(pl.multiple_of(i * count, count), count)


def kernel(
    mask, listed, q, g, saved, k, v, hidden, hidden_p, pool_k, pool_v, down_k, down_v, up_k, up_v,
    pair, prefix, out,
    q_in, g_in, delta_in, kv, own_g, own_s, own_h, own_p, down, pool, up, delta_out, all_g, back_all, back_t, proj_all, proj_t,
    s_ref, acc, qs, gs, pb, dsb, stat, diag,
    tsend, rt, proj_s, proj_r, pt, rp, back_s, back_r,
    s0, r0, s1, r1, s2, r2, full, own_x,
    sem_in, kvx_s, kvx_r, kvy_s, kvy_r, q_s, q_r, t_s, t_r, j_s, j_r, b_s, b_r, p_s, p_r,
    s0_s, s0_r, s1_s, s1_r, s2_s, s2_r, a2_s, a2_r, a1_s, a1_r, a0_s, a0_r,
):
    me, grp = lax.axis_index("seq"), lax.axis_index("grp")
    x, y = me // NX, lax.rem(me, NX)
    z, c = grp // 2, lax.rem(grp, 2)
    peers = [lax.rem(me + o, SEQ) for o in range(1, SEQ)]

    def at(xx, yy, zz):
        return {"seq": xx * NX + yy, "grp": zz * 2 + c}

    def line(t, i):
        n = [lax.rem(place + i, NX) for place in (z, x, y)]
        return (at(x, y, n[0]), at(n[1], y, z), at(x, n[2], z))[t]

    def plane(t, e):
        u, w = e // NX, lax.rem(e, NX)
        return (at(u, w, z), at(x, u, w), at(u, y, w))[t]

    on_line = (z, x, y)
    on_plane = (me, y * NX + z, x * NX + z)
    met = [{"grp": lax.rem(grp + i, GRP)} for i in range(1, GRP)]
    met += [{"seq": d} for d in peers]
    for i in range(1, NX):
        for j in range(1, NX):
            met.append(at(x, lax.rem(y + i, NX), lax.rem(z + j, NX)))
            met.append(at(lax.rem(x + i, NX), y, lax.rem(z + j, NX)))
    greet(met)

    def local(src, dst, i):
        copy = pltpu.make_async_copy(src, dst, sem_in.at[i])
        copy.start()
        return copy

    mine = rows(me, BLK)
    keep = [
        local(k.at[:, cols(x, HEAD)], kv.at[mine, 0:HEAD], 0),
        local(v.at[:, cols(x, HEAD)], kv.at[mine, HEAD:PAIR], 1),
        local(q.at[:, cols(x, DT)], q_in.at[x], 2),
        local(g.at[:, cols(x, DT)], g_in.at[x], 3),
        local(g, own_g, 4),
        local(saved, own_s, 5),
        local(hidden, own_h.at[0:BLK], 6),
        local(down_k, down.at[0:64], 7),
        local(down_v, down.at[64:128], 8),
        local(hidden_p, own_p, 9),
        local(pool_k.at[:, :, cols(x, HEAD)], pool.at[:, :, 0:HEAD], 10),
        local(pool_v.at[:, :, cols(x, HEAD)], pool.at[:, :, HEAD:PAIR], 11),
    ]
    keep[4].wait()
    keep[5].wait()
    ones = jnp.ones((8, HEAD), f32)
    for h in range(KV):
        for t in range(REP):
            cut = slice((h * REP + t) * HEAD, (h * REP + t + 1) * HEAD)
            prod = own_g[:, cut].astype(f32) * own_s[:, cut].astype(f32)
            delta_out[h, :, t * BLK : (t + 1) * BLK] = lax.dot_general(
                ones, prod, NT, preferred_element_type=f32, precision=lax.Precision.HIGHEST
            )
    delta_in[x] = delta_out[x]
    greeted(met)

    step_x, step_y, step_q, step_g = ([], []), ([], []), [], []

    def send_x(n, source, lanes):
        for i in range(1, NX):
            tx = lax.rem(x + i, NX)
            step_x[n].append(
                remote(
                    source.at[:, cols(tx, HEAD)], kv.at[mine, lanes], kvx_s.at[n, i], kvx_r.at[n, i],
                    {"seq": tx * NX + y},
                )
            )

    def send_y(n, k, lanes):
        block = rows(lax.rem(x + NX - k, NX) * NX + y, BLK)
        for i in range(1, NX):
            device = {"seq": x * NX + lax.rem(y + i, NX)}
            piece = kv.at[block, lanes]
            step_y[n].append(remote(piece, piece, kvy_s.at[n, k, i], kvy_r.at[n, k, i], device))

    def send_rows(n, source, target, steps):
        for i in range(1, NX):
            tx = lax.rem(x + i, NX)
            steps.append(
                remote(
                    source.at[:, cols(tx, DT)], target.at[x], q_s.at[n, i], q_r.at[n, i],
                    {"seq": tx * NX + y},
                )
            )

    key_lanes, value_lanes = slice(0, HEAD), slice(HEAD, PAIR)
    send_x(0, k, key_lanes)
    send_x(1, v, value_lanes)
    keep[0].wait()
    send_y(0, 0, key_lanes)
    keep[1].wait()
    send_y(1, 0, value_lanes)
    send_rows(0, q, q_in, step_q)
    for i in range(1, NX):
        tx = lax.rem(x + i, NX)
        device = {"seq": tx * NX + y}
        step_g.append(remote(delta_out.at[tx], delta_in.at[x], q_s.at[2, i], q_r.at[2, i], device))
    send_rows(1, g, g_in, step_g)
    for side, lanes in ((0, key_lanes), (1, value_lanes)):
        for n in (1, 3, 2):
            step_x[side][n - 1].wait_recv()
            send_y(side, n, lanes)

    for i in range(6, 10):
        keep[i].wait()
    own_h[BLK : BLK + SPAN, :] = own_p[...]
    own_h[BLK + SPAN : DEPTH, :] = jnp.zeros((SPAN, D), bf16)
    proj = lax.dot_general(own_h[...], down[...], NT, preferred_element_type=f32)
    proj_s[...] = proj[0:BLK].reshape(SEQ, SPAN, HEAD).astype(bf16)
    proj_all[BLK:DEPTH, :] = proj[BLK:DEPTH].astype(bf16)
    step_j = []
    for o, d in enumerate(peers):
        step_j.append(remote(proj_s.at[d], proj_r.at[me], j_s.at[o], j_r.at[o], {"seq": d}))
    proj_r[me] = proj_s[me]
    up[...] = jnp.zeros_like(up)
    up[0:64, 0:KVW] = up_k[...]
    up[64:128, KVW : 2 * KVW] = up_v[...]

    keep[10].wait()
    keep[11].wait()
    for i in range(2):
        kv[TREE + i * BLK : TREE + (i + 1) * BLK, :] = pool[listed[0, i]]
    acc[...] = jnp.zeros_like(acc)
    key_at = lax.broadcasted_iota(jnp.int32, (GROUP, BLK), 0)
    query_at = lax.broadcasted_iota(jnp.int32, (GROUP, BLK), 1)
    diag[...] = jnp.where(key_at <= y * BLK + query_at, 0.0, MASKED).astype(f32)
    keep[2].wait()
    for copy in step_y[0]:
        copy.wait_recv()

    def score_rows(kk):
        return 2 * BLK * kk * (kk + 2)

    def score_place(start, m):
        return pl.ds(pl.multiple_of(start + 2 * BLK + m * GROUP, 2 * BLK), GROUP)

    def ends_place(start):
        return pl.ds(pl.multiple_of(start, 2 * BLK), 2 * BLK)

    ends = slice(TREE, TREE + 2 * BLK)

    def scores(step, carry):
        off = step + step // 2 * (1 - 2 * lax.rem(step, 2))
        kk = lax.rem(x + NX - off, NX)

        @pl.when(step > 0)
        def _():
            pltpu.make_async_remote_copy(
                src_ref=q.at[:, 0:DT], dst_ref=q_in.at[kk], send_sem=q_s.at[0, off], recv_sem=q_r.at[0, off],
                device_id={"seq": lax.rem(x + off, NX) * NX + y}, device_id_type=MESH,
            ).wait_recv()

        r = y + NX * kk
        start = score_rows(kk)
        for t in range(REP):
            span = slice(t * BLK, (t + 1) * BLK)
            qs[kk, span, :] = q_in[kk, :, span]
        top = stat.at[0, kk]
        low = stat.at[1, kk]
        top[...] = jnp.full_like(top, MASKED)
        low[...] = jnp.zeros_like(low)

        def hides(m):
            return [(mask[r, m * 4 + b].astype(f32) - 1.0) * 1e30 for b in range(4)]

        def score(place, into, hidden_by, diagonal, n):
            for lo, hi in CHUNKS:
                w = hi - lo
                s = lax.dot_general(kv[place, 0:HEAD], qs[kk, lo:hi, :], NT, preferred_element_type=f32)
                s = s * (SCALE * LOG2E)
                if diagonal:
                    s = s + jnp.concatenate([diag[...]] * (w // BLK), axis=1)
                s_ref[into, lo:hi] = s
                cut = s.reshape(n, BLK // 8, 8, w)
                before = top[:, lo:hi]
                now = before
                for b in range(n):
                    now = jnp.maximum(now, jnp.max(cut[b], axis=0) + hidden_by[b])
                part = low[:, lo:hi] * jnp.exp2(before - now)
                for b in range(n):
                    part += jnp.sum(jnp.exp2(cut[b] - (now - hidden_by[b])[None]), axis=0)
                low[:, lo:hi] = part
                top[:, lo:hi] = now

        def score_group(m, cc):
            score(rows(m, GROUP), score_place(start, m), hides(m), False, 4)
            return cc

        score(ends, ends_place(start), [0.0, 0.0], False, 2)
        lax.fori_loop(0, kk, score_group, 0)
        score(rows(kk, GROUP), score_place(start, kk), hides(kk), True, 4)
        best = jnp.max(top[...], axis=0, keepdims=True)
        total = jnp.sum(low[...] * jnp.exp2(top[...] - best), axis=0, keepdims=True)
        top[...] = jnp.broadcast_to(best + jnp.log2(total), (8, W))
        return carry

    lax.fori_loop(0, NX, scores, 0)
    keep[3].wait()
    for copy in step_g + step_y[1]:
        copy.wait_recv()

    def term(n, first_block, count, o):
        part = pl.ds(first_block, count)
        return pltpu.make_async_remote_copy(
            src_ref=tsend.at[peers[o], part], dst_ref=rt.at[me, part], send_sem=t_s.at[n, o],
            recv_sem=t_r.at[n, o], device_id={"seq": peers[o]}, device_id_type=MESH,
        )

    def rollout(step, carry):
        kk = NX - 1 - step
        r = y + NX * kk
        start = score_rows(kk)
        for t in range(REP):
            span = slice(t * BLK, (t + 1) * BLK)
            gs[span, :] = g_in[kk, :, span]
        top = stat.at[0, kk]
        low = delta_in.at[kk]

        def hides(m):
            return [(mask[r, m * 4 + b].astype(f32) - 1.0) * 1e30 for b in range(4)]

        def grads(place, into, hidden_by, n):
            for lo, hi in CHUNKS:
                w = hi - lo
                dp = lax.dot_general(kv[place, HEAD:PAIR], gs[lo:hi, :], NT, preferred_element_type=f32)
                dp = dp.reshape(n, BLK // 8, 8, w)
                cut = s_ref[into, lo:hi].reshape(n, BLK // 8, 8, w)
                for b in range(n):
                    span = slice(b * BLK, (b + 1) * BLK)
                    p = jnp.exp2(cut[b] - (top[:, lo:hi] - hidden_by[b])[None])
                    ds = p * (dp[b] - low[:, lo:hi][None])
                    pb[span, lo:hi] = p.reshape(BLK, w).astype(bf16)
                    dsb[span, lo:hi] = ds.reshape(BLK, w).astype(bf16)
            acc[place, 0:HEAD] += jnp.dot(dsb[0 : n * BLK, :], qs[kk], preferred_element_type=f32)
            acc[place, HEAD:PAIR] += jnp.dot(pb[0 : n * BLK, :], gs[...], preferred_element_type=f32)

        def grads_group(m, cc):
            grads(rows(m, GROUP), score_place(start, m), hides(m), 4)
            return cc

        grads(ends, ends_place(start), [0.0, 0.0], 2)

        @pl.when(step == NX - 1)
        def _():
            for i in range(2):
                part = acc[TREE + i * BLK : TREE + (i + 1) * BLK, :].reshape(SEQ, SPAN, PAIR)
                tsend[:, SEQ + i, :, 0:HEAD] = (part[:, :, 0:HEAD] * SCALE).astype(bf16)
                tsend[:, SEQ + i, :, HEAD:PAIR] = part[:, :, HEAD:PAIR].astype(bf16)
            for o in range(SEQ - 1):
                term(4, SEQ, 2, o).start()

        grads_group(kk, 0)
        for b in range(4):
            j = kk * 4 + b
            part = acc[rows(j, BLK), :].reshape(SEQ, SPAN, PAIR)
            tsend[:, j, :, 0:HEAD] = (part[:, :, 0:HEAD] * SCALE).astype(bf16)
            tsend[:, j, :, HEAD:PAIR] = part[:, :, HEAD:PAIR].astype(bf16)
        for o in range(SEQ - 1):
            term(kk, kk * 4, 4, o).start()
        lax.fori_loop(0, kk, grads_group, 0)
        return carry

    lax.fori_loop(0, NX, rollout, 0)
    step_e = [term(4, SEQ, 2, o) for o in range(SEQ - 1)]
    step_t = [term(kk, kk * 4, 4, o) for kk in range(NX) for o in range(SEQ - 1)]
    rt[me] = tsend[me]
    step_b = [
        pltpu.make_async_remote_copy(
            src_ref=back_s.at[peers[o]], dst_ref=back_r.at[me], send_sem=b_s.at[o], recv_sem=b_r.at[o],
            device_id={"seq": peers[o]}, device_id_type=MESH,
        )
        for o in range(SEQ - 1)
    ]

    def finish(m):
        for copy in step_t[m * 15 : m * 15 + 15]:
            copy.wait_recv()
        span = slice(m * 32, m * 32 + 32)
        for h in range(KV):
            for side in range(2):
                lanes = slice(side * HEAD, (side + 1) * HEAD)
                place = slice(side * KVW + h * HEAD, side * KVW + (h + 1) * HEAD)
                total = rt[NX * h, 4 * m : 4 * m + 4, :, lanes].astype(f32)
                for a in range(1, NX):
                    total += rt[NX * h + a, 4 * m : 4 * m + 4, :, lanes].astype(f32)
                all_g[span, place] = total.reshape(32, HEAD).astype(bf16)
        back = lax.dot_general(all_g[span, :], up[...], NT, preferred_element_type=f32)
        back_s[4 * m : 4 * m + 4] = back.reshape(4, SPAN, HEAD).astype(bf16)
        for j in range(4 * m, 4 * m + 4):

            @pl.when(me != j)
            def _():
                o = lax.rem(j - me + 2 * SEQ - 1, SEQ)
                remote(back_s.at[j], back_r.at[me], b_s.at[o], b_r.at[o], {"seq": j})

    for m in (3, 2, 1):
        finish(m)
    for copy in step_e:
        copy.wait_recv()
    for h in range(KV):
        for side in range(2):
            lanes = slice(side * HEAD, (side + 1) * HEAD)
            place = slice(side * KVW + h * HEAD, side * KVW + (h + 1) * HEAD)
            for i in range(2):
                part = rt[NX * h, SEQ + i, :, lanes].astype(f32)
                for a in range(1, NX):
                    part += rt[NX * h + a, SEQ + i, :, lanes].astype(f32)
                rp[i, :, place] = part
    for b in range(GRP):
        pt[b] = rp[0] * (listed[0, 0] == b).astype(f32) + rp[1] * (listed[0, 1] == b).astype(f32)
    step_p = []
    for i in range(1, GRP):
        b = lax.rem(grp + i, GRP)
        step_p.append(remote(pt.at[b], rp.at[1 + i], p_s.at[i], p_r.at[i], {"grp": b}))
    finish(0)
    back_r[me] = back_s[me]
    for copy in step_p:
        copy.wait_recv()
    total = pt[grp]
    for i in range(1, GRP):
        total += rp[1 + i]
    own_x[...] = total
    keep.append(local(own_x, prefix, 12))
    tail = jnp.concatenate([total, jnp.zeros_like(total)], axis=0).astype(bf16)
    all_g[BLK:DEPTH, :] = tail
    back_all[BLK:DEPTH, :] = lax.dot_general(tail, up[...], NT, preferred_element_type=f32).astype(bf16)
    keep.append(local(all_g.at[0:BLK], pair, 13))
    for copy in step_j:
        copy.wait_recv()
    proj_all[0:BLK, :] = proj_r[...].reshape(BLK, HEAD)
    same = lax.broadcasted_iota(jnp.int32, (HEAD, HEAD), 0) == lax.broadcasted_iota(jnp.int32, (HEAD, HEAD), 1)
    eye = same.astype(f32).astype(bf16)
    proj_t[...] = lax.dot_general(eye, proj_all[...], NT, preferred_element_type=f32).astype(bf16)
    for a in range(NX):
        cut = slice(a * TILE, (a + 1) * TILE)
        s0[1, 2, a] = jnp.dot(proj_t[...], all_g[:, cut], preferred_element_type=f32).astype(bf16)
    for copy in step_b:
        copy.wait_recv()

    back_all[0:BLK, :] = back_r[...].reshape(BLK, HEAD)
    back_t[...] = lax.dot_general(eye, back_all[...], NT, preferred_element_type=f32).astype(bf16)
    sibling = {"grp": grp + 1 - 2 * c}
    zero, first, second, third, fourth, fifth = [], [], [], [], [], []
    for t in range(TYPES):
        for half in range(2):
            for a in range(NX):
                n = (half * TYPES + t) * NX + a
                if n < D // TILE:
                    cut = slice(n * TILE, (n + 1) * TILE)
                    part = jnp.dot(back_t[...], own_h[:, cut], preferred_element_type=f32)
                    s0[half, t, a] = part.astype(bf16)
        zero.append(remote(s0.at[1 - c, t], r0.at[t], s0_s.at[t], s0_r.at[t], sibling))
    for t in range(TYPES):
        zero[t].wait_recv()
        for a in range(NX):
            s1[t, a] = (s0[c, t, a].astype(f32) + r0[t, a].astype(f32)).astype(bf16)
        for i in range(1, NX):
            there = lax.rem(on_line[t] + i, NX)
            first.append(remote(s1.at[t, there], r1.at[t, i - 1], s1_s.at[t, i], s1_r.at[t, i], line(t, i)))
    for t in range(TYPES):
        for copy in first[t * 3 : t * 3 + 3]:
            copy.wait_recv()
        total = s1[t, on_line[t]].astype(f32)
        for i in range(NX - 1):
            total += r1[t, i].astype(f32)
        s2[t] = total.reshape(SEQ, SPAN, TILE).astype(bf16)
        for o in range(SEQ - 1):
            e = lax.rem(on_plane[t] + o + 1, SEQ)
            second.append(remote(s2.at[t, e], r2.at[t, o], s2_s.at[t, o], s2_r.at[t, o], plane(t, e)))
    for t in range(TYPES):
        for copy in second[t * 15 : t * 15 + 15]:
            copy.wait_recv()
        total = s2[t, on_plane[t]].astype(f32)
        for o in range(SEQ - 1):
            total += r2[t, o].astype(f32)
        full[t, on_line[t], on_plane[t]] = total.astype(bf16)
        piece = full.at[t, on_line[t], on_plane[t]]
        for o in range(SEQ - 1):
            e = lax.rem(on_plane[t] + o + 1, SEQ)
            third.append(remote(piece, piece, a2_s.at[t, o], a2_r.at[t, o], plane(t, e)))
    for t in range(TYPES):
        for copy in third[t * 15 : t * 15 + 15]:
            copy.wait_recv()
        piece = full.at[t, on_line[t]]
        for i in range(1, NX):
            fourth.append(remote(piece, piece, a1_s.at[t, i], a1_r.at[t, i], line(t, i)))
    for t in range(TYPES):
        for copy in fourth[t * 3 : t * 3 + 3]:
            copy.wait_recv()
        fifth.append(remote(full.at[t], out.at[c, t], a0_s.at[t], a0_r.at[t], sibling))
        keep.append(local(full.at[t], out.at[c, t], 14 + t))
    for copy in fifth:
        copy.wait_recv()
    for copy in keep[12:]:
        copy.wait()

    for copy in (
        step_x[0] + step_x[1] + step_y[0] + step_y[1] + step_q + step_g + step_j + step_e + step_t + step_p + step_b
        + zero + first + second + third + fourth + fifth
    ):
        copy.wait_send()


def backward(*operands):
    dma = pltpu.SemaphoreType.DMA

    def low(*shape):
        return pltpu.VMEM(shape, bf16)

    def wide(*shape):
        return pltpu.VMEM(shape, f32)

    return pl.pallas_call(
        kernel,
        out_shape=(
            jax.ShapeDtypeStruct((BLK, 2 * KVW), bf16),
            jax.ShapeDtypeStruct((SPAN, 2 * KVW), f32),
            jax.ShapeDtypeStruct((2, TYPES, NX, SEQ, SPAN, TILE), bf16),
        ),
        in_specs=[smem()] * 2 + [hbm()] * 11 + [vmem()] * 2,
        out_specs=(hbm(),) * 3,
        scratch_shapes=[
            low(NX, BLK, DT), low(NX, BLK, DT), wide(NX, 8, W), low(TREE + 2 * BLK, PAIR),
            low(BLK, 4 * DT), low(BLK, 4 * DT), low(DEPTH, D), low(SPAN, D), low(HEAD, D),
            low(GRP, BLK, PAIR), low(HEAD, 2 * KVW), wide(KV, 8, W),
            low(DEPTH, 2 * KVW), low(DEPTH, HEAD), low(HEAD, DEPTH), low(DEPTH, HEAD), low(HEAD, DEPTH),
            wide(2 * BLK * NX * (NX + 2), W), wide(TREE + 2 * BLK, PAIR), low(NX, W, HEAD), low(W, HEAD),
            low(GROUP, W), low(GROUP, W), wide(2, NX, 8, W), wide(GROUP, BLK),
            low(SEQ, SEQ + 2, SPAN, PAIR), low(SEQ, SEQ + 2, SPAN, PAIR),
            low(SEQ, SPAN, HEAD), low(SEQ, SPAN, HEAD),
            wide(GRP, SPAN, 2 * KVW), wide(GRP + 1, SPAN, 2 * KVW),
            low(SEQ, SPAN, HEAD), low(SEQ, SPAN, HEAD),
            low(2, TYPES, NX, BLK, TILE), low(TYPES, NX, BLK, TILE), low(TYPES, NX, BLK, TILE),
            low(TYPES, NX - 1, BLK, TILE), low(TYPES, SEQ, SPAN, TILE), low(TYPES, SEQ - 1, SPAN, TILE),
            low(TYPES, NX, SEQ, SPAN, TILE), wide(SPAN, 2 * KVW),
            dma((17,)),
            dma((2, NX)), dma((2, NX)), dma((2, NX, NX)), dma((2, NX, NX)), dma((3, NX)), dma((3, NX)),
            dma((5, SEQ)), dma((5, SEQ)), dma((SEQ,)), dma((SEQ,)), dma((SEQ,)), dma((SEQ,)),
            dma((GRP,)), dma((GRP,)),
            dma((TYPES,)), dma((TYPES,)), dma((TYPES, NX)), dma((TYPES, NX)),
            dma((TYPES, SEQ)), dma((TYPES, SEQ)), dma((TYPES, SEQ)), dma((TYPES, SEQ)),
            dma((TYPES, NX)), dma((TYPES, NX)), dma((TYPES,)), dma((TYPES,)),
        ],
        compiler_params=pltpu.CompilerParams(
            collective_id=0, has_side_effects=True, vmem_limit_bytes=56 * 2**20
        ),
        name="backward",
    )(*operands)


def spread_kernel(summed, pair, prefix, down, rise, pair_out, prefix_out, got, made, risen, pair_got, prefix_got, sem_got, sem_made):
    factor = 2.0 / (GRP * SEQ)
    arrive = [pltpu.make_async_copy(summed.at[i], got.at[i], sem_got.at[i]) for i in range(2 * TYPES)]
    through = [
        pltpu.make_async_copy(pair, pair_got, sem_got.at[6]),
        pltpu.make_async_copy(prefix, prefix_got, sem_got.at[7]),
    ]
    for copy in arrive + through:
        copy.start()
    leave = []
    for i in range(2 * TYPES):
        arrive[i].wait()
        for a in range(NX):
            part = got[i, a].reshape(BLK, TILE).astype(f32) * factor
            if i < 5:
                made[i, :, a * TILE : (a + 1) * TILE] = part
            else:
                side = a // 2
                risen[side, :, (a % 2) * TILE : (a % 2 + 1) * TILE] = part[side * 64 : side * 64 + 64]
        if i < 5:
            for half in range(2):
                cut = slice(half * 64, half * 64 + 64)
                leave.append(
                    pltpu.make_async_copy(
                        made.at[i, cut], down.at[cut, i * NX * TILE : (i + 1) * NX * TILE],
                        sem_made.at[2 + 2 * i + half],
                    )
                )
                leave[-1].start()
        else:
            leave.append(pltpu.make_async_copy(risen, rise, sem_made.at[12]))
            leave[-1].start()
    for i, (source, target) in enumerate(((pair_got, pair_out), (prefix_got, prefix_out))):
        through[i].wait()
        leave.append(pltpu.make_async_copy(source, target, sem_made.at[i]))
        leave[-1].start()
    for copy in leave:
        copy.wait()


def spread(summed, pair, prefix):
    return pl.pallas_call(
        spread_kernel,
        out_shape=(
            jax.ShapeDtypeStruct((BLK, D), f32),
            jax.ShapeDtypeStruct((2, 64, KVW), f32),
            jax.ShapeDtypeStruct((BLK, 2 * KVW), bf16),
            jax.ShapeDtypeStruct((SPAN, 2 * KVW), f32),
        ),
        in_specs=[hbm()] * 3,
        out_specs=(hbm(),) * 4,
        scratch_shapes=[
            pltpu.VMEM((2 * TYPES, NX, SEQ, SPAN, TILE), bf16),
            pltpu.VMEM((5, BLK, NX * TILE), f32),
            pltpu.VMEM((2, 64, KVW), f32),
            pltpu.VMEM((BLK, 2 * KVW), bf16),
            pltpu.VMEM((SPAN, 2 * KVW), f32),
            pltpu.SemaphoreType.DMA((2 * TYPES + 2,)),
            pltpu.SemaphoreType.DMA((13,)),
        ],
        compiler_params=pltpu.CompilerParams(vmem_limit_bytes=60 * 2**20),
        name="spread",
    )(summed.reshape(2 * TYPES, NX, SEQ, SPAN, TILE), pair, prefix)


def on_device(
    queries, out_grad, saved_output, key_rows, value_rows, hidden_rows, prefix_keys, prefix_values,
    prefix_hidden, block_mask, prefix_list, key_down, value_down, key_up, value_up,
):
    pair, prefix, summed = backward(
        block_mask[0], prefix_list, queries[0, 0], out_grad[0, 0], saved_output[0, 0],
        key_rows[0, 0], value_rows[0, 0], hidden_rows[0, 0], prefix_hidden[0],
        prefix_keys, prefix_values, key_down.T, value_down.T, key_up, value_up,
    )
    down, rise, pair, prefix = spread(summed, pair, prefix)
    down = jnp.swapaxes(down.reshape(2, BLK // 2, D), 1, 2)
    return pair[None], prefix[None], down, rise


def solution(mesh):
    row = P("grp", "seq", None, None)
    in_specs = (
        row, row, row, row, row, row, P(), P(),
        P("grp", "seq", None), P("grp", None, None), P("grp", None), P(), P(), P(), P(),
    )
    out_specs = (P("grp", "seq", None), P("grp", "seq", None), P(), P())
    return jax.shard_map(
        on_device, mesh=mesh, in_specs=in_specs, out_specs=out_specs, check_vma=False
    )
```

```python
import jax
import jax.numpy as jnp
from jax import lax
from jax.experimental import pallas as pl
from jax.experimental.pallas import tpu as pltpu
from jax.sharding import PartitionSpec as P

HEAD = 128
BLK = 128
NX = 4
SEQ = 16
GRP = 8
REP = 5
KV = 4
SPAN = 8
D = 5120
KVW = 512
DT = 640
TILE = 256
DEPTH = 144
TYPES = 3
W = REP * BLK
TREE = SEQ * BLK
GROUP = 4 * BLK
PAIR = 2 * HEAD
CHUNKS = ((0, 256), (256, 512), (512, 640))
MESH = pl.DeviceIdType.MESH
SCALE = HEAD ** (-0.5)
LOG2E = 1.4426950408889634
MASKED = -1e30
NT = (((1,), (1,)), ((), ()))
TN = (((0,), (0,)), ((), ()))
f32 = jnp.float32
bf16 = jnp.bfloat16


def vmem():
    return pl.BlockSpec(memory_space=pltpu.VMEM)


def hbm():
    return pl.BlockSpec(memory_space=pl.ANY)


def smem():
    return pl.BlockSpec(memory_space=pltpu.SMEM)


def remote(src, dst, send, recv, device):
    copy = pltpu.make_async_remote_copy(
        src_ref=src, dst_ref=dst, send_sem=send, recv_sem=recv, device_id=device, device_id_type=MESH
    )
    copy.start()
    return copy


def greet(devices):
    barrier = pltpu.get_barrier_semaphore()
    for device in devices:
        pl.semaphore_signal(barrier, inc=1, device_id=device, device_id_type=MESH)


def greeted(devices):
    pl.semaphore_wait(pltpu.get_barrier_semaphore(), len(devices))


def cols(i, width):
    return pl.ds(pl.multiple_of(i * width, 128), width)


def rows(i, count):
    return pl.ds(pl.multiple_of(i * count, count), count)


def kernel(
    mask, listed, q, g, saved, k, v, hidden, hidden_p, pool_k, pool_v, down_k, down_v, up_k, up_v,
    pair, prefix, out,
    q_in, g_in, delta_in, kv, own_g, own_s, own_h, own_p, down, pool, up, delta_out, all_g, back_all, back_t, proj_all, proj_t,
    s_ref, acc, qs, gs, pb, dsb, stat, diag,
    tsend, rt, proj_s, proj_r, pt, rp, rq, back_s, back_r,
    s0, r0, s1, r1, s2, r2, full, own_x,
    sem_in, kvx_s, kvx_r, kvy_s, kvy_r, q_s, q_r, t_s, t_r, j_s, j_r, b_s, b_r, p_s, p_r,
    s0_s, s0_r, s1_s, s1_r, s2_s, s2_r, a2_s, a2_r, a1_s, a1_r, a0_s, a0_r,
):
    me, grp = lax.axis_index("seq"), lax.axis_index("grp")
    x, y = me // NX, lax.rem(me, NX)
    z, c = grp // 2, lax.rem(grp, 2)
    peers = [lax.rem(me + o, SEQ) for o in range(1, SEQ)]

    def at(xx, yy, zz):
        return {"seq": xx * NX + yy, "grp": zz * 2 + c}

    def line(t, i):
        n = [lax.rem(place + i, NX) for place in (z, x, y)]
        return (at(x, y, n[0]), at(n[1], y, z), at(x, n[2], z))[t]

    def plane(t, e):
        u, w = e // NX, lax.rem(e, NX)
        return (at(u, w, z), at(x, u, w), at(u, y, w))[t]

    on_line = (z, x, y)
    on_plane = (me, y * NX + z, x * NX + z)
    met = [{"grp": lax.rem(grp + i, GRP)} for i in range(1, GRP)]
    met += [{"seq": d} for d in peers]
    for i in range(1, NX):
        for j in range(1, NX):
            met.append(at(x, lax.rem(y + i, NX), lax.rem(z + j, NX)))
            met.append(at(lax.rem(x + i, NX), y, lax.rem(z + j, NX)))
    greet(met)

    def local(src, dst, i):
        copy = pltpu.make_async_copy(src, dst, sem_in.at[i])
        copy.start()
        return copy

    mine = rows(me, BLK)
    keep = [
        local(k.at[:, cols(x, HEAD)], kv.at[mine, 0:HEAD], 0),
        local(v.at[:, cols(x, HEAD)], kv.at[mine, HEAD:PAIR], 1),
        local(q.at[:, cols(x, DT)], q_in.at[x], 2),
        local(g.at[:, cols(x, DT)], g_in.at[x], 3),
        local(g, own_g, 4),
        local(saved, own_s, 5),
        local(hidden, own_h.at[0:BLK], 6),
        local(down_k, down.at[0:64], 7),
        local(down_v, down.at[64:128], 8),
        local(hidden_p, own_p, 9),
        local(pool_k.at[:, :, cols(x, HEAD)], pool.at[:, :, 0:HEAD], 10),
        local(pool_v.at[:, :, cols(x, HEAD)], pool.at[:, :, HEAD:PAIR], 11),
    ]
    keep[4].wait()
    keep[5].wait()
    ones = jnp.ones((8, HEAD), f32)
    for h in range(KV):
        for t in range(REP):
            cut = slice((h * REP + t) * HEAD, (h * REP + t + 1) * HEAD)
            prod = own_g[:, cut].astype(f32) * own_s[:, cut].astype(f32)
            delta_out[h, :, t * BLK : (t + 1) * BLK] = lax.dot_general(
                ones, prod, NT, preferred_element_type=f32, precision=lax.Precision.HIGHEST
            )
    delta_in[x] = delta_out[x]
    greeted(met)

    step_x, step_y, step_q, step_g = ([], []), ([], []), [], []

    def send_x(n, source, lanes):
        for i in range(1, NX):
            tx = lax.rem(x + i, NX)
            step_x[n].append(
                remote(
                    source.at[:, cols(tx, HEAD)], kv.at[mine, lanes], kvx_s.at[n, i], kvx_r.at[n, i],
                    {"seq": tx * NX + y},
                )
            )

    def send_y(n, k, lanes):
        block = rows(lax.rem(x + NX - k, NX) * NX + y, BLK)
        for i in range(1, NX):
            device = {"seq": x * NX + lax.rem(y + i, NX)}
            piece = kv.at[block, lanes]
            step_y[n].append(remote(piece, piece, kvy_s.at[n, k, i], kvy_r.at[n, k, i], device))

    def send_rows(n, source, target, steps):
        for i in range(1, NX):
            tx = lax.rem(x + i, NX)
            steps.append(
                remote(
                    source.at[:, cols(tx, DT)], target.at[x], q_s.at[n, i], q_r.at[n, i],
                    {"seq": tx * NX + y},
                )
            )

    key_lanes, value_lanes = slice(0, HEAD), slice(HEAD, PAIR)
    send_x(0, k, key_lanes)
    send_x(1, v, value_lanes)
    keep[0].wait()
    send_y(0, 0, key_lanes)
    keep[1].wait()
    send_y(1, 0, value_lanes)
    send_rows(0, q, q_in, step_q)
    for i in range(1, NX):
        tx = lax.rem(x + i, NX)
        device = {"seq": tx * NX + y}
        step_g.append(remote(delta_out.at[tx], delta_in.at[x], q_s.at[2, i], q_r.at[2, i], device))
    send_rows(1, g, g_in, step_g)
    for side, lanes in ((0, key_lanes), (1, value_lanes)):
        for n in (1, 3, 2):
            step_x[side][n - 1].wait_recv()
            send_y(side, n, lanes)

    for i in range(6, 10):
        keep[i].wait()
    own_h[BLK : BLK + SPAN, :] = own_p[...]
    own_h[BLK + SPAN : DEPTH, :] = jnp.zeros((SPAN, D), bf16)
    proj = lax.dot_general(own_h[...], down[...], NT, preferred_element_type=f32)
    proj_s[...] = proj[0:BLK].reshape(SEQ, SPAN, HEAD).astype(bf16)
    proj_all[BLK:DEPTH, :] = proj[BLK:DEPTH].astype(bf16)
    step_j = []
    for o, d in enumerate(peers):
        step_j.append(remote(proj_s.at[d], proj_r.at[me], j_s.at[o], j_r.at[o], {"seq": d}))
    proj_r[me] = proj_s[me]
    up[...] = jnp.zeros_like(up)
    up[0:64, 0:KVW] = up_k[...]
    up[64:128, KVW : 2 * KVW] = up_v[...]

    keep[10].wait()
    keep[11].wait()
    for i in range(2):
        kv[TREE + i * BLK : TREE + (i + 1) * BLK, :] = pool[listed[0, i]]
    acc[...] = jnp.zeros_like(acc)
    key_at = lax.broadcasted_iota(jnp.int32, (GROUP, BLK), 0)
    query_at = lax.broadcasted_iota(jnp.int32, (GROUP, BLK), 1)
    diag[...] = jnp.where(key_at <= y * BLK + query_at, 0.0, MASKED).astype(f32)
    keep[2].wait()
    for copy in step_y[0]:
        copy.wait_recv()

    def score_rows(kk):
        return 2 * BLK * kk * (kk + 2)

    def score_place(start, m):
        return pl.ds(pl.multiple_of(start + 2 * BLK + m * GROUP, 2 * BLK), GROUP)

    def ends_place(start):
        return pl.ds(pl.multiple_of(start, 2 * BLK), 2 * BLK)

    ends = slice(TREE, TREE + 2 * BLK)

    def scores(step, carry):
        off = step + step // 2 * (1 - 2 * lax.rem(step, 2))
        kk = lax.rem(x + NX - off, NX)

        @pl.when(step > 0)
        def _():
            pltpu.make_async_remote_copy(
                src_ref=q.at[:, 0:DT], dst_ref=q_in.at[kk], send_sem=q_s.at[0, off], recv_sem=q_r.at[0, off],
                device_id={"seq": lax.rem(x + off, NX) * NX + y}, device_id_type=MESH,
            ).wait_recv()

        r = y + NX * kk
        start = score_rows(kk)
        for t in range(REP):
            span = slice(t * BLK, (t + 1) * BLK)
            qs[kk, span, :] = q_in[kk, :, span]
        top = stat.at[0, kk]
        low = stat.at[1, kk]
        top[...] = jnp.full_like(top, MASKED)
        low[...] = jnp.zeros_like(low)

        def hides(m):
            return [(mask[r, m * 4 + b].astype(f32) - 1.0) * 1e30 for b in range(4)]

        def score(place, into, hidden_by, diagonal, n):
            for lo, hi in CHUNKS:
                w = hi - lo
                s = lax.dot_general(kv[place, 0:HEAD], qs[kk, lo:hi, :], NT, preferred_element_type=f32)
                s = s * (SCALE * LOG2E)
                if diagonal:
                    s = s + jnp.concatenate([diag[...]] * (w // BLK), axis=1)
                s_ref[into, lo:hi] = s
                cut = s.reshape(n, BLK // 8, 8, w)
                before = top[:, lo:hi]
                now = before
                for b in range(n):
                    now = jnp.maximum(now, jnp.max(cut[b], axis=0) + hidden_by[b])
                part = low[:, lo:hi] * jnp.exp2(before - now)
                for b in range(n):
                    part += jnp.sum(jnp.exp2(cut[b] - (now - hidden_by[b])[None]), axis=0)
                low[:, lo:hi] = part
                top[:, lo:hi] = now

        def score_group(m, cc):
            score(rows(m, GROUP), score_place(start, m), hides(m), False, 4)
            return cc

        score(ends, ends_place(start), [0.0, 0.0], False, 2)
        lax.fori_loop(0, kk, score_group, 0)
        score(rows(kk, GROUP), score_place(start, kk), hides(kk), True, 4)
        best = jnp.max(top[...], axis=0, keepdims=True)
        total = jnp.sum(low[...] * jnp.exp2(top[...] - best), axis=0, keepdims=True)
        top[...] = jnp.broadcast_to(best + jnp.log2(total), (8, W))
        return carry

    lax.fori_loop(0, NX, scores, 0)
    keep[3].wait()
    for copy in step_g + step_y[1]:
        copy.wait_recv()

    def term(n, first_block, count, o):
        part = pl.ds(first_block, count)
        return pltpu.make_async_remote_copy(
            src_ref=tsend.at[peers[o], part], dst_ref=rt.at[me, part], send_sem=t_s.at[n, o],
            recv_sem=t_r.at[n, o], device_id={"seq": peers[o]}, device_id_type=MESH,
        )

    def rollout(step, carry):
        kk = NX - 1 - step
        r = y + NX * kk
        start = score_rows(kk)
        for t in range(REP):
            span = slice(t * BLK, (t + 1) * BLK)
            gs[span, :] = g_in[kk, :, span]
        top = stat.at[0, kk]
        low = delta_in.at[kk]

        def hides(m):
            return [(mask[r, m * 4 + b].astype(f32) - 1.0) * 1e30 for b in range(4)]

        def grads(place, into, hidden_by, n):
            for lo, hi in CHUNKS:
                w = hi - lo
                dp = lax.dot_general(kv[place, HEAD:PAIR], gs[lo:hi, :], NT, preferred_element_type=f32)
                dp = dp.reshape(n, BLK // 8, 8, w)
                cut = s_ref[into, lo:hi].reshape(n, BLK // 8, 8, w)
                for b in range(n):
                    span = slice(b * BLK, (b + 1) * BLK)
                    p = jnp.exp2(cut[b] - (top[:, lo:hi] - hidden_by[b])[None])
                    ds = p * (dp[b] - low[:, lo:hi][None])
                    pb[span, lo:hi] = p.reshape(BLK, w).astype(bf16)
                    dsb[span, lo:hi] = ds.reshape(BLK, w).astype(bf16)
            acc[place, 0:HEAD] += jnp.dot(dsb[0 : n * BLK, :], qs[kk], preferred_element_type=f32)
            acc[place, HEAD:PAIR] += jnp.dot(pb[0 : n * BLK, :], gs[...], preferred_element_type=f32)

        def grads_group(m, cc):
            grads(rows(m, GROUP), score_place(start, m), hides(m), 4)
            return cc

        grads_group(kk, 0)
        for b in range(4):
            j = kk * 4 + b
            part = acc[rows(j, BLK), :].reshape(SEQ, SPAN, PAIR)
            tsend[:, j, :, 0:HEAD] = (part[:, :, 0:HEAD] * SCALE).astype(bf16)
            tsend[:, j, :, HEAD:PAIR] = part[:, :, HEAD:PAIR].astype(bf16)
        for o in range(SEQ - 1):
            term(kk, kk * 4, 4, o).start()
        lax.fori_loop(0, kk, grads_group, 0)
        grads(ends, ends_place(start), [0.0, 0.0], 2)

        @pl.when(step == NX - 1)
        def _():
            for i in range(2):
                part = acc[TREE + i * BLK : TREE + (i + 1) * BLK, :].reshape(SEQ, SPAN, PAIR)
                tsend[:, SEQ + i, :, 0:HEAD] = (part[:, :, 0:HEAD] * SCALE).astype(bf16)
                tsend[:, SEQ + i, :, HEAD:PAIR] = part[:, :, HEAD:PAIR].astype(bf16)
            for o in range(SEQ - 1):
                term(4, SEQ, 2, o).start()

        return carry

    lax.fori_loop(0, NX, rollout, 0)
    step_e = [term(4, SEQ, 2, o) for o in range(SEQ - 1)]
    step_t = [term(kk, kk * 4, 4, o) for kk in range(NX) for o in range(SEQ - 1)]
    rt[me] = tsend[me]
    step_b = [
        pltpu.make_async_remote_copy(
            src_ref=back_s.at[peers[o]], dst_ref=back_r.at[me], send_sem=b_s.at[o], recv_sem=b_r.at[o],
            device_id={"seq": peers[o]}, device_id_type=MESH,
        )
        for o in range(SEQ - 1)
    ]

    def finish(m):
        for copy in step_t[m * 15 : m * 15 + 15]:
            copy.wait_recv()
        span = slice(m * 32, m * 32 + 32)
        for h in range(KV):
            for side in range(2):
                lanes = slice(side * HEAD, (side + 1) * HEAD)
                place = slice(side * KVW + h * HEAD, side * KVW + (h + 1) * HEAD)
                total = rt[NX * h, 4 * m : 4 * m + 4, :, lanes].astype(f32)
                for a in range(1, NX):
                    total += rt[NX * h + a, 4 * m : 4 * m + 4, :, lanes].astype(f32)
                all_g[span, place] = total.reshape(32, HEAD).astype(bf16)
        back = lax.dot_general(all_g[span, :], up[...], NT, preferred_element_type=f32)
        back_s[4 * m : 4 * m + 4] = back.reshape(4, SPAN, HEAD).astype(bf16)
        for j in range(4 * m, 4 * m + 4):

            @pl.when(me != j)
            def _():
                o = lax.rem(j - me + 2 * SEQ - 1, SEQ)
                remote(back_s.at[j], back_r.at[me], b_s.at[o], b_r.at[o], {"seq": j})

    for m in (3, 2, 1, 0):
        finish(m)
    back_r[me] = back_s[me]
    for copy in step_e:
        copy.wait_recv()
    for h in range(KV):
        for side in range(2):
            lanes = slice(side * HEAD, (side + 1) * HEAD)
            place = slice(side * KVW + h * HEAD, side * KVW + (h + 1) * HEAD)
            for i in range(2):
                part = rt[NX * h, SEQ + i, :, lanes].astype(f32)
                for a in range(1, NX):
                    part += rt[NX * h + a, SEQ + i, :, lanes].astype(f32)
                rp[i, :, place] = part
    for b in range(GRP):
        part = rp[0] * (listed[0, 0] == b).astype(f32) + rp[1] * (listed[0, 1] == b).astype(f32)
        pt[b] = part.astype(bf16)
    step_p = []
    for i in range(1, GRP):
        b = lax.rem(grp + i, GRP)
        step_p.append(remote(pt.at[b], rq.at[i], p_s.at[i], p_r.at[i], {"grp": b}))
    for copy in step_p:
        copy.wait_recv()
    total = pt[grp].astype(f32)
    for i in range(1, GRP):
        total += rq[i].astype(f32)
    own_x[...] = total
    keep.append(local(own_x, prefix, 12))
    tail = jnp.concatenate([total, jnp.zeros_like(total)], axis=0).astype(bf16)
    all_g[BLK:DEPTH, :] = tail
    back_all[BLK:DEPTH, :] = lax.dot_general(tail, up[...], NT, preferred_element_type=f32).astype(bf16)
    keep.append(local(all_g.at[0:BLK], pair, 13))
    for copy in step_j:
        copy.wait_recv()
    proj_all[0:BLK, :] = proj_r[...].reshape(BLK, HEAD)
    same = lax.broadcasted_iota(jnp.int32, (HEAD, HEAD), 0) == lax.broadcasted_iota(jnp.int32, (HEAD, HEAD), 1)
    eye = same.astype(f32).astype(bf16)
    proj_t[...] = lax.dot_general(eye, proj_all[...], NT, preferred_element_type=f32).astype(bf16)
    for a in range(NX):
        cut = slice(a * TILE, (a + 1) * TILE)
        s0[1, 2, a] = jnp.dot(proj_t[...], all_g[:, cut], preferred_element_type=f32).astype(bf16)
    for copy in step_b:
        copy.wait_recv()

    back_all[0:BLK, :] = back_r[...].reshape(BLK, HEAD)
    back_t[...] = lax.dot_general(eye, back_all[...], NT, preferred_element_type=f32).astype(bf16)
    sibling = {"grp": grp + 1 - 2 * c}
    zero, first, second, third, fourth, fifth = [], [], [], [], [], []

    def down_terms(half, t):
        for a in range(NX):
            cut = cols((half * TYPES + t) * NX + a, TILE)
            s0[half, t, a] = jnp.dot(back_t[...], own_h[:, cut], preferred_element_type=f32).astype(bf16)

    for t in range(TYPES):
        if t < 2:
            down_terms(1 - c, t)
        else:
            down_terms(0, t)
        zero.append(remote(s0.at[1 - c, t], r0.at[t], s0_s.at[t], s0_r.at[t], sibling))
    for t in range(2):
        down_terms(c, t)
    for t in range(TYPES):
        zero[t].wait_recv()
        for a in range(NX):
            s1[t, a] = (s0[c, t, a].astype(f32) + r0[t, a].astype(f32)).astype(bf16)
        for i in range(1, NX):
            there = lax.rem(on_line[t] + i, NX)
            first.append(remote(s1.at[t, there], r1.at[t, i - 1], s1_s.at[t, i], s1_r.at[t, i], line(t, i)))
    for t in range(TYPES):
        for copy in first[t * 3 : t * 3 + 3]:
            copy.wait_recv()
        total = s1[t, on_line[t]].astype(f32)
        for i in range(NX - 1):
            total += r1[t, i].astype(f32)
        s2[t] = total.reshape(SEQ, SPAN, TILE).astype(bf16)
        for o in range(SEQ - 1):
            e = lax.rem(on_plane[t] + o + 1, SEQ)
            second.append(remote(s2.at[t, e], r2.at[t, o], s2_s.at[t, o], s2_r.at[t, o], plane(t, e)))
    for t in range(TYPES):
        for copy in second[t * 15 : t * 15 + 15]:
            copy.wait_recv()
        total = s2[t, on_plane[t]].astype(f32)
        for o in range(SEQ - 1):
            total += r2[t, o].astype(f32)
        full[t, on_line[t], on_plane[t]] = total.astype(bf16)
        piece = full.at[t, on_line[t], on_plane[t]]
        for o in range(SEQ - 1):
            e = lax.rem(on_plane[t] + o + 1, SEQ)
            third.append(remote(piece, piece, a2_s.at[t, o], a2_r.at[t, o], plane(t, e)))
    for t in range(TYPES):
        for copy in third[t * 15 : t * 15 + 15]:
            copy.wait_recv()
        piece = full.at[t, on_line[t]]
        for i in range(1, NX):
            fourth.append(remote(piece, piece, a1_s.at[t, i], a1_r.at[t, i], line(t, i)))
    for t in range(TYPES):
        for copy in fourth[t * 3 : t * 3 + 3]:
            copy.wait_recv()
        fifth.append(remote(full.at[t], out.at[c, t], a0_s.at[t], a0_r.at[t], sibling))
        keep.append(local(full.at[t], out.at[c, t], 14 + t))
    for copy in fifth:
        copy.wait_recv()
    for copy in keep[12:]:
        copy.wait()

    for copy in (
        step_x[0] + step_x[1] + step_y[0] + step_y[1] + step_q + step_g + step_j + step_e + step_t + step_p + step_b
        + zero + first + second + third + fourth + fifth
    ):
        copy.wait_send()


def backward(*operands):
    dma = pltpu.SemaphoreType.DMA

    def low(*shape):
        return pltpu.VMEM(shape, bf16)

    def wide(*shape):
        return pltpu.VMEM(shape, f32)

    return pl.pallas_call(
        kernel,
        out_shape=(
            jax.ShapeDtypeStruct((BLK, 2 * KVW), bf16),
            jax.ShapeDtypeStruct((SPAN, 2 * KVW), f32),
            jax.ShapeDtypeStruct((2, TYPES, NX, SEQ, SPAN, TILE), bf16),
        ),
        in_specs=[smem()] * 2 + [hbm()] * 11 + [vmem()] * 2,
        out_specs=(hbm(),) * 3,
        scratch_shapes=[
            low(NX, BLK, DT), low(NX, BLK, DT), wide(NX, 8, W), low(TREE + 2 * BLK, PAIR),
            low(BLK, 4 * DT), low(BLK, 4 * DT), low(DEPTH, D), low(SPAN, D), low(HEAD, D),
            low(GRP, BLK, PAIR), low(HEAD, 2 * KVW), wide(KV, 8, W),
            low(DEPTH, 2 * KVW), low(DEPTH, HEAD), low(HEAD, DEPTH), low(DEPTH, HEAD), low(HEAD, DEPTH),
            wide(2 * BLK * NX * (NX + 2), W), wide(TREE + 2 * BLK, PAIR), low(NX, W, HEAD), low(W, HEAD),
            low(GROUP, W), low(GROUP, W), wide(2, NX, 8, W), wide(GROUP, BLK),
            low(SEQ, SEQ + 2, SPAN, PAIR), low(SEQ, SEQ + 2, SPAN, PAIR),
            low(SEQ, SPAN, HEAD), low(SEQ, SPAN, HEAD),
            low(GRP, SPAN, 2 * KVW), wide(2, SPAN, 2 * KVW), low(GRP, SPAN, 2 * KVW),
            low(SEQ, SPAN, HEAD), low(SEQ, SPAN, HEAD),
            low(2, TYPES, NX, BLK, TILE), low(TYPES, NX, BLK, TILE), low(TYPES, NX, BLK, TILE),
            low(TYPES, NX - 1, BLK, TILE), low(TYPES, SEQ, SPAN, TILE), low(TYPES, SEQ - 1, SPAN, TILE),
            low(TYPES, NX, SEQ, SPAN, TILE), wide(SPAN, 2 * KVW),
            dma((17,)),
            dma((2, NX)), dma((2, NX)), dma((2, NX, NX)), dma((2, NX, NX)), dma((3, NX)), dma((3, NX)),
            dma((5, SEQ)), dma((5, SEQ)), dma((SEQ,)), dma((SEQ,)), dma((SEQ,)), dma((SEQ,)),
            dma((GRP,)), dma((GRP,)),
            dma((TYPES,)), dma((TYPES,)), dma((TYPES, NX)), dma((TYPES, NX)),
            dma((TYPES, SEQ)), dma((TYPES, SEQ)), dma((TYPES, SEQ)), dma((TYPES, SEQ)),
            dma((TYPES, NX)), dma((TYPES, NX)), dma((TYPES,)), dma((TYPES,)),
        ],
        compiler_params=pltpu.CompilerParams(
            collective_id=0, has_side_effects=True, vmem_limit_bytes=56 * 2**20
        ),
        name="backward",
    )(*operands)


def spread_kernel(summed, pair, prefix, down, rise, pair_out, prefix_out, got, made, risen, pair_got, prefix_got, sem_got, sem_made):
    factor = 2.0 / (GRP * SEQ)
    arrive = [pltpu.make_async_copy(summed.at[i], got.at[i], sem_got.at[i]) for i in range(2 * TYPES)]
    through = [
        pltpu.make_async_copy(pair, pair_got, sem_got.at[6]),
        pltpu.make_async_copy(prefix, prefix_got, sem_got.at[7]),
    ]
    for copy in arrive + through:
        copy.start()
    leave = []
    for i in range(2 * TYPES):
        arrive[i].wait()
        for a in range(NX):
            part = got[i, a].reshape(BLK, TILE).astype(f32) * factor
            if i < 5:
                made[i, :, a * TILE : (a + 1) * TILE] = part
            else:
                side = a // 2
                risen[side, :, (a % 2) * TILE : (a % 2 + 1) * TILE] = part[side * 64 : side * 64 + 64]
        if i < 5:
            for half in range(2):
                cut = slice(half * 64, half * 64 + 64)
                leave.append(
                    pltpu.make_async_copy(
                        made.at[i, cut], down.at[cut, i * NX * TILE : (i + 1) * NX * TILE],
                        sem_made.at[2 + 2 * i + half],
                    )
                )
                leave[-1].start()
        else:
            leave.append(pltpu.make_async_copy(risen, rise, sem_made.at[12]))
            leave[-1].start()
    for i, (source, target) in enumerate(((pair_got, pair_out), (prefix_got, prefix_out))):
        through[i].wait()
        leave.append(pltpu.make_async_copy(source, target, sem_made.at[i]))
        leave[-1].start()
    for copy in leave:
        copy.wait()


def spread(summed, pair, prefix):
    return pl.pallas_call(
        spread_kernel,
        out_shape=(
            jax.ShapeDtypeStruct((BLK, D), f32),
            jax.ShapeDtypeStruct((2, 64, KVW), f32),
            jax.ShapeDtypeStruct((BLK, 2 * KVW), bf16),
            jax.ShapeDtypeStruct((SPAN, 2 * KVW), f32),
        ),
        in_specs=[hbm()] * 3,
        out_specs=(hbm(),) * 4,
        scratch_shapes=[
            pltpu.VMEM((2 * TYPES, NX, SEQ, SPAN, TILE), bf16),
            pltpu.VMEM((5, BLK, NX * TILE), f32),
            pltpu.VMEM((2, 64, KVW), f32),
            pltpu.VMEM((BLK, 2 * KVW), bf16),
            pltpu.VMEM((SPAN, 2 * KVW), f32),
            pltpu.SemaphoreType.DMA((2 * TYPES + 2,)),
            pltpu.SemaphoreType.DMA((13,)),
        ],
        compiler_params=pltpu.CompilerParams(vmem_limit_bytes=60 * 2**20),
        name="spread",
    )(summed.reshape(2 * TYPES, NX, SEQ, SPAN, TILE), pair, prefix)


def on_device(
    queries, out_grad, saved_output, key_rows, value_rows, hidden_rows, prefix_keys, prefix_values,
    prefix_hidden, block_mask, prefix_list, key_down, value_down, key_up, value_up,
):
    pair, prefix, summed = backward(
        block_mask[0], prefix_list, queries[0, 0], out_grad[0, 0], saved_output[0, 0],
        key_rows[0, 0], value_rows[0, 0], hidden_rows[0, 0], prefix_hidden[0],
        prefix_keys, prefix_values, key_down.T, value_down.T, key_up, value_up,
    )
    down, rise, pair, prefix = spread(summed, pair, prefix)
    down = jnp.swapaxes(down.reshape(2, BLK // 2, D), 1, 2)
    return pair[None], prefix[None], down, rise


def solution(mesh):
    row = P("grp", "seq", None, None)
    in_specs = (
        row, row, row, row, row, row, P(), P(),
        P("grp", "seq", None), P("grp", None, None), P("grp", None), P(), P(), P(), P(),
    )
    out_specs = (P("grp", "seq", None), P("grp", "seq", None), P(), P())
    return jax.shard_map(
        on_device, mesh=mesh, in_specs=in_specs, out_specs=out_specs, check_vma=False
    )
```
